32 devices in a mesh: task: 2 (over core), shard: 16 (over z, y, x).
Axes of the slice: x: 2, y: 2, z: 4, core: 2. Of those that a mesh axis runs over, the one named last changes fastest.
Arguments:
- inputs: bfloat16 [32, 512, 768], P(('task', 'shard')), may hold values from -6 to 6
- encoded: bfloat16 [32, 512, 768], P(('task', 'shard')), may hold values from -6 to 6
- cotangent: bfloat16 [32, 512, 768], P(('task', 'shard')), may hold values from -6 to 6
- tgt_len: int32 [32], P(('task', 'shard')), may hold values from 114 to 512, as said below
- src_len: int32 [32], P(('task', 'shard')), may hold values from 64 to 512, as said below
- task_counts: int32 [2], replicated, may hold values from 1 to 16
- gain_self: bfloat16 [768], P('shard'), may hold values from 0.099609375 to 1.8984375
- query_self: bfloat16 [768, 768], P('shard'), may hold values from -0.02734375 to 0.02734375
- key_self: bfloat16 [768, 768], P('shard'), may hold values from -0.21875 to 0.21875
- value_self: bfloat16 [768, 768], P('shard'), may hold values from -0.21875 to 0.21875
- out_self: bfloat16 [768, 768], P('shard'), may hold values from -1.25 to 1.25
- bias_table: bfloat16 [32, 12], P('shard'), may hold values from -4 to 4
- gain_cross: bfloat16 [768], P('shard'), may hold values from 0.099609375 to 1.8984375
- query_cross: bfloat16 [768, 768], P('shard'), may hold values from -0.02734375 to 0.02734375
- key_cross: bfloat16 [768, 768], P('shard'), may hold values from -0.21875 to 0.21875
- value_cross: bfloat16 [768, 768], P('shard'), may hold values from -0.21875 to 0.21875
- out_cross: bfloat16 [768, 768], P('shard'), may hold values from -1.25 to 1.25
- gain_ffn: bfloat16 [768], P('shard'), may hold values from 0.099609375 to 1.8984375
- ffn_in: bfloat16 [768, 3072], P('shard'), may hold values from -0.21875 to 0.21875
- ffn_out: bfloat16 [3072, 768], P('shard'), may hold values from -0.109375 to 0.109375
Outputs:
- layer_out: bfloat16 [32, 512, 768], P(('task', 'shard'))
- grad_inputs: bfloat16 [32, 512, 768], P(('task', 'shard'))
- grad_encoded: bfloat16 [32, 512, 768], P(('task', 'shard'))
- grad_gain_self: float32 [768], P('shard')
- grad_query_self: float32 [768, 768], P('shard')
- grad_key_self: float32 [768, 768], P('shard')
- grad_value_self: float32 [768, 768], P('shard')
- grad_out_self: float32 [768, 768], P('shard')
- grad_bias_table: float32 [32, 12], P('shard')
- grad_gain_cross: float32 [768], P('shard')
- grad_query_cross: float32 [768, 768], P('shard')
- grad_key_cross: float32 [768, 768], P('shard')
- grad_value_cross: float32 [768, 768], P('shard')
- grad_out_cross: float32 [768, 768], P('shard')
- grad_gain_ffn: float32 [768], P('shard')
- grad_ffn_in: float32 [768, 3072], P('shard')
- grad_ffn_out: float32 [3072, 768], P('shard')
The draws below stay inside these ranges and needn't reach their ends.
Inputs may be any that keep to these rules, and one draw needn't show every extreme that they name: `tgt_len`: each entry is 114 or 512; the first example has 512 and the second 114. `src_len`: the first example has 512.
All inputs are finite; a program needn't handle non-finite values.
Results may differ from the reference program's by a relative error of at most 0.025.
Values may be sent and summed in bfloat16 or wider, within the bound.
A program may use at most 192 MiB of HBM per device.

```python
import math
import jax
import jax.numpy as jnp
import numpy as np
from jax import lax

D = 768
H = 12
DH = 64
FF = 3072
NB = 32
TGT = 512
SHORT = 114
SRC = 512
EX_DEV = 1
EXAMPLES = 32
N_TASK = 2
N_SHARD = 16


def draw_tgt_len(key, part):
    outcome = jax.random.randint(key, (EXAMPLES,), 0, 2)
    lengths = jnp.where(outcome == 1, TGT, SHORT).astype(jnp.int32)
    lengths = lengths.at[0].set(TGT)
    return lengths.at[1].set(SHORT)


def draw_src_len(key, part):
    lengths = jax.random.randint(key, (EXAMPLES,), SRC // 8, SRC + 1).astype(jnp.int32)
    return lengths.at[0].set(SRC)


def levels(own_key, dims, pieces, low, top_value):
    level, own = 1.0, jax.random.fold_in(own_key, 6)
    for dim, shards_of in pieces:
        steps = jnp.exp(jax.random.uniform(jax.random.fold_in(own, dim), (shards_of,), jnp.float32, low / len(pieces), top_value / len(pieces)))
        level = level * jnp.repeat(steps, dims[dim] // shards_of).reshape([-1 if axis == dim else 1 for axis in range(len(dims))])
    return level


def centred(stream_key, extent, scale, most, split=(), kind=jnp.bfloat16):
    gain = levels(stream_key, extent, split, -0.22, 0.18) if split else 1.0
    values = jax.random.normal(stream_key, extent, jnp.float32) * scale * gain
    return jnp.minimum(jnp.maximum(values, -most), most).astype(kind)


def setup_inputs(seed: int = 0) -> dict:
    streams_of = jax.random.split(jax.random.key(seed), 21)
    inputs = centred(streams_of[0], (EXAMPLES, TGT, D), 1.0, 6.0, ((0, 32),))
    encoded = centred(streams_of[1], (EXAMPLES, SRC, D), 1.0, 6.0, ((0, 32),))
    cotangent = centred(streams_of[2], (EXAMPLES, TGT, D), 1.0, 6.0, ((0, 32),))
    tgt_len = draw_tgt_len(jax.random.fold_in(streams_of[20], 71), 0)
    src_len = draw_src_len(jax.random.fold_in(streams_of[20], 71), 0)
    task_counts = jax.random.randint(streams_of[5], (N_TASK,), 1, 17).astype(jnp.int32)
    gain_self = jnp.clip(1.0 + 0.18 * jax.random.normal(streams_of[6], (D,), jnp.float32), 0.099609375, 1.8984375).astype(jnp.bfloat16)
    query_self = centred(streams_of[7], (D, D), (D * DH) ** -0.5, 0.02734375, ((0, 16),))
    key_self = centred(streams_of[8], (D, D), D ** -0.5, 0.21875, ((0, 16),))
    value_self = centred(streams_of[9], (D, D), D ** -0.5, 0.21875, ((0, 16),))
    out_self = centred(streams_of[10], (D, D), (D * 16 // TGT) ** -0.5, 1.25, ((0, 16),))
    bias_table = centred(streams_of[11], (NB, H), 1.0, 4.0, ((0, 16),))
    gain_cross = jnp.clip(1.0 + 0.18 * jax.random.normal(streams_of[12], (D,), jnp.float32), 0.099609375, 1.8984375).astype(jnp.bfloat16)
    query_cross = centred(streams_of[13], (D, D), (D * DH) ** -0.5, 0.02734375, ((0, 16),))
    key_cross = centred(streams_of[14], (D, D), D ** -0.5, 0.21875, ((0, 16),))
    value_cross = centred(streams_of[15], (D, D), D ** -0.5, 0.21875, ((0, 16),))
    out_cross = centred(streams_of[16], (D, D), (D * 16 // TGT) ** -0.5, 1.25, ((0, 16),))
    gain_ffn = jnp.clip(1.0 + 0.18 * jax.random.normal(streams_of[17], (D,), jnp.float32), 0.099609375, 1.8984375).astype(jnp.bfloat16)
    ffn_in = centred(streams_of[18], (D, FF), D ** -0.5, 0.21875, ((0, 16),))
    ffn_out = centred(streams_of[19], (FF, D), FF ** -0.5, 0.109375, ((0, 16),))
    return {"inputs": inputs, "encoded": encoded, "cotangent": cotangent, "tgt_len": tgt_len, "src_len": src_len, "task_counts": task_counts, "gain_self": gain_self, "query_self": query_self, "key_self": key_self, "value_self": value_self, "out_self": out_self, "bias_table": bias_table, "gain_cross": gain_cross, "query_cross": query_cross, "key_cross": key_cross, "value_cross": value_cross, "out_cross": out_cross, "gain_ffn": gain_ffn, "ffn_in": ffn_in, "ffn_out": ffn_out}


EPSILON = 1e-06
MASKED = -1000000000.0
HIGHEST = lax.Precision.HIGHEST
LIMITS = np.array(list(range(1, 16)) + [math.ceil(16.0 * 8.0 ** ((bucket - 16) / 16.0)) for bucket in range(16, 32)], dtype=np.int32)

@jax.custom_vjp
def low(v):
    return lax.optimization_barrier(v.astype(jnp.bfloat16)).astype(jnp.float32)

@jax.custom_vjp
def low_back(v):
    return v

def low_keep(v):
    return (low(v), None)

def low_pass(kept, grad):
    return (grad,)

def back_keep(v):
    return (v, None)

def back_low(kept, grad):
    return (low(grad),)
low.defvjp(low_keep, low_pass)
low_back.defvjp(back_keep, back_low)

def round_both(quantity):
    return low_back(low(quantity))

def product(matrix, factor):
    return jnp.dot(matrix, factor, precision=HIGHEST)

def normalize(residual, gain_value):
    inverse_rms = lax.rsqrt(lax.optimization_barrier(jnp.mean(residual * residual, axis=-1, keepdims=True)) + EPSILON)
    return residual * inverse_rms * gain_value

def bucket_onehot(length):
    positions = jnp.arange(length, dtype=jnp.int32)
    distance = jnp.maximum(positions[:, None] - positions[None, :], 0).astype(jnp.int32)
    buckets = lax.optimization_barrier(jnp.sum((distance[:, :, None] >= jnp.asarray(LIMITS, dtype=jnp.int32)).astype(jnp.int32), axis=2, dtype=jnp.int32))
    return buckets[:, :, None] == jnp.arange(NB, dtype=jnp.int32)

def causal_mask(length, live_count):
    positions = jnp.arange(length, dtype=jnp.int32)
    return (positions[None, :] <= positions[:, None]) & (positions[None, :] < live_count.astype(jnp.int32))

def source_mask(length, source, live_count):
    columns = jnp.arange(source, dtype=jnp.int32)
    return jnp.broadcast_to(columns[None, :] < live_count.astype(jnp.int32), (length, source))

def attend(query, keys, values, rel_bias, allowed):
    queries = query.reshape(query.shape[0], H, DH)
    keyset = keys.reshape(keys.shape[0], H, DH)
    valueset = values.reshape(values.shape[0], H, DH)
    scores = low_back(jnp.einsum('ihd,jhd->hij', queries, keyset, precision=HIGHEST) + rel_bias)
    scores = jnp.where(allowed[None], scores, MASKED)
    weights = round_both(jax.nn.softmax(scores, axis=-1))
    mixture = jnp.einsum('hij,jhd->ihd', weights, valueset, precision=HIGHEST)
    return round_both(mixture.reshape(query.shape[0], H * DH))

def one_example(params, rel_bias, residual, encoded, target_live, source_live):
    gain_self, query_self, key_self, value_self, out_self, bias_table, gain_cross, query_cross, key_cross, value_cross, out_cross, gain_ffn, ffn_in, ffn_out = params
    length = residual.shape[0]
    normed = low(normalize(residual, gain_self))
    mixture = attend(round_both(product(normed, query_self)), round_both(product(normed, key_self)), round_both(product(normed, value_self)), rel_bias, causal_mask(length, target_live))
    after_self = residual + low_back(product(mixture, out_self))
    normed = low(normalize(after_self, gain_cross))
    mixture = attend(round_both(product(normed, query_cross)), round_both(product(encoded, key_cross)), round_both(product(encoded, value_cross)), 0.0, source_mask(length, encoded.shape[0], source_live))
    after_cross = after_self + low_back(product(mixture, out_cross))
    normed = low(normalize(after_cross, gain_ffn))
    hidden = low(jax.nn.gelu(low_back(product(normed, ffn_in)), approximate=True))
    result = after_cross + low_back(product(hidden, ffn_out))
    live_rows = jnp.arange(length, dtype=jnp.int32) < target_live.astype(jnp.int32)
    return jnp.where(live_rows[:, None], result, 0.0)

def forward_slice(params, residual, encoded, target_len, source_len):
    onehot = bucket_onehot(residual.shape[1]).astype(jnp.float32)
    rel_bias = jnp.einsum('ijb,bh->hij', onehot, params[5], precision=HIGHEST)

    def single(element):
        return one_example(params, rel_bias, element[0], element[1], element[2], element[3])
    return lax.map(jax.checkpoint(single), (residual, encoded, target_len, source_len))

def reference(inputs, encoded, cotangent, tgt_len, src_len, task_counts, gain_self, query_self, key_self, value_self, out_self, bias_table, gain_cross, query_cross, key_cross, value_cross, out_cross, gain_ffn, ffn_in, ffn_out):
    params = tuple((weight.astype(jnp.float32) for weight in (gain_self, query_self, key_self, value_self, out_self, bias_table, gain_cross, query_cross, key_cross, value_cross, out_cross, gain_ffn, ffn_in, ffn_out)))
    per_slice = EX_DEV * N_SHARD

    def slice_pass(element):
        residual, source, cotangent_part, target_len, source_len = element

        def forward(weights, residual_value, source_value):
            return forward_slice(weights, residual_value, source_value, target_len, source_len)
        result, pullback = jax.vjp(forward, params, residual.astype(jnp.float32), source.astype(jnp.float32))
        grad_params, grad_residual, grad_source = pullback(cotangent_part.astype(jnp.float32))
        return (result.astype(jnp.bfloat16), grad_residual.astype(jnp.bfloat16), grad_source.astype(jnp.bfloat16), grad_params)

    def grouped(tensor):
        return tensor.reshape((N_TASK, per_slice) + tensor.shape[1:])

    def flatten_slices(tensor):
        return tensor.reshape((N_TASK * per_slice,) + tensor.shape[2:])
    outputs, grad_in, grad_enc, grad_params = lax.map(slice_pass, (grouped(inputs), grouped(encoded), grouped(cotangent), grouped(tgt_len.astype(jnp.int32)), grouped(src_len.astype(jnp.int32))))
    counts = task_counts.astype(jnp.float32)
    slice_share = counts / jnp.sum(counts)
    weighted = tuple((lax.optimization_barrier(jnp.sum(gradient * slice_share.reshape((N_TASK,) + (1,) * (gradient.ndim - 1)), axis=0)) for gradient in grad_params))
    grad_gain_self, grad_query_self, grad_key_self, grad_value_self, grad_out_self, grad_bias_table, grad_gain_cross, grad_query_cross, grad_key_cross, grad_value_cross, grad_out_cross, grad_gain_ffn, grad_ffn_in, grad_ffn_out = weighted
    return (flatten_slices(outputs), flatten_slices(grad_in), flatten_slices(grad_enc), grad_gain_self, grad_query_self, grad_key_self, grad_value_self, grad_out_self, grad_bias_table, grad_gain_cross, grad_query_cross, grad_key_cross, grad_value_cross, grad_out_cross, grad_gain_ffn, grad_ffn_in, grad_ffn_out)
```

```python
import functools
import math

import jax
import jax.numpy as jnp
import numpy as np
from jax import lax
from jax.experimental import pallas as pl
from jax.experimental.pallas import tpu as pltpu
from jax.sharding import PartitionSpec as P

H = 12
DH = 64
NB = 32
D = 768


EPSILON = 1e-06
MASKED = -1000000000.0
LIMITS = np.array(
    list(range(1, 16))
    + [math.ceil(16.0 * 8.0 ** ((bucket - 16) / 16.0)) for bucket in range(16, 32)],
    dtype=np.int32,
)


def smooth_act(value):
    return jax.nn.gelu(value, approximate=True)


def matmul(matrix, factor):
    return jnp.dot(matrix, factor, preferred_element_type=jnp.float32)


def times_transposed(matrix, factor):
    return lax.dot_general(
        matrix, factor, (((1,), (1,)), ((), ())), preferred_element_type=jnp.float32
    )


def outer_rows(matrix, factor):
    return lax.dot_general(
        matrix, factor, (((0,), (0,)), ((), ())), preferred_element_type=jnp.float32
    )


def norm_forward(residual, gain_value):
    inverse_rms = lax.rsqrt(jnp.mean(residual * residual, axis=-1, keepdims=True) + EPSILON)
    normed = residual * inverse_rms
    return (normed, inverse_rms, (normed * gain_value).astype(jnp.bfloat16))


def norm_backward(grad_normed, normed, inverse_rms, gain_value):
    grad_gain = jnp.sum(grad_normed * normed, axis=0)
    grad_scaled = grad_normed * gain_value
    grad_residual = inverse_rms * (
        grad_scaled - normed * jnp.mean(grad_scaled * normed, axis=-1, keepdims=True)
    )
    return (grad_residual, grad_gain)


def bucket_onehot(length):
    positions = jnp.arange(length, dtype=jnp.int32)
    distance = jnp.maximum(positions[:, None] - positions[None, :], 0)
    buckets = jnp.sum(
        (distance[:, :, None] >= jnp.asarray(LIMITS, dtype=jnp.int32)).astype(jnp.int32),
        axis=2,
        dtype=jnp.int32,
    )
    return buckets[:, :, None] == jnp.arange(NB, dtype=jnp.int32)


def causal_mask(length, live_count):
    positions = jnp.arange(length, dtype=jnp.int32)
    return (positions[None, :] <= positions[:, None]) & (positions[None, :] < live_count)


def source_mask(length, source, live_count):
    columns = jnp.arange(source, dtype=jnp.int32)
    return jnp.broadcast_to(columns[None, :] < live_count, (length, source))


def split_heads(matrix, examples):
    return matrix.reshape(examples, -1, H, DH)


def probabilities_of(queries, keyset, rel_bias, allowed):
    scores = jnp.einsum("ihd,jhd->hij", queries, keyset, preferred_element_type=jnp.float32)
    if rel_bias is not None:
        scores = scores + rel_bias
    scores = jnp.where(allowed[None], scores, MASKED)
    return jax.nn.softmax(scores, axis=-1)


def attend_forward(queries, keyset, valueset, rel_bias, allowed):
    probabilities = probabilities_of(queries, keyset, rel_bias, allowed)
    mixture = jnp.einsum(
        "hij,jhd->ihd",
        probabilities.astype(jnp.bfloat16),
        valueset,
        preferred_element_type=jnp.float32,
    )
    return mixture.astype(jnp.bfloat16)


def attend_backward(queries, keyset, valueset, rel_bias, allowed, grad_mixture, onehot):
    probabilities = probabilities_of(queries, keyset, rel_bias, allowed)
    rounded = probabilities.astype(jnp.bfloat16)
    mixture = jnp.einsum(
        "hij,jhd->ihd", rounded, valueset, preferred_element_type=jnp.float32
    ).astype(jnp.bfloat16)
    grad_probs = (
        jnp.einsum("ihd,jhd->hij", grad_mixture, valueset, preferred_element_type=jnp.float32)
        .astype(jnp.bfloat16)
        .astype(jnp.float32)
    )
    grad_values = jnp.einsum(
        "hij,ihd->jhd", rounded, grad_mixture, preferred_element_type=jnp.float32
    ).astype(jnp.bfloat16)
    grad_scores = (
        probabilities * (grad_probs - jnp.sum(grad_probs * probabilities, axis=-1, keepdims=True))
    ).astype(jnp.bfloat16)
    grad_queries = jnp.einsum(
        "hij,jhd->ihd", grad_scores, keyset, preferred_element_type=jnp.float32
    ).astype(jnp.bfloat16)
    grad_keys = jnp.einsum(
        "hij,ihd->jhd", grad_scores, queries, preferred_element_type=jnp.float32
    ).astype(jnp.bfloat16)
    if onehot is None:
        grad_table = jnp.zeros((1, 1), jnp.float32)
    else:
        grad_table = jnp.einsum(
            "ijb,hij->bh", onehot, grad_scores, preferred_element_type=jnp.float32
        )
    return (mixture, grad_queries, grad_keys, grad_values, grad_table)


def run_forward(weights, residual, source_rows, rel_bias, tgt_len, src_len, examples):
    (
        gain_self,
        query_self,
        key_self,
        value_self,
        out_self,
        bias_table,
        gain_cross,
        query_cross,
        key_cross,
        value_cross,
        out_cross,
        gain_ffn,
        ffn_in,
        ffn_out,
    ) = weights
    length = residual.shape[0] // examples
    source = source_rows.shape[0] // examples
    normed_self = norm_forward(residual, gain_self)[2]
    queries = split_heads(matmul(normed_self, query_self).astype(jnp.bfloat16), examples)
    keyset = split_heads(matmul(normed_self, key_self).astype(jnp.bfloat16), examples)
    valueset = split_heads(matmul(normed_self, value_self).astype(jnp.bfloat16), examples)

    def self_item(element):
        return attend_forward(
            element[0], element[1], element[2], rel_bias, causal_mask(length, element[3])
        )

    mixture = lax.map(self_item, (queries, keyset, valueset, tgt_len)).reshape(residual.shape)
    after_self = residual + matmul(mixture, out_self)
    normed_cross = norm_forward(after_self, gain_cross)[2]
    queries = split_heads(matmul(normed_cross, query_cross).astype(jnp.bfloat16), examples)
    keyset = split_heads(matmul(source_rows, key_cross).astype(jnp.bfloat16), examples)
    valueset = split_heads(matmul(source_rows, value_cross).astype(jnp.bfloat16), examples)

    def cross_item(element):
        return attend_forward(
            element[0], element[1], element[2], None, source_mask(length, source, element[3])
        )

    mixture = lax.map(cross_item, (queries, keyset, valueset, src_len)).reshape(residual.shape)
    after_cross = after_self + matmul(mixture, out_cross)
    normed_ffn = norm_forward(after_cross, gain_ffn)[2]
    hidden = smooth_act(matmul(normed_ffn, ffn_in)).astype(jnp.bfloat16)
    result = after_cross + matmul(hidden, ffn_out)
    return (after_self, after_cross, result)


MESH = pl.DeviceIdType.MESH
BF = jnp.bfloat16
F32 = jnp.float32
COLS = 4
SMALL = 16


class Place:
    def __init__(self, tasks, shards):
        self.tasks, self.zs = tasks, shards // COLS
        self.t, self.s = lax.axis_index("task"), lax.axis_index("shard")
        self.half = lax.rem(self.t, 2)
        self.other = 1 - self.half
        self.z, self.q = lax.div(self.s, COLS), lax.rem(self.s, COLS)
        flip_x = self.q + 1 - 2 * lax.rem(self.q, 2)
        flip_y = lax.rem(self.q + 2, COLS)
        self.qx, self.qy = flip_x, flip_y
        self.q2 = flip_x + self.half * (flip_y - flip_x)
        self.q3 = flip_y + self.half * (flip_x - flip_y)
        self.q4 = COLS - 1 - self.q
        self.core = (self.t + 1 - 2 * self.half, self.s)
        self.second = (self.t, self.z * COLS + self.q2)
        self.third = (self.t, self.z * COLS + self.q3)

    def along_z(self, step):
        z = lax.rem(self.z + step, self.zs)
        return z, (self.t, z * COLS + self.q)

    def along_task(self, step):
        return (lax.rem(self.t + 2 * step, self.tasks), self.s)

    def greet(self, task_peers):
        peers = [self.core, self.second, self.third]
        peers += [self.along_z(k)[1] for k in range(1, self.zs)]
        if task_peers:
            peers += [self.along_task(k) for k in range(1, self.tasks // 2)]
        barrier = pltpu.get_barrier_semaphore()
        for peer in peers:
            pl.semaphore_signal(barrier, inc=1, device_id=peer, device_id_type=MESH)
        pl.semaphore_wait(barrier, len(peers))


class Sends:
    def __init__(self, send_sem, recv_sem):
        self.send_sem, self.recv_sem, self.made = send_sem, recv_sem, {}

    def start(self, key, src, dst, device):
        number = len(self.made)
        copy = pltpu.make_async_remote_copy(
            src_ref=src,
            dst_ref=dst,
            send_sem=self.send_sem.at[number],
            recv_sem=self.recv_sem.at[number],
            device_id=device,
            device_id_type=MESH,
        )
        copy.start()
        self.made[key] = copy

    def arrived(self, key):
        self.made[key].wait_recv()

    def finish(self):
        for copy in self.made.values():
            copy.wait_send()


def column(ref, chunk, half, q):
    if chunk == 3:
        return ref.at[:, q, half]
    return ref.at[pl.ds(2 * half, 2), :, q]


def slab(ref, chunk, half, z, q):
    if chunk == 3:
        return ref.at[z, q, half]
    return ref.at[pl.ds(2 * half, 2), z, q]


def gather_kernel(tasks, shards, *refs):
    mats, small_ref = refs[:10], refs[10]
    outs, small_out = refs[11:15], refs[15]
    local_sem, send_sem, recv_sem = refs[16:]
    place = Place(tasks, shards)
    z, q, half = place.z, place.q, place.half
    copies = []
    for chunk in range(2):
        for unit in range(4):
            copies.append((mats[4 * chunk + unit], outs[chunk].at[unit, z, q]))
    for unit in range(4):
        copies.append((mats[8].at[:, pl.ds(768 * unit, 768)], outs[2].at[unit, z, q]))
    rows = mats[9].shape[0] // 2
    for part in range(2):
        copies.append((mats[9].at[pl.ds(rows * part, rows)], outs[3].at[z, q, part]))
    copies.append((small_ref, small_out.at[z, q]))
    made = []
    for number, (src, dst) in enumerate(copies):
        made.append(pltpu.make_async_copy(src, dst, local_sem.at[number]))

    def own(number, part):
        @pl.when(half == part)
        def _():
            made[number].start()

    def own_wait(number, part):
        @pl.when(half == part)
        def _():
            made[number].wait()

    parts = [0, 0, 1, 1] * 3 + [0, 1]
    for number in range(14):
        own(number, parts[number])
    made[14].start()
    place.greet(False)
    for number in range(14):
        own_wait(number, parts[number])
    made[14].wait()
    sends = Sends(send_sem, recv_sem)

    def z_start(chunk):
        ref = outs[chunk]
        mine = slab(ref, chunk, half, z, q)
        for k in range(1, place.zs):
            sends.start(("z", chunk, k), mine, mine, place.along_z(k)[1])

    def col_start(name, chunk, col, device):
        mine = column(outs[chunk], chunk, half, col)
        sends.start((name, chunk), mine, mine, device)

    for k in range(1, place.zs):
        sends.start(("zs", k), small_out.at[z, q], small_out.at[z, q], place.along_z(k)[1])
    z_start(0)
    for k in range(1, place.zs):
        sends.arrived(("zs", k))
    sends.start("as", small_out.at[:, q], small_out.at[:, q], place.second)
    sends.start("bs", small_out.at[:, q], small_out.at[:, q], place.third)
    for chunk in range(4):
        for k in range(1, place.zs):
            sends.arrived(("z", chunk, k))
        col_start("a", chunk, q, place.second)
        col_start("b", chunk, q, place.third)
        if chunk < 3:
            z_start(chunk + 1)
        col_start("d1", chunk, q, place.core)
        if chunk == 0:
            sends.arrived("as")
            sends.start("cs", small_out.at[:, place.q2], small_out.at[:, place.q2], place.third)
        if chunk:
            sends.arrived(("b", chunk - 1))
            col_start("d3", chunk - 1, place.q3, place.core)
            sends.arrived(("c", chunk - 1))
            col_start("d4", chunk - 1, place.q4, place.core)
        sends.arrived(("a", chunk))
        col_start("c", chunk, place.q2, place.third)
        col_start("d2", chunk, place.q2, place.core)
    sends.arrived(("b", 3))
    col_start("d3", 3, place.q3, place.core)
    sends.arrived(("c", 3))
    col_start("d4", 3, place.q4, place.core)
    sends.arrived("bs")
    sends.arrived("cs")
    for chunk in range(4):
        for name in ("d1", "d2", "d3", "d4"):
            sends.arrived((name, chunk))
    sends.finish()


def gather_weights(tasks, shards, mats, small):
    zs = shards // COLS
    rows, wide = mats[0].shape[0], mats[9].shape[0] // 2
    unit = jax.ShapeDtypeStruct((4, zs, COLS, rows, 768), BF)
    out_shape = (
        unit,
        unit,
        unit,
        jax.ShapeDtypeStruct((zs, COLS, 2, wide, 768), BF),
        jax.ShapeDtypeStruct((zs, COLS, SMALL, 768), BF),
    )
    number = 4 * ((zs - 1) + 7) + (zs - 1) + 3
    return pl.pallas_call(
        functools.partial(gather_kernel, tasks, shards),
        out_shape=out_shape,
        in_specs=[pl.BlockSpec(memory_space=pl.ANY)] * 11,
        out_specs=[pl.BlockSpec(memory_space=pl.ANY)] * 5,
        scratch_shapes=[
            pltpu.SemaphoreType.DMA((15,)),
            pltpu.SemaphoreType.DMA((number,)),
            pltpu.SemaphoreType.DMA((number,)),
        ],
        compiler_params=pltpu.CompilerParams(collective_id=1, has_side_effects=True),
        name="gather_weights",
    )(*mats, small)


def scatter_kernel(tasks, shards, *refs):
    parts, small_ref = refs[:4], refs[4]
    outs, small_out = refs[5:9], refs[9]
    from_core, from_third, from_second, from_z = refs[10:14], refs[14:18], refs[18:22], refs[22:26]
    from_task, small_slots, send_sem, recv_sem = refs[26:28], *refs[28:31]
    place = Place(tasks, shards)
    z, q, half, other = place.z, place.q, place.half, place.other
    place.greet(True)
    sends = Sends(send_sem, recv_sem)

    def add_into(chunk, col, arrived, arrived_col):
        @pl.loop(0, place.zs)
        def _(row):
            if chunk == 3:
                here = parts[chunk].at[row, col, half]
                total = here[...].astype(F32) + arrived.at[row, arrived_col][...].astype(F32)
                here[...] = total.astype(BF)
            else:
                for u in range(2):
                    here = parts[chunk].at[2 * half + u, row, col]
                    total = here[...].astype(F32) + arrived.at[u, row, arrived_col][...].astype(F32)
                    here[...] = total.astype(BF)

    def whole_half(ref, chunk, part):
        return ref.at[:, :, part] if chunk == 3 else ref.at[pl.ds(2 * part, 2)]

    def slot_col(ref, chunk, col):
        return ref.at[:, col] if chunk == 3 else ref.at[:, :, col]

    def step_core(chunk):
        sends.start(("d", chunk), whole_half(parts[chunk], chunk, other), from_core[chunk], place.core)

    def step_third(chunk):
        sends.arrived(("d", chunk))
        for col in range(COLS):
            add_into(chunk, col, from_core[chunk], col)
        sends.start(("b", chunk), column(parts[chunk], chunk, half, place.q3), slot_col(from_third[chunk], chunk, 0), place.third)
        sends.start(("c", chunk), column(parts[chunk], chunk, half, place.q4), slot_col(from_third[chunk], chunk, 1), place.third)

    def step_second(chunk):
        sends.arrived(("c", chunk))
        add_into(chunk, place.q2, from_third[chunk], 1)
        sends.start(("a", chunk), column(parts[chunk], chunk, half, place.q2), from_second[chunk], place.second)

    def step_z(chunk):
        sends.arrived(("b", chunk))
        add_into(chunk, q, from_third[chunk], 0)
        sends.arrived(("a", chunk))
        @pl.loop(0, place.zs)
        def _(row):
            if chunk == 3:
                here = parts[chunk].at[row, q, half]
                here[...] = (here[...].astype(F32) + from_second[chunk].at[row][...].astype(F32)).astype(BF)
            else:
                for u in range(2):
                    here = parts[chunk].at[2 * half + u, row, q]
                    here[...] = (here[...].astype(F32) + from_second[chunk].at[u, row][...].astype(F32)).astype(BF)
        for k in range(1, place.zs):
            to, device = place.along_z(k)
            sends.start(("z", chunk, k), slab(parts[chunk], chunk, half, to, q), from_z[chunk].at[k - 1], device)

    def step_last(chunk):
        for k in range(1, place.zs):
            sends.arrived(("z", chunk, k))
        total = slab(parts[chunk], chunk, half, z, q)[...].astype(F32)
        for k in range(1, place.zs):
            total = total + from_z[chunk][k - 1].astype(F32)
        mine = outs[chunk].at[half]
        mine[...] = total
        if tasks > 2:
            group = lax.div(place.t, 2)
            held = from_task[1] if chunk == 3 else from_task[0].at[chunk]
            held[group] = total
            for k in range(1, tasks // 2):
                sends.start(("t", chunk, k), held.at[group], held.at[group], place.along_task(k))
            for k in range(1, tasks // 2):
                sends.arrived(("t", chunk, k))
            total = held[0]
            for k in range(1, tasks // 2):
                total = total + held[k]
            mine[...] = total
        sends.start(("f", chunk), mine, mine, place.core)

    steps = [step_core, step_third, step_second, step_z, step_last]
    order = (3, 2, 1, 0)
    for chunk in order:
        step_core(chunk)
    small_out[...] = small_ref[...]
    hops = [place.core, (place.t, z * COLS + place.qx), (place.t, z * COLS + place.qy)]
    for number, device in enumerate(hops):
        small_slots[2 * number] = small_out[...]
        sends.start(("s", number), small_slots.at[2 * number], small_slots.at[2 * number + 1], device)
        sends.arrived(("s", number))
        small_out[...] += small_slots[2 * number + 1]
    small_slots[6 + z] = small_out[...]
    for k in range(1, place.zs):
        sends.start(("sz", k), small_slots.at[6 + z], small_slots.at[6 + z], place.along_z(k)[1])
    for k in range(1, place.zs):
        sends.arrived(("sz", k))
    total = small_slots[6]
    for k in range(1, place.zs):
        total = total + small_slots[6 + k]
    small_out[...] = total
    if tasks > 2:
        base = 6 + place.zs
        group = lax.div(place.t, 2)
        small_slots[base + group] = total
        for k in range(1, tasks // 2):
            sends.start(("st", k), small_slots.at[base + group], small_slots.at[base + group], place.along_task(k))
        for k in range(1, tasks // 2):
            sends.arrived(("st", k))
        total = small_slots[base]
        for k in range(1, tasks // 2):
            total = total + small_slots[base + k]
        small_out[...] = total
    for tick in range(7):
        for number, chunk in enumerate(order):
            step = tick - number + 1
            if 1 <= step <= 4:
                steps[step](chunk)
    for tick in range(4):
        sends.arrived(("f", order[tick]))
    sends.finish()


def scatter_grads(tasks, shards, parts, small):
    zs = shards // COLS
    rows, wide = parts[0].shape[3], parts[3].shape[3]
    final = [jax.ShapeDtypeStruct((2, 2, rows, 768), F32)] * 3 + [jax.ShapeDtypeStruct((2, wide, 768), F32)]
    final.append(jax.ShapeDtypeStruct((SMALL, 768), F32))
    pairs = tasks // 2

    def slots(shape, last):
        return [pltpu.VMEM(shape, BF)] * 3 + [pltpu.VMEM(last, BF)]

    scratch = (
        slots((2, zs, COLS, rows, 768), (zs, COLS, wide, 768))
        + slots((2, zs, 2, rows, 768), (zs, 2, wide, 768))
        + slots((2, zs, rows, 768), (zs, wide, 768))
        + slots((zs - 1, 2, rows, 768), (zs - 1, wide, 768))
        + [pltpu.VMEM((3, pairs, 2, rows, 768) if tasks > 2 else (8, 128), F32)]
        + [pltpu.VMEM((pairs, wide, 768) if tasks > 2 else (8, 128), F32)]
        + [pltpu.VMEM((6 + zs + pairs, SMALL, 768), F32)]
    )
    number = 4 * (5 + zs - 1 + pairs - 1) + 3 + zs - 1 + pairs - 1
    return pl.pallas_call(
        functools.partial(scatter_kernel, tasks, shards),
        out_shape=final,
        in_specs=[pl.BlockSpec(memory_space=pltpu.VMEM)] * 5,
        out_specs=[pl.BlockSpec(memory_space=pltpu.VMEM)] * 5,
        scratch_shapes=scratch
        + [pltpu.SemaphoreType.DMA((number,)), pltpu.SemaphoreType.DMA((number,))],
        compiler_params=pltpu.CompilerParams(
            collective_id=2, has_side_effects=True, vmem_limit_bytes=60 * 2**20
        ),
        name="scatter_grads",
    )(*parts, small)


def on_device(
    inputs,
    encoded,
    cotangent,
    tgt_len,
    src_len,
    task_counts,
    gain_self,
    query_self,
    key_self,
    value_self,
    out_self,
    bias_table,
    gain_cross,
    query_cross,
    key_cross,
    value_cross,
    out_cross,
    gain_ffn,
    ffn_in,
    ffn_out,
):
    tasks, shards = task_counts.shape[0], D // gain_self.shape[0]
    place_s = lax.axis_index("shard")
    small = jnp.zeros((SMALL, D), BF)
    gains = jnp.stack([gain_self, gain_cross, gain_ffn])
    small = lax.dynamic_update_slice(small, gains, (0, place_s * gains.shape[1]))
    small = lax.dynamic_update_slice(small, bias_table.T, (3, place_s * bias_table.shape[0]))
    mats = (query_self, key_self, value_self, out_self, query_cross, key_cross, value_cross, out_cross, ffn_in, ffn_out)
    full = gather_weights(tasks, shards, mats, small)
    small = jnp.sum(full[4].astype(F32), axis=(0, 1)).astype(BF)
    full_query_self, full_key_self, full_value_self, full_out_self = full[0].reshape(4, D, D)
    full_query_cross, full_key_cross, full_value_cross, full_out_cross = full[1].reshape(4, D, D)
    full_ffn_in = full[2].reshape(4, D, D).transpose(1, 0, 2).reshape(D, 4 * D)
    full_ffn_out = full[3].reshape(4 * D, D)
    full_gain_self, full_gain_cross, full_gain_ffn = small[:3]
    full_table = small[3:15, :NB].T
    weights = (full_gain_self, full_query_self, full_key_self, full_value_self, full_out_self, full_table,
        full_gain_cross, full_query_cross, full_key_cross, full_value_cross, full_out_cross, full_gain_ffn,
        full_ffn_in, full_ffn_out)
    gathered = weights
    examples, length, features = inputs.shape
    source = encoded.shape[1]
    row_count = examples * length
    residual = inputs.reshape(row_count, features).astype(jnp.float32)
    source_rows = encoded.reshape(examples * source, features)
    onehot = bucket_onehot(length).astype(jnp.bfloat16)
    rel_bias = jnp.einsum("ijb,bh->hij", onehot, gathered[5], preferred_element_type=jnp.float32)
    live_rows = (jnp.arange(length, dtype=jnp.int32)[None, :] < tgt_len[:, None]).reshape(
        row_count, 1
    )
    after_self, after_cross, result = run_forward(
        gathered, residual, source_rows, rel_bias, tgt_len, src_len, examples
    )
    layer_out = jnp.where(live_rows, result, 0.0).astype(jnp.bfloat16).reshape(inputs.shape)
    bias_back = rel_bias
    counts = task_counts.astype(jnp.float32)
    slice_share = lax.dynamic_index_in_dim(
        counts, lax.axis_index("task"), 0, keepdims=False
    ) / jnp.sum(counts)
    upstream_rows = jnp.where(
        live_rows, cotangent.reshape(row_count, features).astype(jnp.float32), 0.0
    )
    normed, inverse_rms, normed_ffn = norm_forward(after_cross, full_gain_ffn)
    pre_act = matmul(normed_ffn, full_ffn_in)
    activated, act_pullback = jax.vjp(smooth_act, pre_act)
    hidden = activated.astype(jnp.bfloat16)
    grad_branch = upstream_rows.astype(jnp.bfloat16)
    grad_ffn_out = outer_rows(hidden, grad_branch)
    grad_pre = act_pullback(times_transposed(grad_branch, full_ffn_out))[0].astype(jnp.bfloat16)
    grad_ffn_in = outer_rows(normed_ffn, grad_pre)
    grad_back, grad_gain_ffn = norm_backward(
        times_transposed(grad_pre, full_ffn_in), normed, inverse_rms, full_gain_ffn
    )
    grad_residual = upstream_rows + grad_back
    normed, inverse_rms, normed_cross = norm_forward(after_self, full_gain_cross)
    queries = split_heads(matmul(normed_cross, full_query_cross).astype(jnp.bfloat16), examples)
    keyset = split_heads(matmul(source_rows, full_key_cross).astype(jnp.bfloat16), examples)
    valueset = split_heads(matmul(source_rows, full_value_cross).astype(jnp.bfloat16), examples)
    grad_branch = grad_residual.astype(jnp.bfloat16)
    grad_mixture = split_heads(
        times_transposed(grad_branch, full_out_cross).astype(jnp.bfloat16), examples
    )

    def cross_back(element):
        return attend_backward(
            element[0],
            element[1],
            element[2],
            None,
            source_mask(length, source, element[3]),
            element[4],
            None,
        )

    mixture, grad_queries, grad_keys, grad_values, unused_table = lax.map(
        cross_back, (queries, keyset, valueset, src_len, grad_mixture)
    )
    mixture = mixture.reshape(row_count, features)
    grad_queries = grad_queries.reshape(row_count, features)
    grad_keys = grad_keys.reshape(examples * source, features)
    grad_values = grad_values.reshape(examples * source, features)
    grad_out_cross = outer_rows(mixture, grad_branch)
    grad_query_cross = outer_rows(normed_cross, grad_queries)
    grad_key_cross = outer_rows(source_rows, grad_keys)
    grad_value_cross = outer_rows(source_rows, grad_values)
    grad_source = times_transposed(grad_keys, full_key_cross) + times_transposed(
        grad_values, full_value_cross
    )
    grad_back, grad_gain_cross = norm_backward(
        times_transposed(grad_queries, full_query_cross), normed, inverse_rms, full_gain_cross
    )
    grad_residual = grad_residual + grad_back
    normed, inverse_rms, normed_self = norm_forward(residual, full_gain_self)
    queries = split_heads(matmul(normed_self, full_query_self).astype(jnp.bfloat16), examples)
    keyset = split_heads(matmul(normed_self, full_key_self).astype(jnp.bfloat16), examples)
    valueset = split_heads(matmul(normed_self, full_value_self).astype(jnp.bfloat16), examples)
    grad_branch = grad_residual.astype(jnp.bfloat16)
    grad_mixture = split_heads(
        times_transposed(grad_branch, full_out_self).astype(jnp.bfloat16), examples
    )

    def self_back(element):
        return attend_backward(
            element[0],
            element[1],
            element[2],
            bias_back,
            causal_mask(length, element[3]),
            element[4],
            onehot,
        )

    mixture, grad_queries, grad_keys, grad_values, table_terms = lax.map(
        self_back, (queries, keyset, valueset, tgt_len, grad_mixture)
    )
    mixture = mixture.reshape(row_count, features)
    grad_queries = grad_queries.reshape(row_count, features)
    grad_keys = grad_keys.reshape(row_count, features)
    grad_values = grad_values.reshape(row_count, features)
    grad_bias_table = jnp.sum(table_terms, axis=0)
    grad_out_self = outer_rows(mixture, grad_branch)
    grad_query_self = outer_rows(normed_self, grad_queries)
    grad_key_self = outer_rows(normed_self, grad_keys)
    grad_value_self = outer_rows(normed_self, grad_values)
    grad_normed = (
        times_transposed(grad_queries, full_query_self)
        + times_transposed(grad_keys, full_key_self)
        + times_transposed(grad_values, full_value_self)
    )
    grad_back, grad_gain_self = norm_backward(grad_normed, normed, inverse_rms, full_gain_self)
    grad_residual = grad_residual + grad_back

    def share(grad):
        return (grad * slice_share).astype(BF)

    zs = shards // COLS
    rows, wide = query_self.shape[0], ffn_out.shape[0] // 2
    unit = (4, zs, COLS, rows, D)
    parts = (
        jnp.stack([share(g) for g in (grad_query_self, grad_key_self, grad_value_self, grad_out_self)]).reshape(unit),
        jnp.stack([share(g) for g in (grad_query_cross, grad_key_cross, grad_value_cross, grad_out_cross)]).reshape(unit),
        share(grad_ffn_in).reshape(D, 4, D).transpose(1, 0, 2).reshape(unit),
        share(grad_ffn_out).reshape(zs, COLS, 2, wide, D),
    )
    small = jnp.zeros((SMALL, D), F32)
    small = small.at[0].set(grad_gain_self).at[1].set(grad_gain_cross).at[2].set(grad_gain_ffn)
    small = small.at[3:15, :NB].set(grad_bias_table.T) * slice_share
    sums = scatter_grads(tasks, shards, parts, small)
    grad_query_self, grad_key_self, grad_value_self, grad_out_self = sums[0].reshape(4, rows, D)
    grad_query_cross, grad_key_cross, grad_value_cross, grad_out_cross = sums[1].reshape(4, rows, D)
    grad_ffn_in = sums[2].reshape(4, rows, D).transpose(1, 0, 2).reshape(rows, 4 * D)
    grad_ffn_out = sums[3].reshape(2 * wide, D)
    grad_gain_self, grad_gain_cross, grad_gain_ffn = lax.dynamic_slice(sums[4], (0, place_s * rows), (3, rows))
    grad_bias_table = lax.dynamic_slice(sums[4], (3, place_s * bias_table.shape[0]), (H, bias_table.shape[0])).T
    grad_inputs = grad_residual.astype(jnp.bfloat16).reshape(inputs.shape)
    grad_encoded = grad_source.astype(jnp.bfloat16).reshape(encoded.shape)
    return (
        layer_out,
        grad_inputs,
        grad_encoded,
        grad_gain_self,
        grad_query_self,
        grad_key_self,
        grad_value_self,
        grad_out_self,
        grad_bias_table,
        grad_gain_cross,
        grad_query_cross,
        grad_key_cross,
        grad_value_cross,
        grad_out_cross,
        grad_gain_ffn,
        grad_ffn_in,
        grad_ffn_out,
    )


def solution(mesh):
    placed = (
        P(("task", "shard"), None, None),
        P(("task", "shard"), None, None),
        P(("task", "shard"), None, None),
        P(("task", "shard")),
        P(("task", "shard")),
        P(),
        P("shard"),
        P("shard", None),
        P("shard", None),
        P("shard", None),
        P("shard", None),
        P("shard", None),
        P("shard"),
        P("shard", None),
        P("shard", None),
        P("shard", None),
        P("shard", None),
        P("shard"),
        P("shard", None),
        P("shard", None),
    )
    return jax.shard_map(
        on_device,
        mesh=mesh,
        in_specs=placed,
        out_specs=(
            P(("task", "shard"), None, None),
            P(("task", "shard"), None, None),
            P(("task", "shard"), None, None),
            P("shard"),
            P("shard", None),
            P("shard", None),
            P("shard", None),
            P("shard", None),
            P("shard", None),
            P("shard"),
            P("shard", None),
            P("shard", None),
            P("shard", None),
            P("shard", None),
            P("shard"),
            P("shard", None),
            P("shard", None),
        ),
        check_vma=False,
    )
```

```python
import functools
import math

import jax
import jax.numpy as jnp
import numpy as np
from jax import lax
from jax.experimental import pallas as pl
from jax.experimental.pallas import tpu as pltpu
from jax.sharding import PartitionSpec as P

H = 12
DH = 64
NB = 32
D = 768
EPSILON = 1e-06
MASKED = -1000000000.0
LIMITS = np.array(
    list(range(1, 16))
    + [math.ceil(16.0 * 8.0 ** ((bucket - 16) / 16.0)) for bucket in range(16, 32)],
    dtype=np.int32,
)
MESH = pl.DeviceIdType.MESH
BF = jnp.bfloat16
F32 = jnp.float32
COLS = 4
SMALL = 16


class Place:
    def __init__(self, tasks, shards):
        self.tasks, self.zs = tasks, shards // COLS
        self.t, self.s = lax.axis_index("task"), lax.axis_index("shard")
        self.half = lax.rem(self.t, 2)
        self.other = 1 - self.half
        self.z, self.q = lax.div(self.s, COLS), lax.rem(self.s, COLS)
        flip_x = self.q + 1 - 2 * lax.rem(self.q, 2)
        flip_y = lax.rem(self.q + 2, COLS)
        self.qx, self.qy = flip_x, flip_y
        self.q2 = flip_x + self.half * (flip_y - flip_x)
        self.q3 = flip_y + self.half * (flip_x - flip_y)
        self.q4 = COLS - 1 - self.q
        self.core = (self.t + 1 - 2 * self.half, self.s)
        self.second = (self.t, self.z * COLS + self.q2)
        self.third = (self.t, self.z * COLS + self.q3)

    def along_z(self, step):
        z = lax.rem(self.z + step, self.zs)
        return z, (self.t, z * COLS + self.q)

    def along_task(self, step):
        return (lax.rem(self.t + 2 * step, self.tasks), self.s)

    def greet(self, task_peers):
        peers = [self.core, self.second, self.third]
        peers += [self.along_z(k)[1] for k in range(1, self.zs)]
        if task_peers:
            peers += [self.along_task(k) for k in range(1, self.tasks // 2)]
        barrier = pltpu.get_barrier_semaphore()
        for peer in peers:
            pl.semaphore_signal(barrier, inc=1, device_id=peer, device_id_type=MESH)
        pl.semaphore_wait(barrier, len(peers))


class Sends:
    def __init__(self, send_sem, recv_sem):
        self.send_sem, self.recv_sem, self.made, self.done = send_sem, recv_sem, {}, set()

    def copy(self, key):
        number, describe = self.made[key]
        src, dst, device = describe()
        return pltpu.make_async_remote_copy(
            src_ref=src,
            dst_ref=dst,
            send_sem=self.send_sem.at[number],
            recv_sem=self.recv_sem.at[number],
            device_id=device,
            device_id_type=MESH,
        )

    def start(self, key, describe):
        self.made[key] = (len(self.made), describe)
        self.copy(key).start()

    def arrived(self, key):
        self.copy(key).wait_recv()

    def sent(self, key):
        self.copy(key).wait_send()
        self.done.add(key)

    def finish(self):
        for key in [key for key in self.made if key not in self.done]:
            self.sent(key)


NS, QS, KS, VS, MS, NC, QC, KC, VC, MC, NF, G3, DQ, DK, DV = range(15)
DM = NF
ROWS = 512
BLOCK = 128
BLOCKS = ROWS // BLOCK


def dot(a, b):
    return jnp.dot(a, b, preferred_element_type=F32)


def dot_t(a, b):
    return lax.dot_general(a, b, (((1,), (1,)), ((), ())), preferred_element_type=F32)


def t_dot(a, b):
    return lax.dot_general(a, b, (((0,), (0,)), ((), ())), preferred_element_type=F32)


def normed(v):
    inverse = lax.rsqrt(jnp.mean(v * v, axis=-1, keepdims=True) + EPSILON)
    return v * inverse, inverse


def smooth_parts(v):
    c = math.sqrt(2.0 / math.pi)
    square = v * v
    tanh = jnp.tanh(v * (c + (c * 0.044715) * square))
    left = 0.5 * (1.0 + tanh)
    slope = left + 0.5 * v * (1.0 - tanh * tanh) * (c + (3.0 * c * 0.044715) * square)
    return v * left, slope


class Layer:
    def __init__(
        self, tgt_len, src_len, x, enc, w, wo, got_small, pi, po, act, after_self, after_cross, dn, small, dsmall, strip, line,
        key_mask, share,
    ):
        self.tgt_len = tgt_len
        self.src_len = src_len
        self.x = x
        self.enc = enc
        self.w = w
        self.wo = wo
        self.got_small = got_small
        self.pi = pi
        self.po = po
        self.act = act
        self.after_self = after_self
        self.after_cross = after_cross
        self.dn = dn
        self.small = small
        self.dsmall = dsmall
        self.strip = strip
        self.line = line
        self.key_mask = key_mask
        self.share = share

    def unit(self, n):
        return self.w[n].reshape(D, D)

    def live(self, start, size):
        rows = start + lax.broadcasted_iota(jnp.int32, (size, 1), 0)
        return rows < self.tgt_len[0]

    def gain(self, row):
        return self.small[pl.ds(row, 1), :]


    def sum_small(self):
        zs = self.got_small.shape[0]
        total = self.got_small[0, 0].astype(F32)
        for z in range(zs):
            for q in range(COLS):
                if z or q:
                    total = total + self.got_small[z, q].astype(F32)
        self.small[...] = total

    def masks(self):
        cols = lax.broadcasted_iota(jnp.int32, (8, ROWS), 1)
        self.key_mask[0:8, :] = jnp.where(cols < self.tgt_len[0], 0.0, MASKED)
        self.key_mask[8:16, :] = jnp.where(cols < self.src_len[0], 0.0, MASKED)

    def bucket_of(self, distance):
        bucket = jnp.zeros(distance.shape, jnp.int32)
        for limit in LIMITS:
            bucket = bucket + (distance >= int(limit)).astype(jnp.int32)
        return bucket

    def bias_strip(self):
        wide = 768
        lane = lax.broadcasted_iota(jnp.int32, (NB, wide), 1)
        bucket = self.bucket_of(jnp.maximum(511 - lane, 0))
        onehot = (bucket == lax.broadcasted_iota(jnp.int32, (NB, wide), 0)).astype(F32)
        table = self.small[:, 0:NB]
        line = jnp.dot(table, onehot, precision=lax.Precision.HIGHEST, preferred_element_type=F32)
        line = jnp.where(lax.broadcasted_iota(jnp.int32, (SMALL, wide), 1) <= 511, line, MASKED)
        self.line[...] = line

        @pl.loop(0, H)
        def _(h):
            row = jnp.broadcast_to(self.line[pl.ds(h + 3, 1), :], (BLOCK, wide))
            rolled = pltpu.roll(row, wide - 127, 1, stride=1, stride_axis=0)
            self.strip[h] = rolled[:, 0:ROWS].astype(BF)

    def clear_strip(self):
        self.dstrip[...] = jnp.zeros_like(self.dstrip)

    def bias_grad(self):
        wide = ROWS + BLOCK

        @pl.loop(0, H)
        def _(h):
            total = None
            for r in range(BLOCK // 8):
                rows = jnp.concatenate(
                    [self.dstrip[h, 8 * r : 8 * r + 8, :], jnp.zeros((8, BLOCK), F32)], axis=1
                )
                if r:
                    rows = pltpu.roll(rows, wide - 8 * r, 1)
                total = rows if total is None else total + rows
            self.lines[h] = total

        grad = jnp.zeros((H, NB), F32)
        lane = lax.broadcasted_iota(jnp.int32, (NB, wide), 1)
        for s in range(8):
            distance = ROWS - BLOCK + s - lane + jnp.where(lane >= ROWS, wide, 0)
            bucket = self.bucket_of(jnp.maximum(distance, 0))
            fits = bucket == lax.broadcasted_iota(jnp.int32, (NB, wide), 0)
            grad = grad + lax.dot_general(
                self.lines[:, s, :], fits.astype(F32), (((1,), (1,)), ((), ())),
                precision=lax.Precision.HIGHEST, preferred_element_type=F32,
            )
        self.dsmall[3 : 3 + H, 0:NB] = grad


    def norm_self(self):
        @pl.loop(0, BLOCKS)
        def _(i):
            rows = pl.ds(pl.multiple_of(i * BLOCK, BLOCK), BLOCK)
            n, _ = normed(self.x[rows, :].astype(F32))
            self.act[NS, rows, :] = (n * self.gain(0)).astype(BF)

    def pair(self, value, h):
        lane = lax.broadcasted_iota(jnp.int32, value.shape, 1)
        return jnp.where((lane < 64) == (h == 0), value, jnp.zeros_like(value))

    def probs(self, q, k, h, head, block, keys, cross):
        s = dot_t(self.pair(q, h), k)
        if cross:
            s = s + self.key_mask[8:9, 0:keys]
        else:
            s = s + (self.strip[head, :, ROWS - keys :].astype(F32) + self.key_mask[0:1, 0:keys])
        p = jnp.exp(s - jnp.max(s, axis=-1, keepdims=True))
        return p * (1.0 / jnp.sum(p, axis=-1, keepdims=True))

    def attend(self, hp, cross):
        base = NC if cross else NS
        cols = pl.ds(pl.multiple_of(hp * 128, 128), 128)
        k, v = self.act[base + 2, :, cols], self.act[base + 3, :, cols]
        for block in range(BLOCKS):
            rows = slice(block * BLOCK, (block + 1) * BLOCK)
            keys = ROWS if cross else (block + 1) * BLOCK
            q = self.act[base + 1, rows, cols]
            total = None
            for h in range(2):
                p = self.probs(q, k[:keys], h, 2 * hp + h, block, keys, cross).astype(BF)
                term = dot(p, self.pair(v[:keys], h))
                total = term if total is None else total + term
            self.act[base + 4, rows, cols] = total.astype(BF)

    def close_self(self):
        w = self.unit(3)
        for i in range(BLOCKS):
            rows = slice(i * BLOCK, (i + 1) * BLOCK)
            after = self.x[rows, :].astype(F32) + dot(self.act[MS, rows, :], w)
            self.after_self[rows, :] = after
            n, _ = normed(after)
            self.act[NC, rows, :] = (n * self.gain(1)).astype(BF)

    def project_query(self):
        self.act[QC] = dot(self.act[NC], self.unit(4)).astype(BF)

    def close_cross(self):
        w = self.unit(7)
        for i in range(BLOCKS):
            rows = slice(i * BLOCK, (i + 1) * BLOCK)
            after = self.after_self[rows, :] + dot(self.act[MC, rows, :], w)
            self.after_cross[rows, :] = after
            n, _ = normed(after)
            self.act[NF, rows, :] = (n * self.gain(2)).astype(BF)

    def live_cot(self):
        @pl.loop(0, BLOCKS)
        def _(i):
            start = pl.multiple_of(i * BLOCK, BLOCK)
            rows = pl.ds(start, BLOCK)
            cot = self.act[G3, rows, :]
            self.act[G3, rows, :] = jnp.where(self.live(start, BLOCK), cot, jnp.zeros_like(cot))

    def ffn_hidden(self, j):
        w = self.unit(8 + j)
        for i in range(BLOCKS):
            rows = slice(i * BLOCK, (i + 1) * BLOCK)
            act, slope = smooth_parts(dot(self.act[NF, rows, :], w))
            self.hidden[j, rows, :] = act.astype(BF)
            self.slope[j, rows, :] = slope.astype(BF)

    def outer(self, a, b, store):
        for m in range(2):
            cols = slice(m * 384, (m + 1) * 384)
            store(m, (t_dot(a[:, cols], b[...]) * self.share[0]).astype(BF))

    def grad_unit(self, n, a, b):
        zs = self.w.shape[1]
        half = zs // 2
        rows = self.w.shape[3]

        def store(m, value):
            place = self.w if 4 <= n < 8 else self.pi
            number = {0: n, 1: n + 4, 2: n - 8}[n // 4]
            place[number, m * half : (m + 1) * half] = value.reshape(half, COLS, rows, D)

        self.outer(a, b, store)

    def grad_ffn_out(self, j):
        zs, rows = self.wo.shape[0], self.wo.shape[3]
        eighth = zs // 4

        value = (t_dot(self.hidden[j], self.act[G3]) * self.share[0]).astype(BF)
        self.po[pl.ds(j * eighth, eighth)] = value.reshape(eighth, COLS, 4, rows, D)

    def ffn_out(self):
        for i in range(BLOCKS):
            rows = slice(i * BLOCK, (i + 1) * BLOCK)
            total = self.after_cross[rows, :]
            for j in range(4):
                total = total + dot(self.hidden[j, rows, :], self.wo_rows(j))
            self.act[DQ, rows, :] = jnp.where(self.live(i * BLOCK, BLOCK), total, 0.0).astype(BF)

    def wo_rows(self, j):
        eighth = self.wo.shape[0] // 4
        return self.wo[pl.ds(j * eighth, eighth)].reshape(D, D)


    def ffn_back(self, j):
        w, wo = self.unit(8 + j), self.wo_rows(j)
        for i in range(BLOCKS):
            rows = slice(i * BLOCK, (i + 1) * BLOCK)
            grad = dot_t(self.act[G3, rows, :], wo) * self.slope[j, rows, :].astype(F32)
            grad = grad.astype(BF)
            self.slope[j, rows, :] = grad
            back = dot_t(grad, w)

            @pl.when(j == 0)
            def _():
                self.dn[rows, :] = back

            @pl.when(j > 0)
            def _():
                self.dn[rows, :] += back

    def norm_back(self, values, gain_row, upstream, dst, branch):
        gain = self.gain(gain_row)
        dgain = jnp.zeros((1, D), F32)
        for i in range(BLOCKS):
            rows = slice(i * BLOCK, (i + 1) * BLOCK)
            n, inverse = normed(values(rows))
            dn = self.dn[rows, :]
            dgain = dgain + jnp.sum(dn * n, axis=0, keepdims=True)
            scaled = dn * gain
            back = inverse * (scaled - n * jnp.mean(scaled * n, axis=-1, keepdims=True))
            total = upstream(rows) + back
            if dst is not None:
                dst[rows, :] = total
            branch[rows, :] = total.astype(BF)
        self.dsmall[gain_row : gain_row + 1, :] = dgain

    def ffn_norm_back(self):
        self.norm_back(
            lambda rows: self.after_cross[rows, :], 2,
            lambda rows: self.act[G3, rows, :].astype(F32), self.after_cross, self.act.at[G3],
        )

    def mix_back(self, unit):
        self.act[DM] = dot_t(self.act[G3], self.unit(unit)).astype(BF)

    def attend_back(self, hp, cross):
        base, to = (NC, DQ) if cross else (NS, QC)
        cols = pl.ds(pl.multiple_of(hp * 128, 128), 128)
        k, v = self.act[base + 2, :, cols], self.act[base + 3, :, cols]
        halves = [(self.pair(k, h), h) for h in range(2)]
        self.dkv[...] = jnp.zeros_like(self.dkv)
        for block in range(BLOCKS):
            rows = slice(block * BLOCK, (block + 1) * BLOCK)
            keys = ROWS if cross else (block + 1) * BLOCK
            q, dm = self.act[base + 1, rows, cols], self.act[DM, rows, cols]
            mix = self.act[base + 4, rows, cols]
            prod = dm.astype(F32) * mix.astype(F32)
            dq = dk = dv = None
            for h in range(2):
                qh, dmh = self.pair(q, h), self.pair(dm, h)
                p = self.probs(q, k[:keys], h, 2 * hp + h, block, keys, cross)
                dp = dot_t(dmh, v[:keys])
                delta = jnp.sum(self.pair(prod, h), axis=-1, keepdims=True)
                ds = p * (dp - delta)
                if not cross:
                    self.dstrip[2 * hp + h, :, ROWS - keys :] += ds
                ds = ds.astype(BF)
                terms = (dot(ds, halves[h][0][:keys]), t_dot(ds, qh), t_dot(p.astype(BF), dmh))
                dq, dk, dv = terms if dq is None else (dq + terms[0], dk + terms[1], dv + terms[2])
            self.act[to, rows, cols] = dq.astype(BF)
            self.dkv[0, :keys] += dk
            self.dkv[1, :keys] += dv
        self.act[to + 1, :, cols] = self.dkv[0].astype(BF)
        self.act[to + 2, :, cols] = self.dkv[1].astype(BF)

    def source_back(self):
        for i in range(BLOCKS):
            rows = slice(i * BLOCK, (i + 1) * BLOCK)
            total = dot_t(self.act[DK, rows, :], self.unit(5)) + dot_t(self.act[DV, rows, :], self.unit(6))
            self.act[MC, rows, :] = total.astype(BF)

    def query_back(self):
        self.dn[...] = dot_t(self.act[DQ], self.unit(4))

    def cross_norm_back(self):
        self.norm_back(
            lambda rows: self.after_self[rows, :], 1,
            lambda rows: self.after_cross[rows, :], self.after_cross, self.act.at[G3],
        )

    def self_back(self):
        for i in range(BLOCKS):
            rows = slice(i * BLOCK, (i + 1) * BLOCK)
            total = dot_t(self.act[QC, rows, :], self.unit(0)) + dot_t(self.act[KC, rows, :], self.unit(1))
            self.dn[rows, :] = total + dot_t(self.act[VC, rows, :], self.unit(2))

    def self_norm_back(self):
        self.norm_back(
            lambda rows: self.x[rows, :].astype(F32), 0,
            lambda rows: self.after_cross[rows, :], None, self.act.at[NC],
        )


UNITS = 8
WINDOW = 2


class Plan:
    def __init__(self):
        self.work, self.events, self.at, self.log = [], [], {}, []
        self.now = 0.0

    def piece(self, name, cost, needs, run):
        self.work.append((name, cost, needs, run))

    def event(self, name, cost, needs, run):
        self.events.append((name, cost, needs, run))

    def due(self, needs):
        if any(name not in self.at for name, _ in needs):
            return None
        return max([self.at[name] + wait for name, wait in needs], default=0.0)

    def take(self, where, item, start):
        name, cost, _, run = item
        where.remove(item)
        self.now = max(self.now, start) + cost
        run()
        self.at[name] = self.now
        self.log.append((round(self.now, 1), name))

    def run_until(self, name):
        while (self.work or self.events) if name is None else name not in self.at:
            dues = [(self.due(item[2]), number) for number, item in enumerate(self.events)]
            dues = [pair for pair in dues if pair[0] is not None]
            first = min(dues, default=None)
            if first is not None and first[0] <= self.now:
                self.take(self.events, self.events[first[1]], first[0])
                continue
            ready = [item for item in self.work if all(name in self.at for name in item[2])]
            if ready:
                self.take(self.work, ready[0], self.now)
            else:
                self.take(self.events, self.events[first[1]], first[0])


class Gather:
    def __init__(self, place, layer, mats, small_ref, local_sem, sends):
        self.place, self.layer, self.mats, self.small_ref = place, layer, mats, small_ref
        self.local_sem, self.sends = local_sem, sends

    def column(self, c, q):
        if c < 6:
            return self.layer.w.at[2 * c + self.place.half, :, q]
        return self.layer.wo.at[:, q, 2 * (c - 6) + self.place.half]

    def slab(self, c, z, q):
        if c < 6:
            return self.layer.w.at[2 * c + self.place.half, z, q]
        return self.layer.wo.at[z, q, 2 * (c - 6) + self.place.half]

    def both(self, key, here, device):
        self.sends.start(key, lambda: (here(), here(), device()))

    def local(self):
        place, w, wo = self.place, self.layer.w, self.layer.wo
        z, q = place.z, place.q
        rows = w.shape[3]
        self.copies = []
        for n in range(16):
            if n < 8:
                src, dst = self.mats[n], w.at[n, z, q]
            elif n < 12:
                src, dst = self.mats[8].at[:, pl.ds(D * (n - 8), D)], w.at[n, z, q]
            else:
                src, dst = self.mats[9].at[pl.ds(rows * (n - 12), rows)], wo.at[z, q, n - 12]
            self.copies.append(pltpu.make_async_copy(src, dst, self.local_sem.at[n // 2]))
        for n in range(16):
            @pl.when(place.half == n % 2)
            def _():
                self.copies[n].start()
        self.small_copy = pltpu.make_async_copy(self.small_ref, self.layer.got_small.at[z, q], self.local_sem.at[8])
        self.small_copy.start()

    def start_small(self):
        self.small_copy.wait()
        place, got = self.place, self.layer.got_small
        for k in range(1, place.zs):
            self.both(("zs", k), lambda: got.at[place.z, place.q], lambda k=k: place.along_z(k)[1])

    def small_second(self):
        place, got = self.place, self.layer.got_small
        for k in range(1, place.zs):
            self.sends.arrived(("zs", k))
        self.both("as", lambda: got.at[:, place.q], lambda: place.second)
        self.both("bs", lambda: got.at[:, place.q], lambda: place.third)

    def small_third(self):
        place, got = self.place, self.layer.got_small
        self.sends.arrived("as")
        self.both("cs", lambda: got.at[:, place.q2], lambda: place.third)

    def small_ready(self):
        self.sends.arrived("bs")
        self.sends.arrived("cs")

    def start_z(self, c):
        place = self.place
        self.copies[2 * c].wait()
        for k in range(1, place.zs):
            self.both(("z", c, k), lambda: self.slab(c, place.z, place.q), lambda k=k: place.along_z(k)[1])

    def send_column(self, name, c, q, device):
        self.both((name, c), lambda: self.column(c, q), lambda: device)

    def from_z(self, c):
        place = self.place
        for k in range(1, place.zs):
            self.sends.arrived(("z", c, k))
        self.send_column("a", c, place.q, place.second)
        self.send_column("b", c, place.q, place.third)
        self.send_column("d1", c, place.q, place.core)

    def from_second(self, c):
        place = self.place
        self.sends.arrived(("a", c))
        self.send_column("c", c, place.q2, place.third)
        self.send_column("d2", c, place.q2, place.core)

    def from_third(self, c):
        place = self.place
        self.sends.arrived(("b", c))
        self.send_column("d3", c, place.q3, place.core)
        self.sends.arrived(("c", c))
        self.send_column("d4", c, place.q4, place.core)

    def sent(self, part):
        for c in range(2 * part, 2 * part + 2):
            for key in [("z", c, k) for k in range(1, self.place.zs)]:
                self.sends.sent(key)
            for name in ("a", "b", "c", "d1", "d2", "d3", "d4"):
                self.sends.sent((name, c))

    def ready(self, c):
        for name in ("d1", "d2", "d3", "d4"):
            self.sends.arrived((name, c))

    def plan(self, plan):
        hop = HOP
        plan.event("zs", 0.3, [], self.start_small)
        for c in range(UNITS):
            needs = [("zs", 0.0)] if c < AHEAD else [(f"a{c - AHEAD}", 0.0)]
            plan.event(f"z{c}", 0.2, needs, functools.partial(self.start_z, c))
            needs = [(f"z{c}", hop["z"])] + ([(f"a{c - 1}", hop["period"])] if c else [])
            plan.event(f"a{c}", 0.2, needs, functools.partial(self.from_z, c))
            plan.event(f"b{c}", 0.2, [(f"a{c}", hop["a"])], functools.partial(self.from_second, c))
            plan.event(f"c{c}", 0.2, [(f"b{c}", hop["c"])], functools.partial(self.from_third, c))
            plan.event(f"w{c}", 0.1, [(f"c{c}", hop["core"])], functools.partial(self.ready, c))
        plan.event("as", 0.2, [("zs", 2.5)], self.small_second)
        plan.event("cs", 0.1, [("as", 2.0)], self.small_third)
        plan.event("small", 0.1, [("cs", 2.0)], self.small_ready)


class Scatter:
    def __init__(self, place, layer, slots, outs, fin, from_task, tasks_here, credits, local_sem, task_sem, sends):
        self.place, self.layer, self.outs, self.fin, self.from_task = place, layer, outs, fin, from_task
        self.tasks_here, self.task_sem = tasks_here, task_sem
        self.from_core, self.from_third, self.from_second, self.from_z = slots
        self.core_credit, self.third_credit, self.second_credit, self.z_credit = credits
        self.local_sem, self.sends = local_sem, sends

    def part(self, c, part):
        layer = self.layer
        if c < 2:
            return layer.pi.at[2 * c + part]
        if c < 4:
            return layer.w.at[2 * c + part + 4]
        if c < 6:
            return layer.pi.at[2 * c + part - 8]
        return layer.po.at[:, :, 2 * (c - 6) + part]

    def column(self, c, q):
        if c < 6:
            return self.part(c, self.place.half).at[:, q]
        return self.layer.po.at[:, q, 2 * (c - 6) + self.place.half]

    def slab(self, c, z, q):
        if c < 6:
            return self.part(c, self.place.half).at[z, q]
        return self.layer.po.at[z, q, 2 * (c - 6) + self.place.half]

    def add(self, c, q, arrived):
        @pl.loop(0, self.place.zs)
        def _(z):
            here = self.slab(c, z, q)
            here[...] = (here[...].astype(F32) + arrived(z)[...].astype(F32)).astype(BF)

    def credit(self, semaphore, device):
        pl.semaphore_signal(semaphore, inc=1, device_id=device, device_id_type=MESH)

    def to_core(self, r, c):
        place = self.place
        if r >= WINDOW:
            pl.semaphore_wait(self.core_credit, 1)
        self.sends.start(("D", c), lambda: (self.part(c, place.other), self.from_core.at[r % WINDOW], place.core))

    def to_third(self, r, c, last):
        place, slot = self.place, r % WINDOW
        self.sends.arrived(("D", c))
        for q in (place.q4, place.q3):
            self.add(c, q, lambda z, q=q: self.from_core.at[slot, z, q])
        if r >= WINDOW:
            pl.semaphore_wait(self.third_credit, 1)
        self.sends.start(("C", c), lambda: (self.column(c, place.q4), self.from_third.at[slot, 1], place.third))
        self.sends.start(("B", c), lambda: (self.column(c, place.q3), self.from_third.at[slot, 0], place.third))
        for q in (place.q2, place.q):
            self.add(c, q, lambda z, q=q: self.from_core.at[slot, z, q])
        if not last:
            self.credit(self.core_credit, place.core)

    def to_second(self, r, c):
        place, slot = self.place, r % WINDOW
        self.sends.arrived(("C", c))
        self.add(c, place.q2, lambda z: self.from_third.at[slot, 1, z])
        if r >= WINDOW:
            pl.semaphore_wait(self.second_credit, 1)
        self.sends.start(("A", c), lambda: (self.column(c, place.q2), self.from_second.at[slot], place.second))

    def to_z(self, r, c, last):
        place, slot = self.place, r % WINDOW
        self.sends.arrived(("B", c))
        self.sends.arrived(("A", c))

        @pl.loop(0, place.zs)
        def _(z):
            here = self.slab(c, z, place.q)
            total = here[...].astype(F32) + self.from_third[slot, 0, z].astype(F32)
            here[...] = (total + self.from_second[slot, z].astype(F32)).astype(BF)

        if not last:
            self.credit(self.third_credit, place.third)
            self.credit(self.second_credit, place.second)
        for k in range(1, place.zs):
            if r >= WINDOW:
                pl.semaphore_wait(self.z_credit.at[k - 1], 1)

            def describe(k=k):
                to, device = place.along_z(k)
                return self.slab(c, to, place.q), self.from_z.at[slot, k - 1], device

            self.sends.start(("Z", c, k), describe)

    def target(self, c):
        half = self.place.half
        if c < 4:
            return self.outs[0].at[2 * c + half]
        if c < 6:
            return self.outs[1].at[:, pl.ds(pl.multiple_of((2 * c - 8 + half) * D, D), D)]
        return self.outs[2].at[2 * (c - 6) + half]

    def last(self, r, c, last):
        place, slot = self.place, r % WINDOW
        for k in range(1, place.zs):
            self.sends.arrived(("Z", c, k))
        total = self.slab(c, place.z, place.q)[...].astype(F32)
        for k in range(1, place.zs):
            total = total + self.from_z[slot, k - 1].astype(F32)
        if not last:
            for k in range(1, place.zs):
                self.credit(self.z_credit.at[k - 1], place.along_z(place.zs - k)[1])
        if r >= WINDOW:
            before = self.order[r - WINDOW]
            self.store(before).wait()
            self.sends.sent(("F", before))
        self.fin[slot] = total
        if place.tasks > 2:
            self.over_tasks(r, c, slot)
        self.store(c).start()
        self.sends.start(("F", c), lambda: (self.fin.at[slot], self.target(c), place.core))

    def over_tasks(self, r, c, slot):
        place, pairs = self.place, self.place.tasks // 2
        group = lax.div(place.t, 2)

        def local(src, dst):
            copy = pltpu.make_async_copy(src, dst, self.task_sem)
            copy.start()
            copy.wait()

        for k in range(1, pairs):
            self.sends.start(("T", c, k), lambda k=k: (
                self.fin.at[slot], self.from_task.at[r, lax.div(place.t, 2)], place.along_task(k)))
        local(self.fin.at[slot], self.from_task.at[r, group])
        for k in range(1, pairs):
            self.sends.arrived(("T", c, k))
        for k in range(1, pairs):
            self.sends.sent(("T", c, k))
        local(self.from_task.at[r], self.tasks_here)
        total = self.tasks_here[0]
        for k in range(1, pairs):
            total = total + self.tasks_here[k]
        self.fin[slot] = total

    def store(self, c):
        slot = self.order.index(c) % WINDOW
        return pltpu.make_async_copy(self.fin.at[slot], self.target(c), self.local_sem.at[slot])

    def sent(self, c):
        for name in "DCBA":
            self.sends.sent((name, c))
        for k in range(1, self.place.zs):
            self.sends.sent(("Z", c, k))

    def finish(self):
        for c in self.order[-WINDOW:]:
            self.store(c).wait()
        for c in self.order:
            self.sends.arrived(("F", c))

    def plan(self, plan, order, needs):
        self.order, hop = order, HOP
        for r, c in enumerate(order):
            last = r >= len(order) - WINDOW
            first = [(name, 0.0) for name in needs[c]]
            if r >= WINDOW:
                first.append((f"t{order[r - WINDOW]}", 1.0))
            plan.event(f"d{c}", 0.2, first, functools.partial(self.to_core, r, c))
            first = [(f"d{c}", hop["D"])]
            if r:
                first.append((f"t{order[r - 1]}", 1.0))
            if r >= WINDOW:
                first.append((f"y{order[r - WINDOW]}", 1.0))
            plan.event(f"t{c}", 1.4, first, functools.partial(self.to_third, r, c, last))
            first = [(f"t{c}", hop["C"])]
            if r >= WINDOW:
                first.append((f"y{order[r - WINDOW]}", 1.0))
            plan.event(f"s{c}", 0.5, first, functools.partial(self.to_second, r, c))
            first = [(f"s{c}", hop["A"])]
            if r >= WINDOW:
                first.append((f"l{order[r - WINDOW]}", 1.0))
            plan.event(f"y{c}", 0.7, first, functools.partial(self.to_z, r, c, last))
            plan.event(f"l{c}", 0.4, [(f"y{c}", hop["Z"])], functools.partial(self.last, r, c, last))


class SmallSums:
    def __init__(self, place, layer, slots, sends):
        self.place, self.layer, self.slots, self.sends = place, layer, slots, sends

    def device(self, number):
        place = self.place
        return [place.core, (place.t, place.z * COLS + place.qx), (place.t, place.z * COLS + place.qy)][number]

    def hop(self, number):
        place, slots = self.place, self.slots
        if number == 0:
            slots[0] = self.layer.dsmall[...] * self.layer.share[0]
        else:
            self.sends.arrived(("s", number - 1))
            slots[2 * number] = slots[2 * number - 2] + slots[2 * number - 1]
        if number < 3:
            self.sends.start(("s", number), lambda: (slots.at[2 * number], slots.at[2 * number + 1], self.device(number)))

    def along_z(self):
        place, slots = self.place, self.slots
        self.sends.arrived(("s", 2))
        mine = slots.at[6 + place.z]
        mine[...] = slots[4] + slots[5]
        for k in range(1, place.zs):
            self.sends.start(("sz", k), lambda k=k: (slots.at[6 + place.z], slots.at[6 + place.z], place.along_z(k)[1]))

    def end(self, out):
        place, slots = self.place, self.slots
        for k in range(1, place.zs):
            self.sends.arrived(("sz", k))
        total = slots[6]
        for k in range(1, place.zs):
            total = total + slots[6 + k]
        if place.tasks > 2:
            base, group = 6 + place.zs, lax.div(place.t, 2)
            mine = slots.at[base + group]
            mine[...] = total
            for k in range(1, place.tasks // 2):
                self.sends.start(("st", k), lambda k=k: (
                    slots.at[base + lax.div(place.t, 2)], slots.at[base + lax.div(place.t, 2)], place.along_task(k)))
            for k in range(1, place.tasks // 2):
                self.sends.arrived(("st", k))
            total = slots[base]
            for k in range(1, place.tasks // 2):
                total = total + slots[base + k]
        out[...] = total

    def plan(self, plan, needs, out):
        plan.event("m0", 0.1, [(name, 0.0) for name in needs], functools.partial(self.hop, 0))
        plan.event("m1", 0.1, [("m0", 2.0)], functools.partial(self.hop, 1))
        plan.event("m2", 0.1, [("m1", 3.0)], functools.partial(self.hop, 2))
        plan.event("m3", 0.1, [("m2", 3.0)], self.along_z)
        plan.event("m4", 0.1, [("m3", 4.0)], functools.partial(self.end, out))


HOP = {"z": 7.0, "period": 9.0, "a": 5.0, "c": 6.0, "core": 2.5, "D": 3.0, "C": 6.0, "A": 5.0, "Z": 6.0}
AHEAD = 2


def layer_kernel(tasks, shards, *refs):
    tgt_len, src_len, counts, x_hbm, enc_hbm, cot_hbm, small_ref = refs[:7]
    mats = refs[7:17]
    layer_out, grad_in, grad_enc, *outs, from_task, small_out = refs[17:25]
    (w, wo, pi, po, act, after_self, after_cross, dn, x, enc, got_small, small, dsmall, strip, line, key_mask,
     share, *slots_refs) = refs[25:]
    from_core, from_third, from_second, from_z, fin, tasks_here, small_slots = slots_refs[:7]
    credits, local_sem, in_sem, out_sem, send_sem, recv_sem = slots_refs[7:11], *slots_refs[11:]
    place = Place(tasks, shards)
    layer = Layer(
        tgt_len=tgt_len, src_len=src_len, x=x, enc=enc, w=w, wo=wo, got_small=got_small, pi=pi, po=po, act=act,
        after_self=after_self, after_cross=after_cross, dn=dn, small=small, dsmall=dsmall, strip=strip, line=line,
        key_mask=key_mask, share=share,
    )
    sends = Sends(send_sem, recv_sem)
    gather = Gather(place, layer, mats, small_ref, local_sem, sends)
    gather.local()
    loads = []
    for number, (src, dst) in enumerate([(x_hbm, x), (cot_hbm, act.at[G3]), (enc_hbm, enc)]):
        loads.append(pltpu.make_async_copy(src, dst, in_sem.at[number]))
        loads[-1].start()
    total = counts[0]
    for task in range(1, tasks):
        total = total + counts[task]
    share[0] = counts[place.t].astype(F32) / total.astype(F32)
    place.greet(True)
    scatter = Scatter(
        place, layer, (from_core, from_third, from_second, from_z), outs, fin, from_task, tasks_here, credits,
        local_sem.at[pl.ds(9, WINDOW)], local_sem.at[9 + WINDOW], sends,
    )
    tail = SmallSums(place, layer, small_slots, sends)
    plan = Plan()
    gather.plan(plan)
    stores = {}

    def store(number, slot, out):
        stores[number] = lambda: pltpu.make_async_copy(act.at[slot], out, out_sem.at[number])
        stores[number]().start()

    part = functools.partial

    def attend(cross, third):
        @pl.loop(0, H // 4)
        def _(hp):
            layer.attend(hp + third * (H // 4), cross)

    def attend_back(cross, third):
        @pl.loop(0, H // 6)
        def _(hp):
            layer.attend_back(hp + third * (H // 6), cross)

    def project_self(first, last):
        @pl.loop(first, last)
        def _(u):
            act[QS + u] = dot(act[NS], layer.unit(u)).astype(BF)

    def source(u):
        act[KC + u] = dot(enc[...], layer.unit(5 + u)).astype(BF)

    piece = plan.piece

    def begin():
        loads[1].wait()
        layer.masks()
        layer.live_cot()
        loads[0].wait()
        loads[2].wait()

    piece("begin", 0.8, ["zs"], begin)
    piece("strip", 1.5, ["small", "begin"], lambda: [layer.sum_small(), layer.bias_strip(), layer.norm_self()])
    piece("qk", 1.6, ["strip", "w0"], part(project_self, 0, 2))
    piece("v", 0.8, ["strip", "w1"], part(project_self, 2, 3))
    piece("self0", 5.3, ["qk", "v"], part(attend, False, 0))
    piece("self1", 5.3, ["self0"], part(attend, False, 1))
    piece("close_self", 1.5, ["self1"], layer.close_self)
    piece("kc", 0.8, ["w2", "begin"], part(source, 0))
    piece("qc", 0.8, ["close_self", "w2"], layer.project_query)
    piece("vc", 0.8, ["w3", "begin"], part(source, 1))
    piece("cross0", 6.0, ["qc", "kc", "vc"], part(attend, True, 0))
    piece("cross1", 6.0, ["cross0"], part(attend, True, 1))
    piece("close_cross", 0.7, ["cross1", "w3"], layer.close_cross)

    for c in range(4):
        piece(f"sent{c}", 0.1, [f"w{UNITS - 1}", "close_cross"] if c == 0 else [f"sent{c - 1}"], part(gather.sent, c))

    def ffn(hidden, slope):
        layer.hidden, layer.slope = hidden, slope
        for j in range(4):
            piece(f"h{j}", 2.0, ["close_cross", f"w{4 + j // 2}"], part(layer.ffn_hidden, j))
        for j in range(4):
            piece(f"go{j}", 1.4, [f"h{j}"], part(layer.grad_ffn_out, j))
        for j in range(4):
            piece(f"fb{j}", 3.0, [f"h{j}", "w6", "w7"], part(layer.ffn_back, j))
        for j in range(4):
            piece(f"gi{j}", 1.2, [f"fb{k}" for k in range(4)], part(layer.grad_unit, 8 + j, act.at[NF], slope.at[j]))
        piece("out", 6.7, [f"gi{j}" for j in range(4)], lambda: [layer.ffn_out(), store(0, DQ, layer_out)])
        plan.run_until("out")

    def back(dstrip, lines, dkv):
        layer.dstrip, layer.lines, layer.dkv = dstrip, lines, dkv
        piece("fnb", 2.0, ["out"], layer.ffn_norm_back)
        piece("g7", 1.2, ["fnb", "sent3"], part(layer.grad_unit, 7, act.at[MC], act.at[G3]))
        piece("dmc", 1.2, ["fnb"], part(layer.mix_back, 7))
        piece("kept", 0.1, ["dmc"], lambda: stores[0]().wait())
        for k in range(3):
            piece(f"bc{k}", 6.8, [f"bc{k - 1}"] if k else ["kept"], part(attend_back, True, k))
        piece("g6", 1.2, ["bc2", "sent3"], part(layer.grad_unit, 6, enc, act.at[DV]))
        piece("g5", 1.2, ["bc2", "sent3"], part(layer.grad_unit, 5, enc, act.at[DK]))
        piece("g4", 1.2, ["bc2", "sent3"], part(layer.grad_unit, 4, act.at[NC], act.at[DQ]))
        piece("qb", 1.5, ["bc2"], layer.query_back)
        piece("cnb", 2.0, ["qb"], layer.cross_norm_back)
        piece("dms", 1.2, ["cnb"], lambda: [layer.mix_back(3), layer.clear_strip()])
        for k in range(3):
            needs = [f"bs{k - 1}"] if k else ["dms", "g4"]
            piece(f"bs{k}", 5.5, needs, part(attend_back, False, k))
        piece("free", 0.1, ["bs2", "l4", "l5"], lambda: [scatter.sent(4), scatter.sent(5)])
        piece("g3", 1.2, ["free", "cnb"], part(layer.grad_unit, 3, act.at[MS], act.at[G3]))
        for k in (2, 1, 0):
            piece(f"g{k}", 1.2, ["free"], part(layer.grad_unit, k, act.at[NS], act.at[QC + k]))
        piece("sb", 5.0, ["bs2"], layer.self_back)
        piece("bias", 2.4, ["bs2"], layer.bias_grad)
        piece("snb", 2.0, ["sb", "g4"], lambda: [layer.self_norm_back(), store(1, NC, grad_in)])
        piece("eb", 5.0, ["bs2", "g7"], lambda: [layer.source_back(), store(2, MC, grad_enc)])
        plan.run_until(None)

    order = (6, 7, 4, 5, 3, 2, 1, 0)
    needs = {c: [f"g{2 * c}", f"g{2 * c + 1}"] for c in range(4)}
    needs.update({4: ["gi0", "gi1"], 5: ["gi2", "gi3"]})
    needs.update({c: [f"go{j}" for j in range(4)] + [f"w{UNITS - 1}"] for c in (6, 7)})
    scatter.plan(plan, order, needs)
    tail.plan(plan, ["snb", "bias", "cnb", "fnb"], small_out)
    pl.run_scoped(ffn, pltpu.VMEM((4, ROWS, D), BF), pltpu.VMEM((4, ROWS, D), BF))
    pl.run_scoped(
        back, pltpu.VMEM((H, BLOCK, ROWS), F32), pltpu.VMEM((H, 8, ROWS + BLOCK), F32), pltpu.VMEM((2, ROWS, 128), F32)
    )
    scatter.finish()
    stores[1]().wait()
    stores[2]().wait()
    sends.finish()


def run_layer(arrays, mats, small, counts, tasks, shards):
    zs, pairs, rows = shards // COLS, tasks // 2, mats[0].shape[0]
    shape = jax.ShapeDtypeStruct
    vmem = pltpu.VMEM
    unit = (zs, COLS, rows, D)
    full = shape((ROWS, D), BF)
    out_shape = (
        full, full, full,
        shape((8, rows, D), F32), shape((rows, 4 * D), F32), shape((4, rows, D), F32),
        shape((UNITS, pairs, rows, D) if tasks > 2 else (8, 128), F32), shape((SMALL, D), F32),
    )
    scratch = [
        vmem((12,) + unit, BF),
        vmem((zs, COLS, 4, rows, D), BF),
        vmem((4,) + unit, BF),
        vmem((zs, COLS, 4, rows, D), BF),
        vmem((15, ROWS, D), BF),
        vmem((ROWS, D), F32),
        vmem((ROWS, D), F32),
        vmem((ROWS, D), F32),
        vmem((ROWS, D), BF),
        vmem((ROWS, D), BF),
        vmem((zs, COLS, SMALL, D), BF),
        vmem((SMALL, D), F32),
        vmem((SMALL, D), F32),
        vmem((H, BLOCK, ROWS), BF),
        vmem((SMALL, D), F32),
        vmem((SMALL, ROWS), F32),
        pltpu.SMEM((1,), F32),
        vmem((WINDOW,) + unit, BF),
        vmem((WINDOW, 2, zs, rows, D), BF),
        vmem((WINDOW, zs, rows, D), BF),
        vmem((WINDOW, zs - 1, rows, D), BF),
        vmem((WINDOW, rows, D), F32),
        vmem((pairs, rows, D) if tasks > 2 else (8, 128), F32),
        vmem((6 + zs + pairs, SMALL, D), F32),
        pltpu.SemaphoreType.REGULAR,
        pltpu.SemaphoreType.REGULAR,
        pltpu.SemaphoreType.REGULAR,
        pltpu.SemaphoreType.REGULAR((zs - 1,)),
    ]
    number = UNITS * (zs - 1 + 7) + (zs - 1) + 3 + UNITS * (5 + zs - 1 + pairs - 1) + 3 + zs - 1 + pairs - 1
    scratch += [
        pltpu.SemaphoreType.DMA((10 + WINDOW,)),
        pltpu.SemaphoreType.DMA((3,)),
        pltpu.SemaphoreType.DMA((3,)),
        pltpu.SemaphoreType.DMA((number,)),
        pltpu.SemaphoreType.DMA((number,)),
    ]
    anywhere = pl.BlockSpec(memory_space=pl.ANY)
    return pl.pallas_call(
        functools.partial(layer_kernel, tasks, shards),
        out_shape=out_shape,
        in_specs=[pl.BlockSpec(memory_space=pltpu.SMEM)] * 3 + [anywhere] * 14,
        out_specs=[anywhere] * 7 + [pl.BlockSpec(memory_space=pltpu.VMEM)],
        scratch_shapes=scratch,
        compiler_params=pltpu.CompilerParams(
            collective_id=1, has_side_effects=True, vmem_limit_bytes=61 * 2**20
        ),
        cost_estimate=pl.CostEstimate(flops=35_000_000_000, bytes_accessed=60_000_000, transcendentals=10_000_000),
        name="layer",
    )(*counts, *arrays, small, *mats)


def on_device(
    inputs, encoded, cotangent, tgt_len, src_len, task_counts,
    gain_self, query_self, key_self, value_self, out_self, bias_table,
    gain_cross, query_cross, key_cross, value_cross, out_cross, gain_ffn, ffn_in, ffn_out,
):
    tasks, rows = task_counts.shape[0], gain_self.shape[0]
    shards, buckets = D // rows, bias_table.shape[0]
    at = lax.axis_index("shard")
    small = jnp.zeros((SMALL, D), BF)
    gains = jnp.stack([gain_self, gain_cross, gain_ffn])
    small = lax.dynamic_update_slice(small, gains, (0, at * rows))
    small = lax.dynamic_update_slice(small, bias_table.T, (3, at * buckets))
    mats = (
        query_self, key_self, value_self, out_self, query_cross, key_cross, value_cross, out_cross, ffn_in, ffn_out,
    )
    arrays = (inputs.reshape(ROWS, D), encoded.reshape(ROWS, D), cotangent.reshape(ROWS, D))
    layer_out, grad_in, grad_enc, units, g_in, g_out, _, sums = run_layer(
        arrays, mats, small, (tgt_len, src_len, task_counts), tasks, shards
    )
    g_gain = lax.dynamic_slice(sums, (0, at * rows), (3, rows))
    g_table = lax.dynamic_slice(sums, (3, at * buckets), (H, buckets)).T
    return (
        layer_out.reshape(inputs.shape), grad_in.reshape(inputs.shape), grad_enc.reshape(inputs.shape),
        g_gain[0], units[0], units[1], units[2], units[3], g_table,
        g_gain[1], units[4], units[5], units[6], units[7],
        g_gain[2], g_in, g_out.reshape(4 * rows, D),
    )


def solution(mesh):
    placed = (
        P(("task", "shard"), None, None),
        P(("task", "shard"), None, None),
        P(("task", "shard"), None, None),
        P(("task", "shard")),
        P(("task", "shard")),
        P(),
        P("shard"),
        P("shard", None),
        P("shard", None),
        P("shard", None),
        P("shard", None),
        P("shard", None),
        P("shard"),
        P("shard", None),
        P("shard", None),
        P("shard", None),
        P("shard", None),
        P("shard"),
        P("shard", None),
        P("shard", None),
    )
    return jax.shard_map(
        on_device,
        mesh=mesh,
        in_specs=placed,
        out_specs=(
            P(("task", "shard"), None, None),
            P(("task", "shard"), None, None),
            P(("task", "shard"), None, None),
            P("shard"),
            P("shard", None),
            P("shard", None),
            P("shard", None),
            P("shard", None),
            P("shard", None),
            P("shard"),
            P("shard", None),
            P("shard", None),
            P("shard", None),
            P("shard", None),
            P("shard"),
            P("shard", None),
            P("shard", None),
        ),
        check_vma=False,
    )
```

```python
import functools
import math

import jax
import jax.numpy as jnp
import numpy as np
from jax import lax
from jax.experimental import pallas as pl
from jax.experimental.pallas import tpu as pltpu
from jax.sharding import PartitionSpec as P

H = 12
DH = 64
NB = 32
D = 768
EPSILON = 1e-06
MASKED = -1000000000.0
LIMITS = np.array(
    list(range(1, 16))
    + [math.ceil(16.0 * 8.0 ** ((bucket - 16) / 16.0)) for bucket in range(16, 32)],
    dtype=np.int32,
)
MESH = pl.DeviceIdType.MESH
BF = jnp.bfloat16
F32 = jnp.float32
COLS = 4
SMALL = 16


class Place:
    def __init__(self, tasks, shards):
        self.tasks, self.zs = tasks, shards // COLS
        self.t, self.s = lax.axis_index("task"), lax.axis_index("shard")
        self.half = lax.rem(self.t, 2)
        self.other = 1 - self.half
        self.z, self.q = lax.div(self.s, COLS), lax.rem(self.s, COLS)
        flip_x = self.q + 1 - 2 * lax.rem(self.q, 2)
        flip_y = lax.rem(self.q + 2, COLS)
        self.qx, self.qy = flip_x, flip_y
        self.q2 = flip_x + self.half * (flip_y - flip_x)
        self.q3 = flip_y + self.half * (flip_x - flip_y)
        self.q4 = COLS - 1 - self.q
        self.core = (self.t + 1 - 2 * self.half, self.s)
        self.second = (self.t, self.z * COLS + self.q2)
        self.third = (self.t, self.z * COLS + self.q3)

    def along_z(self, step):
        z = lax.rem(self.z + step, self.zs)
        return z, (self.t, z * COLS + self.q)

    def along_task(self, step):
        return (lax.rem(self.t + 2 * step, self.tasks), self.s)

    def greet(self, task_peers):
        peers = [self.core, self.second, self.third]
        peers += [self.along_z(k)[1] for k in range(1, self.zs)]
        if task_peers:
            peers += [self.along_task(k) for k in range(1, self.tasks // 2)]
        barrier = pltpu.get_barrier_semaphore()
        for peer in peers:
            pl.semaphore_signal(barrier, inc=1, device_id=peer, device_id_type=MESH)
        pl.semaphore_wait(barrier, len(peers))


class Sends:
    def __init__(self, send_sem, recv_sem):
        self.send_sem, self.recv_sem, self.made, self.done = send_sem, recv_sem, {}, set()

    def copy(self, key):
        number, describe = self.made[key]
        src, dst, device = describe()
        return pltpu.make_async_remote_copy(
            src_ref=src,
            dst_ref=dst,
            send_sem=self.send_sem.at[number],
            recv_sem=self.recv_sem.at[number],
            device_id=device,
            device_id_type=MESH,
        )

    def start(self, key, describe):
        self.made[key] = (len(self.made), describe)
        self.copy(key).start()

    def arrived(self, key):
        self.copy(key).wait_recv()

    def sent(self, key):
        self.copy(key).wait_send()
        self.done.add(key)

    def finish(self):
        for key in [key for key in self.made if key not in self.done]:
            self.sent(key)


NS, QS, KS, VS, MS, NC, QC, KC, VC, MC, NF, G3, DQ, DK, DV = range(15)
DM = NF
ROWS = 512
BLOCK = 128
BLOCKS = ROWS // BLOCK
TALL = 256


def halves(body):
    @pl.loop(0, 2)
    def _(i):
        body(pl.ds(pl.multiple_of(i * (ROWS // 2), ROWS // 2), ROWS // 2))


def dot(a, b):
    return jnp.dot(a, b, preferred_element_type=F32)


def dot_t(a, b):
    return lax.dot_general(a, b, (((1,), (1,)), ((), ())), preferred_element_type=F32)


def t_dot(a, b):
    return lax.dot_general(a, b, (((0,), (0,)), ((), ())), preferred_element_type=F32)


def normed(v):
    inverse = lax.rsqrt(jnp.mean(v * v, axis=-1, keepdims=True) + EPSILON)
    return v * inverse, inverse


def smooth_parts(v):
    c = math.sqrt(2.0 / math.pi)
    square = v * v
    tanh = jnp.tanh(v * (c + (c * 0.044715) * square))
    left = 0.5 * (1.0 + tanh)
    slope = left + 0.5 * v * (1.0 - tanh * tanh) * (c + (3.0 * c * 0.044715) * square)
    return v * left, slope


class Layer:
    def __init__(
        self, tgt_len, src_len, x, enc, w, wo, pi, po, act, after_self, after_cross, upstream, dn, small, dsmall, strip, line,
        key_mask, share, places,
    ):
        self.tgt_len = tgt_len
        self.src_len = src_len
        self.x = x
        self.enc = enc
        self.w = w
        self.wo = wo
        self.pi = pi
        self.po = po
        self.act = act
        self.after_self = after_self
        self.after_cross = after_cross
        self.upstream = upstream
        self.dn = dn
        self.small = small
        self.dsmall = dsmall
        self.strip = strip
        self.line = line
        self.key_mask = key_mask
        self.share = share
        self.places = places

    def unit(self, n):
        return self.w[n].reshape(D, D)

    def live(self, start, size):
        rows = start + lax.broadcasted_iota(jnp.int32, (size, 1), 0)
        return rows < self.tgt_len[0]

    def gain(self, row):
        return self.small[pl.ds(row, 1), :]


    def sum_small(self):
        @pl.loop(0, self.places)
        def _(n):
            more = self.act[DV, pl.ds(pl.multiple_of(n * SMALL, SMALL), SMALL), :].astype(F32)
            self.add_rows(self.small, slice(0, SMALL), more, True)

    def masks(self):
        cols = lax.broadcasted_iota(jnp.int32, (8, ROWS), 1)
        self.key_mask[0:8, :] = jnp.where(cols < self.tgt_len[0], 0.0, MASKED)
        self.key_mask[8:16, :] = jnp.where(cols < self.src_len[0], 0.0, MASKED)

    def bucket_of(self, distance):
        bucket = jnp.zeros(distance.shape, jnp.int32)
        for limit in LIMITS:
            bucket = bucket + (distance >= int(limit)).astype(jnp.int32)
        return bucket

    def bias_strip(self):
        wide = 768
        lane = lax.broadcasted_iota(jnp.int32, (NB, wide), 1)
        bucket = self.bucket_of(jnp.maximum(511 - lane, 0))
        onehot = (bucket == lax.broadcasted_iota(jnp.int32, (NB, wide), 0)).astype(F32)
        table = self.small[:, 0:NB]
        line = jnp.dot(table, onehot, precision=lax.Precision.HIGHEST, preferred_element_type=F32)
        line = jnp.where(lax.broadcasted_iota(jnp.int32, (SMALL, wide), 1) <= 511, line, MASKED)
        self.line[...] = line

        @pl.loop(0, H)
        def _(h):
            row = jnp.broadcast_to(self.line[pl.ds(h + 3, 1), :], (BLOCK, wide))
            rolled = pltpu.roll(row, wide - 127, 1, stride=1, stride_axis=0)
            self.strip[h] = rolled[:, 0:ROWS].astype(BF)

    def clear_strip(self):
        self.dstrip[...] = jnp.zeros_like(self.dstrip)

    def bias_grad(self):
        wide = ROWS + BLOCK

        @pl.loop(0, H)
        def _(h):
            total = None
            for r in range(BLOCK // 8):
                rows = jnp.concatenate(
                    [self.dstrip[h, 8 * r : 8 * r + 8, :], jnp.zeros((8, BLOCK), F32)], axis=1
                )
                if r:
                    rows = pltpu.roll(rows, wide - 8 * r, 1)
                total = rows if total is None else total + rows
            self.lines[h] = total

        grad = jnp.zeros((H, NB), F32)
        lane = lax.broadcasted_iota(jnp.int32, (NB, wide), 1)
        for s in range(8):
            distance = ROWS - BLOCK + s - lane + jnp.where(lane >= ROWS, wide, 0)
            bucket = self.bucket_of(jnp.maximum(distance, 0))
            fits = bucket == lax.broadcasted_iota(jnp.int32, (NB, wide), 0)
            grad = grad + lax.dot_general(
                self.lines[:, s, :], fits.astype(F32), (((1,), (1,)), ((), ())),
                precision=lax.Precision.HIGHEST, preferred_element_type=F32,
            )
        self.dsmall[3 : 3 + H, 0:NB] = grad


    def norm_self(self):
        @pl.loop(0, BLOCKS)
        def _(i):
            rows = pl.ds(pl.multiple_of(i * BLOCK, BLOCK), BLOCK)
            n, _ = normed(self.x[rows, :].astype(F32))
            self.act[NS, rows, :] = (n * self.gain(0)).astype(BF)

    def pair(self, value, h):
        lane = lax.broadcasted_iota(jnp.int32, value.shape, 1)
        return jnp.where((lane < 64) == (h == 0), value, jnp.zeros_like(value))

    def probs(self, q, k, head, first, keys, cross):
        s = dot_t(q, k)
        if cross:
            s = s + self.key_mask[8:9, 0:keys]
        else:
            parts = []
            for here in range(first, keys, BLOCK):
                strip = self.strip[head, :, ROWS - here - BLOCK :].astype(F32)
                if here + BLOCK < keys:
                    beyond = jnp.full((BLOCK, keys - here - BLOCK), MASKED, F32)
                    strip = jnp.concatenate([strip, beyond], axis=1)
                parts.append(strip)
            s = s + (jnp.concatenate(parts, axis=0) + self.key_mask[0:1, 0:keys])
        p = jnp.exp(s - jnp.max(s, axis=-1, keepdims=True))
        return p * (1.0 / jnp.sum(p, axis=-1, keepdims=True))

    def attend(self, hp, cross):
        base = NC if cross else NS
        cols = pl.ds(pl.multiple_of(hp * 128, 128), 128)
        k, v = self.act[base + 2, :, cols], self.act[base + 3, :, cols]
        for first in range(0, ROWS, TALL):
            rows = slice(first, first + TALL)
            keys = ROWS if cross else first + TALL
            q = self.act[base + 1, rows, cols]
            total = None
            for h in range(2):
                p = self.probs(self.pair(q, h), k[:keys], 2 * hp + h, first, keys, cross).astype(BF)
                term = dot(p, self.pair(v[:keys], h))
                total = term if total is None else total + term
            self.act[base + 4, rows, cols] = total.astype(BF)

    def close_self(self):
        self.dn[...] = dot(self.act[MS], self.unit(3))

        @pl.loop(0, BLOCKS)
        def _(i):
            rows = pl.ds(pl.multiple_of(i * BLOCK, BLOCK), BLOCK)
            after = self.x[rows, :].astype(F32) + self.dn[rows, :]
            self.after_self[rows, :] = after
            n, _ = normed(after)
            self.act[NC, rows, :] = (n * self.gain(1)).astype(BF)

    def project_query(self):
        self.act[QC] = dot(self.act[NC], self.unit(4)).astype(BF)

    def close_cross(self):
        self.dn[...] = dot(self.act[MC], self.unit(7))

        @pl.loop(0, BLOCKS)
        def _(i):
            rows = pl.ds(pl.multiple_of(i * BLOCK, BLOCK), BLOCK)
            after = self.after_self[rows, :] + self.dn[rows, :]
            self.after_cross[rows, :] = after
            n, _ = normed(after)
            self.act[NF, rows, :] = (n * self.gain(2)).astype(BF)

    def live_cot(self):
        @pl.loop(0, BLOCKS)
        def _(i):
            start = pl.multiple_of(i * BLOCK, BLOCK)
            rows = pl.ds(start, BLOCK)
            cot = self.act[G3, rows, :]
            self.act[G3, rows, :] = jnp.where(self.live(start, BLOCK), cot, jnp.zeros_like(cot))

    def ffn_hidden(self, j):
        self.dn[...] = dot(self.act[NF], self.unit(8 + j))

        @pl.loop(0, BLOCKS)
        def _(i):
            rows = pl.ds(pl.multiple_of(i * BLOCK, BLOCK), BLOCK)
            act, slope = smooth_parts(self.dn[rows, :])
            self.hidden[j, rows, :] = act.astype(BF)
            self.slope[j, rows, :] = slope.astype(BF)

    def outer(self, a, b, store):
        @pl.loop(0, 2)
        def _(m):
            cols = pl.ds(pl.multiple_of(m * 384, 128), 384)
            store(m, (t_dot(a[:, cols], b[...]) * self.share[0]).astype(BF))

    def grad_unit(self, n, a, b):
        half, rows = self.w.shape[1] // 2, self.w.shape[3]
        place = self.w if n < 8 else self.pi
        number = {0: n, 1: n + 4, 2: n - 8}[n // 4]

        def store(m, value):
            place[number, pl.ds(m * half, half)] = value.reshape(half, COLS, rows, D)

        self.outer(a, b, store)

    def grad_ffn_out(self, j):
        some, rows = self.wo.shape[0] // 4, self.wo.shape[3]

        def store(m, value):
            if some == 1:
                self.po[j, pl.ds(2 * m, 2)] = value.reshape(2, 4, rows, D)
            else:
                self.po[pl.ds(j * some + m * (some // 2), some // 2)] = value.reshape(some // 2, COLS, 4, rows, D)

        self.outer(self.hidden.at[j], self.act.at[G3], store)

    def ffn_out(self, j):
        @halves
        def _(rows):
            self.after_cross[rows, :] += dot(self.hidden[j, rows, :], self.wo_rows(j))

    def ffn_result(self):
        @pl.loop(0, BLOCKS)
        def _(i):
            start = pl.multiple_of(i * BLOCK, BLOCK)
            rows = pl.ds(start, BLOCK)
            self.act[DQ, rows, :] = jnp.where(self.live(start, BLOCK), self.after_cross[rows, :], 0.0).astype(BF)

    def wo_rows(self, j):
        eighth = self.wo.shape[0] // 4
        return self.wo[pl.ds(j * eighth, eighth)].reshape(D, D)


    def ffn_back(self, j):
        @halves
        def _(rows):
            grad = dot_t(self.act[G3, rows, :], self.wo_rows(j)) * self.slope[j, rows, :].astype(F32)
            self.slope[j, rows, :] = grad.astype(BF)
        @halves
        def _(rows):
            self.add_rows(self.dn, rows, dot_t(self.slope[j, rows, :], self.unit(8 + j)), j)

    def add_rows(self, ref, rows, value, more):
        if more:
            ref[rows, :] += value
        else:
            ref[rows, :] = value

    def norm_back(self, values, gain_row, upstream, dst, branch):
        self.dsmall[gain_row : gain_row + 1, :] = jnp.zeros((1, D), F32)

        @pl.loop(0, BLOCKS)
        def _(i):
            rows = pl.ds(pl.multiple_of(i * BLOCK, BLOCK), BLOCK)
            n, inverse = normed(values(rows))
            dn = self.dn[rows, :]
            self.dsmall[gain_row : gain_row + 1, :] += jnp.sum(dn * n, axis=0, keepdims=True)
            scaled = dn * self.gain(gain_row)
            back = inverse * (scaled - n * jnp.mean(scaled * n, axis=-1, keepdims=True))
            total = upstream(rows) + back
            if dst is not None:
                dst[rows, :] = total
            branch[rows, :] = total.astype(BF)

    def ffn_norm_back(self):
        self.norm_back(
            lambda rows: self.after_cross[rows, :], 2,
            lambda rows: self.act[G3, rows, :].astype(F32), self.upstream, self.act.at[G3],
        )

    def mix_back(self, unit):
        self.act[DM] = dot_t(self.act[G3], self.unit(unit)).astype(BF)

    def attend_back(self, hp, cross):
        base, to = (NC, DQ) if cross else (NS, QC)
        cols = pl.ds(pl.multiple_of(hp * 128, 128), 128)
        k, v = self.act[base + 2, :, cols], self.act[base + 3, :, cols]
        own = [self.pair(k, h) for h in range(2)]
        for first in reversed(range(0, ROWS, TALL)):
            rows = slice(first, first + TALL)
            keys = ROWS if cross else first + TALL
            q, dm = self.act[base + 1, rows, cols], self.act[DM, rows, cols]
            prod = dm.astype(F32) * self.act[base + 4, rows, cols].astype(F32)
            dq = dk = dv = None
            for h in range(2):
                qh, dmh = self.pair(q, h), self.pair(dm, h)
                p = self.probs(qh, k[:keys], 2 * hp + h, first, keys, cross)
                dp = dot_t(dmh, v[:keys])
                delta = jnp.sum(self.pair(prod, h), axis=-1, keepdims=True)
                ds = p * (dp - delta)
                if not cross:
                    for here in range(first, keys, BLOCK):
                        upto = here + BLOCK
                        self.dstrip[2 * hp + h, :, ROWS - upto :] += ds[here - first : upto - first, :upto]
                ds = ds.astype(BF)
                terms = (dot(ds, own[h][:keys]), t_dot(ds, qh), t_dot(p.astype(BF), dmh))
                dq, dk, dv = terms if dq is None else (dq + terms[0], dk + terms[1], dv + terms[2])
            self.act[to, rows, cols] = dq.astype(BF)
            self.add_rows(self.dn.at[:, 0:128], slice(0, keys), dk, first + TALL < ROWS)
            self.add_rows(self.dn.at[:, 128:256], slice(0, keys), dv, first + TALL < ROWS)
        self.act[to + 1, :, cols] = self.dn[:, 0:128].astype(BF)
        self.act[to + 2, :, cols] = self.dn[:, 128:256].astype(BF)

    def source_back(self, k):
        @halves
        def _(rows):
            back = dot_t(self.act[DK + k, rows, :], self.unit(5 + k))
            if k:
                self.act[MC, rows, :] = (self.after_self[rows, :] + back).astype(BF)
            else:
                self.after_self[rows, :] = back

    def query_back(self):
        self.dn[...] = dot_t(self.act[DQ], self.unit(4))

    def cross_norm_back(self):
        self.norm_back(
            lambda rows: self.after_self[rows, :], 1,
            lambda rows: self.upstream[rows, :], self.upstream, self.act.at[G3],
        )

    def self_back(self, k):
        @halves
        def _(rows):
            self.add_rows(self.dn, rows, dot_t(self.act[QC + k, rows, :], self.unit(k)), k)

    def self_norm_back(self):
        self.norm_back(
            lambda rows: self.x[rows, :].astype(F32), 0,
            lambda rows: self.upstream[rows, :], None, self.act.at[NC],
        )


UNITS = 8
WINDOW = 2


class Plan:
    def __init__(self):
        self.work, self.events, self.at, self.log = [], [], {}, []
        self.now = 0.0

    def piece(self, name, cost, needs, run):
        self.work.append((name, cost, needs, run))

    def event(self, name, cost, needs, run):
        self.events.append((name, cost, needs, run))

    def due(self, needs):
        if any(name not in self.at for name, _ in needs):
            return None
        return max([self.at[name] + wait for name, wait in needs], default=0.0)

    def take(self, where, item, start):
        name, cost, _, run = item
        where.remove(item)
        self.now = max(self.now, start) + cost
        run()
        self.at[name] = self.now
        self.log.append((round(self.now, 1), name))

    def run_until(self, name):
        while (self.work or self.events) if name is None else any(each not in self.at for each in name):
            dues = [(self.due(item[2]), number) for number, item in enumerate(self.events)]
            dues = [pair for pair in dues if pair[0] is not None]
            first = min(dues, default=None)
            if first is not None and first[0] <= self.now:
                self.take(self.events, self.events[first[1]], first[0])
                continue
            ready = [item for item in self.work if all(name in self.at for name in item[2])]
            if ready:
                self.take(self.work, ready[0], self.now)
            else:
                self.take(self.events, self.events[first[1]], first[0])


class Gather:
    def __init__(self, place, layer, mats, small_ref, local_sem, sends):
        self.place, self.layer, self.mats, self.small_ref = place, layer, mats, small_ref
        self.local_sem, self.sends = local_sem, sends

    def column(self, c, q):
        if c < 6:
            return self.layer.w.at[2 * c + self.place.half, :, q]
        return self.layer.wo.at[:, q, 2 * (c - 6) + self.place.half]

    def slab(self, c, z, q):
        if c < 6:
            return self.layer.w.at[2 * c + self.place.half, z, q]
        return self.layer.wo.at[z, q, 2 * (c - 6) + self.place.half]

    def both(self, key, here, device):
        self.sends.start(key, lambda: (here(), here(), device()))

    def local(self):
        place, w, wo = self.place, self.layer.w, self.layer.wo
        z, q = place.z, place.q
        rows = w.shape[3]
        self.copies = []
        for n in range(16):
            if n < 8:
                src, dst = self.mats[n], w.at[n, z, q]
            elif n < 12:
                src, dst = self.mats[8].at[:, pl.ds(D * (n - 8), D)], w.at[n, z, q]
            else:
                src, dst = self.mats[9].at[pl.ds(rows * (n - 12), rows)], wo.at[z, q, n - 12]
            self.copies.append(pltpu.make_async_copy(src, dst, self.local_sem.at[n // 2]))
        for n in range(16):
            @pl.when(place.half == n % 2)
            def _():
                self.copies[n].start()
        self.small_copy = pltpu.make_async_copy(self.small_ref, self.small_at(z, q), self.local_sem.at[8])
        self.small_copy.start()

    def small_at(self, z, q):
        row = (q * self.place.zs + z) * SMALL
        return self.layer.act.at[DV, pl.ds(pl.multiple_of(row, SMALL), SMALL)]

    def small_column(self, q):
        size = self.place.zs * SMALL
        return self.layer.act.at[DV, pl.ds(pl.multiple_of(q * size, SMALL), size)]

    def start_small(self):
        self.small_copy.wait()
        place = self.place
        for k in range(1, place.zs):
            self.both(("zs", k), lambda: self.small_at(place.z, place.q), lambda k=k: place.along_z(k)[1])

    def small_second(self):
        place = self.place
        for k in range(1, place.zs):
            self.sends.arrived(("zs", k))
        self.both("as", lambda: self.small_column(place.q), lambda: place.second)
        self.both("bs", lambda: self.small_column(place.q), lambda: place.third)

    def small_third(self):
        place = self.place
        self.sends.arrived("as")
        self.both("cs", lambda: self.small_column(place.q2), lambda: place.third)

    def small_ready(self):
        self.sends.arrived("bs")
        self.sends.arrived("cs")

    def start_z(self, c):
        place = self.place
        self.copies[2 * c].wait()
        for k in range(1, place.zs):
            self.both(("z", c, k), lambda: self.slab(c, place.z, place.q), lambda k=k: place.along_z(k)[1])

    def send_column(self, name, c, q, device):
        self.both((name, c), lambda: self.column(c, q), lambda: device)

    def from_z(self, c):
        place = self.place
        for k in range(1, place.zs):
            self.sends.arrived(("z", c, k))
        self.send_column("a", c, place.q, place.second)
        self.send_column("b", c, place.q, place.third)
        self.send_column("d1", c, place.q, place.core)

    def from_second(self, c):
        place = self.place
        self.sends.arrived(("a", c))
        self.send_column("c", c, place.q2, place.third)
        self.send_column("d2", c, place.q2, place.core)

    def from_third(self, c):
        place = self.place
        self.sends.arrived(("b", c))
        self.send_column("d3", c, place.q3, place.core)
        self.sends.arrived(("c", c))
        self.send_column("d4", c, place.q4, place.core)

    def sent(self, part):
        for c in range(2 * part, 2 * part + 2):
            for key in [("z", c, k) for k in range(1, self.place.zs)]:
                self.sends.sent(key)
            for name in ("a", "b", "c", "d1", "d2", "d3", "d4"):
                self.sends.sent((name, c))
        if part == 3:
            for key in [("zs", k) for k in range(1, self.place.zs)] + ["as", "bs", "cs"]:
                self.sends.sent(key)

    def ready(self, c):
        for name in ("d1", "d2", "d3", "d4"):
            self.sends.arrived((name, c))

    def plan(self, plan):
        hop = HOP
        plan.event("zs", 0.3, [], self.start_small)
        for c in range(UNITS):
            needs = [("zs", 0.0)] if c < AHEAD else [(f"a{c - AHEAD}", 0.0)]
            plan.event(f"z{c}", 0.2, needs, functools.partial(self.start_z, c))
            needs = [(f"z{c}", hop["z"])] + ([(f"a{c - 1}", hop["period"])] if c else [])
            plan.event(f"a{c}", 0.2, needs, functools.partial(self.from_z, c))
            plan.event(f"b{c}", 0.2, [(f"a{c}", hop["a"])], functools.partial(self.from_second, c))
            plan.event(f"c{c}", 0.2, [(f"b{c}", hop["c"])], functools.partial(self.from_third, c))
            plan.event(f"w{c}", 0.1, [(f"c{c}", hop["core"])], functools.partial(self.ready, c))
        plan.event("as", 0.2, [("zs", 2.5)], self.small_second)
        plan.event("cs", 0.1, [("as", 2.0)], self.small_third)
        plan.event("small", 0.1, [("cs", 2.0)], self.small_ready)


class Scatter:
    def __init__(self, place, layer, slots, outs, fin, from_task, tasks_here, credits, local_sem, task_sem, sends):
        self.place, self.layer, self.outs, self.fin, self.from_task = place, layer, outs, fin, from_task
        self.tasks_here, self.task_sem = tasks_here, task_sem
        self.from_core, self.from_third, self.from_second, self.from_z = slots
        self.core_credit, self.third_credit, self.second_credit, self.z_credit = credits
        self.local_sem, self.sends = local_sem, sends

    def part(self, c, part):
        layer = self.layer
        if c < 2:
            return layer.w.at[2 * c + part]
        if c < 4:
            return layer.w.at[2 * c + part + 4]
        if c < 6:
            return layer.pi.at[2 * c + part - 8]
        return layer.po.at[:, :, 2 * (c - 6) + part]

    def column(self, c, q):
        if c < 6:
            return self.part(c, self.place.half).at[:, q]
        return self.layer.po.at[:, q, 2 * (c - 6) + self.place.half]

    def slab(self, c, z, q):
        if c < 6:
            return self.part(c, self.place.half).at[z, q]
        return self.layer.po.at[z, q, 2 * (c - 6) + self.place.half]

    def add(self, c, q, arrived):
        @pl.loop(0, self.place.zs)
        def _(z):
            here = self.slab(c, z, q)
            here[...] = (here[...].astype(F32) + arrived(z)[...].astype(F32)).astype(BF)

    def credit(self, semaphore, device):
        pl.semaphore_signal(semaphore, inc=1, device_id=device, device_id_type=MESH)

    def to_core(self, r, c):
        place = self.place
        if r >= WINDOW:
            pl.semaphore_wait(self.core_credit, 1)
        self.sends.start(("D", c), lambda: (self.part(c, place.other), self.from_core.at[r % WINDOW], place.core))

    def to_third(self, r, c, last):
        place, slot = self.place, r % WINDOW
        self.sends.arrived(("D", c))
        for q in (place.q4, place.q3):
            self.add(c, q, lambda z, q=q: self.from_core.at[slot, z, q])
        if r >= WINDOW:
            pl.semaphore_wait(self.third_credit, 1)
        self.sends.start(("C", c), lambda: (self.column(c, place.q4), self.from_third.at[slot, 1], place.third))
        self.sends.start(("B", c), lambda: (self.column(c, place.q3), self.from_third.at[slot, 0], place.third))
        for q in (place.q2, place.q):
            self.add(c, q, lambda z, q=q: self.from_core.at[slot, z, q])
        if not last:
            self.credit(self.core_credit, place.core)

    def to_second(self, r, c):
        place, slot = self.place, r % WINDOW
        self.sends.arrived(("C", c))
        self.add(c, place.q2, lambda z: self.from_third.at[slot, 1, z])
        if r >= WINDOW:
            pl.semaphore_wait(self.second_credit, 1)
        self.sends.start(("A", c), lambda: (self.column(c, place.q2), self.from_second.at[slot], place.second))

    def to_z(self, r, c, last):
        place, slot = self.place, r % WINDOW
        self.sends.arrived(("B", c))
        self.sends.arrived(("A", c))

        @pl.loop(0, place.zs)
        def _(z):
            here = self.slab(c, z, place.q)
            total = here[...].astype(F32) + self.from_third[slot, 0, z].astype(F32)
            here[...] = (total + self.from_second[slot, z].astype(F32)).astype(BF)

        if not last:
            self.credit(self.third_credit, place.third)
            self.credit(self.second_credit, place.second)
        for k in range(1, place.zs):
            if r >= WINDOW:
                pl.semaphore_wait(self.z_credit.at[k - 1], 1)

            def describe(k=k):
                to, device = place.along_z(k)
                return self.slab(c, to, place.q), self.from_z.at[slot, k - 1], device

            self.sends.start(("Z", c, k), describe)

    def target(self, c):
        half = self.place.half
        if c < 4:
            return self.outs[0].at[2 * c + half]
        if c < 6:
            return self.outs[1].at[:, pl.ds(pl.multiple_of((2 * c - 8 + half) * D, D), D)]
        return self.outs[2].at[2 * (c - 6) + half]

    def last(self, r, c, last):
        place, slot = self.place, r % WINDOW
        for k in range(1, place.zs):
            self.sends.arrived(("Z", c, k))
        total = self.slab(c, place.z, place.q)[...].astype(F32)
        for k in range(1, place.zs):
            total = total + self.from_z[slot, k - 1].astype(F32)
        if not last:
            for k in range(1, place.zs):
                self.credit(self.z_credit.at[k - 1], place.along_z(place.zs - k)[1])
        if r >= WINDOW:
            before = self.order[r - WINDOW]
            self.store(before).wait()
            self.sends.sent(("F", before))
        self.fin[slot] = total
        if place.tasks > 2:
            self.over_tasks(r, c, slot)
        self.store(c).start()
        self.sends.start(("F", c), lambda: (self.fin.at[slot], self.target(c), place.core))

    def over_tasks(self, r, c, slot):
        place, pairs = self.place, self.place.tasks // 2
        group = lax.div(place.t, 2)

        def local(src, dst):
            copy = pltpu.make_async_copy(src, dst, self.task_sem)
            copy.start()
            copy.wait()

        for k in range(1, pairs):
            self.sends.start(("T", c, k), lambda k=k: (
                self.fin.at[slot], self.from_task.at[r, lax.div(place.t, 2)], place.along_task(k)))
        local(self.fin.at[slot], self.from_task.at[r, group])
        for k in range(1, pairs):
            self.sends.arrived(("T", c, k))
        for k in range(1, pairs):
            self.sends.sent(("T", c, k))
        local(self.from_task.at[r], self.tasks_here)
        total = self.tasks_here[0]
        for k in range(1, pairs):
            total = total + self.tasks_here[k]
        self.fin[slot] = total

    def store(self, c):
        slot = self.order.index(c) % WINDOW
        return pltpu.make_async_copy(self.fin.at[slot], self.target(c), self.local_sem.at[slot])

    def sent(self, c):
        for name in "DCBA":
            self.sends.sent((name, c))
        for k in range(1, self.place.zs):
            self.sends.sent(("Z", c, k))

    def finish(self):
        for c in self.order[-WINDOW:]:
            self.store(c).wait()
        for c in self.order:
            self.sends.arrived(("F", c))

    def plan(self, plan, order, needs):
        self.order, hop = order, HOP
        for r, c in enumerate(order):
            last = r >= len(order) - WINDOW
            first = [(name, 0.0) for name in needs[c]]
            if r >= WINDOW:
                first.append((f"t{order[r - WINDOW]}", 1.0))
            plan.event(f"d{c}", 0.2, first, functools.partial(self.to_core, r, c))
            first = [(f"d{c}", hop["D"])]
            if r:
                first.append((f"t{order[r - 1]}", hop["turn"]))
            if r >= WINDOW:
                first.append((f"y{order[r - WINDOW]}", 1.0))
            plan.event(f"t{c}", 1.4, first, functools.partial(self.to_third, r, c, last))
            first = [(f"t{c}", hop["C"])]
            if r >= WINDOW:
                first.append((f"y{order[r - WINDOW]}", 1.0))
            plan.event(f"s{c}", 0.5, first, functools.partial(self.to_second, r, c))
            first = [(f"s{c}", hop["A"])]
            if r >= WINDOW:
                first.append((f"l{order[r - WINDOW]}", 1.0))
            plan.event(f"y{c}", 0.7, first, functools.partial(self.to_z, r, c, last))
            plan.event(f"l{c}", 0.4, [(f"y{c}", hop["Z"])], functools.partial(self.last, r, c, last))


class SmallSums:
    def __init__(self, place, layer, slots, sends):
        self.place, self.layer, self.slots, self.sends = place, layer, slots, sends

    def device(self, number):
        place = self.place
        return [place.core, (place.t, place.z * COLS + place.qx), (place.t, place.z * COLS + place.qy)][number]

    def hop(self, number):
        place, slots = self.place, self.slots
        if number == 0:
            slots[0] = self.layer.dsmall[...] * self.layer.share[0]
        else:
            self.sends.arrived(("s", number - 1))
            slots[2 * number] = slots[2 * number - 2] + slots[2 * number - 1]
        if number < 3:
            self.sends.start(("s", number), lambda: (slots.at[2 * number], slots.at[2 * number + 1], self.device(number)))

    def along_z(self):
        place, slots = self.place, self.slots
        self.sends.arrived(("s", 2))
        mine = slots.at[6 + place.z]
        mine[...] = slots[4] + slots[5]
        for k in range(1, place.zs):
            self.sends.start(("sz", k), lambda k=k: (slots.at[6 + place.z], slots.at[6 + place.z], place.along_z(k)[1]))

    def end(self, out):
        place, slots = self.place, self.slots
        for k in range(1, place.zs):
            self.sends.arrived(("sz", k))
        total = slots[6]
        for k in range(1, place.zs):
            total = total + slots[6 + k]
        if place.tasks > 2:
            base, group = 6 + place.zs, lax.div(place.t, 2)
            mine = slots.at[base + group]
            mine[...] = total
            for k in range(1, place.tasks // 2):
                self.sends.start(("st", k), lambda k=k: (
                    slots.at[base + lax.div(place.t, 2)], slots.at[base + lax.div(place.t, 2)], place.along_task(k)))
            for k in range(1, place.tasks // 2):
                self.sends.arrived(("st", k))
            total = slots[base]
            for k in range(1, place.tasks // 2):
                total = total + slots[base + k]
        out[...] = total

    def plan(self, plan, needs, out):
        plan.event("m0", 0.1, [(name, 0.0) for name in needs], functools.partial(self.hop, 0))
        plan.event("m1", 0.1, [("m0", 2.0)], functools.partial(self.hop, 1))
        plan.event("m2", 0.1, [("m1", 3.0)], functools.partial(self.hop, 2))
        plan.event("m3", 0.1, [("m2", 3.0)], self.along_z)
        plan.event("m4", 0.1, [("m3", 4.0)], functools.partial(self.end, out))


HOP = {"z": 8.0, "period": 9.5, "a": 9.0, "c": 10.0, "core": 3.0, "turn": 9.8, "D": 4.0, "C": 8.0, "A": 8.0, "Z": 12.0}
AHEAD = 2


def layer_kernel(tasks, shards, *refs):
    tgt_len, src_len, counts, x_hbm, enc_hbm, cot_hbm, small_ref = refs[:7]
    mats = refs[7:17]
    layer_out, grad_in, grad_enc, *outs, from_task, small_out = refs[17:25]
    (w, wo, pi, po, act, hidden, after_self, after_cross, upstream, dn, x, enc, small, dsmall, strip, line, key_mask,
     share, *slots_refs) = refs[25:]
    from_core, from_third, from_second, from_z, fin, tasks_here, small_slots = slots_refs[:7]
    credits, local_sem, in_sem, out_sem, send_sem, recv_sem = slots_refs[7:11], *slots_refs[11:]
    place = Place(tasks, shards)
    layer = Layer(
        tgt_len=tgt_len, src_len=src_len, x=x, enc=enc, w=w, wo=wo, pi=pi, po=po, act=act,
        after_self=after_self, after_cross=after_cross, upstream=upstream, dn=dn, small=small, dsmall=dsmall, strip=strip, line=line,
        key_mask=key_mask, share=share, places=shards,
    )
    sends = Sends(send_sem, recv_sem)
    gather = Gather(place, layer, mats, small_ref, local_sem, sends)
    gather.local()
    loads = []
    for number, (src, dst) in enumerate([(x_hbm, x), (cot_hbm, act.at[G3]), (enc_hbm, enc)]):
        loads.append(pltpu.make_async_copy(src, dst, in_sem.at[number]))
        loads[-1].start()
    total = counts[0]
    for task in range(1, tasks):
        total = total + counts[task]
    share[0] = counts[place.t].astype(F32) / total.astype(F32)
    place.greet(True)
    scatter = Scatter(
        place, layer, (from_core, from_third, from_second, from_z), outs, fin, from_task, tasks_here, credits,
        local_sem.at[pl.ds(9, WINDOW)], local_sem.at[9 + WINDOW], sends,
    )
    tail = SmallSums(place, layer, small_slots, sends)
    plan = Plan()
    gather.plan(plan)
    stores = {}

    def store(number, slot, out):
        stores[number] = lambda: pltpu.make_async_copy(act.at[slot], out, out_sem.at[number])
        stores[number]().start()

    part = functools.partial

    def attend(cross, third):
        @pl.loop(0, H // 6)
        def _(hp):
            layer.attend(hp + third * (H // 6), cross)

    none = lax.div(place.t, tasks)

    def attend_back(cross, hp):
        @pl.loop(hp + none, hp + 1)
        def _(here):
            layer.attend_back(here, cross)

    def project_self(first, last):
        @pl.loop(first, last)
        def _(u):
            act[QS + u] = dot(act[NS], layer.unit(u)).astype(BF)

    def source(u):
        act[KC + u] = dot(enc[...], layer.unit(5 + u)).astype(BF)

    piece = plan.piece

    def begin():
        loads[1].wait()
        layer.masks()
        small[...] = jnp.zeros_like(small)
        layer.live_cot()
        loads[0].wait()
        loads[2].wait()

    piece("begin", 0.8, ["zs"], begin)
    piece("strip", 1.5, ["small", "begin"], lambda: [layer.sum_small(), layer.bias_strip(), layer.norm_self()])
    piece("qk", 1.6, ["strip", "w0"], part(project_self, 0, 2))
    piece("v", 0.8, ["strip", "w1"], part(project_self, 2, 3))
    for k in range(3):
        piece(f"self{k}", 2.6, [f"self{k - 1}"] if k else ["qk", "v"], part(attend, False, k))
    piece("close_self", 1.5, ["self2"], layer.close_self)
    piece("kc", 0.8, ["w2", "begin"], part(source, 0))
    piece("qc", 0.8, ["close_self", "w2"], layer.project_query)
    piece("vc", 0.8, ["w3", "begin"], part(source, 1))
    for k in range(3):
        piece(f"cross{k}", 3.0, [f"cross{k - 1}"] if k else ["qc", "kc", "vc"], part(attend, True, k))
    piece("close_cross", 0.7, ["cross2", "w3"], layer.close_cross)

    for c in range(4):
        piece(f"sent{c}", 0.1, [f"w{UNITS - 1}", "close_cross"] if c == 0 else [f"sent{c - 1}"], part(gather.sent, c))

    layer.hidden = hidden

    def ffn(slope):
        layer.slope = slope
        for j in range(4):
            piece(f"h{j}", 1.4, ["close_cross", f"w{4 + j // 2}"], part(layer.ffn_hidden, j))
        for j in range(4):
            piece(f"go{j}", 0.8, [f"h{j}"], part(layer.grad_ffn_out, j))
        for j in range(4):
            piece(f"fb{j}", 1.6, [f"h{k}" for k in range(4)] + ["w6", "w7"], part(layer.ffn_back, j))
        for j in range(4):
            piece(f"gi{j}", 0.9, [f"fb{j}"], part(layer.grad_unit, 8 + j, act.at[NF], slope.at[j]))
        plan.run_until([f"gi{j}" for j in range(4)] + [f"fb{j}" for j in range(4)])

    def back(dstrip, lines):
        layer.dstrip, layer.lines = dstrip, lines
        piece("fnb", 2.0, [], layer.ffn_norm_back)
        piece("dmc", 0.8, ["fnb", "sent3"], part(layer.mix_back, 7))
        piece("g7", 0.8, ["fnb", "sent3"], part(layer.grad_unit, 7, act.at[MC], act.at[G3]))
        for k in range(H // 2):
            piece(f"bc{k}", 2.3, [f"bc{k - 1}"] if k else ["dmc"], part(attend_back, True, k))
        for n, src, grad in ((6, enc, DV), (5, enc, DK), (4, act.at[NC], DQ)):
            piece(f"g{n}", 0.8, ["bc5", "sent3"], part(layer.grad_unit, n, src, act.at[grad]))
        piece("qb", 0.8, ["bc5"], layer.query_back)
        piece("cnb", 2.0, ["qb"], layer.cross_norm_back)
        piece("dms", 1.2, ["cnb", "g7"], lambda: [layer.mix_back(3), layer.clear_strip()])
        piece("g3", 0.8, ["dms"], part(layer.grad_unit, 3, act.at[MS], act.at[G3]))
        for k in range(H // 2):
            needs = [f"bs{k - 1}"] if k else ["dms", "g4", "g5", "g6"]
            piece(f"bs{k}", 1.9, needs, part(attend_back, False, k))
        for k in range(3):
            piece(f"sb{k}", 0.9, [f"sb{k - 1}"] if k else ["bs5"], part(layer.self_back, k))
        for k in (2, 1, 0):
            piece(f"g{k}", 0.8, ["sb2"], part(layer.grad_unit, k, act.at[NS], act.at[QC + k]))
        piece("bias", 2.4, ["bs5"], layer.bias_grad)
        piece("snb", 2.0, ["sb2"], lambda: [layer.self_norm_back(), store(1, NC, grad_in)])
        piece("eb0", 0.8, ["bs5"], part(layer.source_back, 0))
        piece("eb1", 0.8, ["eb0"], lambda: [layer.source_back(1), store(2, MC, grad_enc)])
        for j in range(4):
            piece(f"out{j}", 0.9, ["bs5"], part(layer.ffn_out, j))
        piece("out", 0.6, [f"out{j}" for j in range(4)], lambda: [layer.ffn_result(), store(0, DQ, layer_out)])
        plan.run_until(None)

    order = (6, 7, 4, 5, 3, 2, 1, 0)
    needs = {c: [f"g{2 * c}", f"g{2 * c + 1}"] for c in range(4)}
    needs.update({4: ["gi0", "gi1"], 5: ["gi2", "gi3"]})
    needs.update({c: [f"go{j}" for j in range(4)] + [f"w{UNITS - 1}"] for c in (6, 7)})
    scatter.plan(plan, order, needs)
    tail.plan(plan, ["snb", "bias", "cnb", "fnb"], small_out)
    pl.run_scoped(ffn, pltpu.VMEM((4, ROWS, D), BF))
    pl.run_scoped(
        back, pltpu.VMEM((H, BLOCK, ROWS), F32), pltpu.VMEM((H, 8, ROWS + BLOCK), F32)
    )
    scatter.finish()
    for number in range(3):
        stores[number]().wait()
    sends.finish()


def run_layer(arrays, mats, small, counts, tasks, shards):
    zs, pairs, rows = shards // COLS, tasks // 2, mats[0].shape[0]
    shape = jax.ShapeDtypeStruct
    vmem = pltpu.VMEM
    unit = (zs, COLS, rows, D)
    full = shape((ROWS, D), BF)
    out_shape = (
        full, full, full,
        shape((8, rows, D), F32), shape((rows, 4 * D), F32), shape((4, rows, D), F32),
        shape((UNITS, pairs, rows, D) if tasks > 2 else (8, 128), F32), shape((SMALL, D), F32),
    )
    scratch = [
        vmem((12,) + unit, BF),
        vmem((zs, COLS, 4, rows, D), BF),
        vmem((4,) + unit, BF),
        vmem((zs, COLS, 4, rows, D), BF),
        vmem((15, ROWS, D), BF),
        vmem((4, ROWS, D), BF),
        vmem((ROWS, D), F32),
        vmem((ROWS, D), F32),
        vmem((ROWS, D), F32),
        vmem((ROWS, D), F32),
        vmem((ROWS, D), BF),
        vmem((ROWS, D), BF),
        vmem((SMALL, D), F32),
        vmem((SMALL, D), F32),
        vmem((H, BLOCK, ROWS), BF),
        vmem((SMALL, D), F32),
        vmem((SMALL, ROWS), F32),
        pltpu.SMEM((1,), F32),
        vmem((WINDOW,) + unit, BF),
        vmem((WINDOW, 2, zs, rows, D), BF),
        vmem((WINDOW, zs, rows, D), BF),
        vmem((WINDOW, zs - 1, rows, D), BF),
        vmem((WINDOW, rows, D), F32),
        vmem((pairs, rows, D) if tasks > 2 else (8, 128), F32),
        vmem((6 + zs + pairs, SMALL, D), F32),
        pltpu.SemaphoreType.REGULAR,
        pltpu.SemaphoreType.REGULAR,
        pltpu.SemaphoreType.REGULAR,
        pltpu.SemaphoreType.REGULAR((zs - 1,)),
    ]
    number = UNITS * (zs - 1 + 7) + (zs - 1) + 3 + UNITS * (5 + zs - 1 + pairs - 1) + 3 + zs - 1 + pairs - 1
    scratch += [
        pltpu.SemaphoreType.DMA((10 + WINDOW,)),
        pltpu.SemaphoreType.DMA((3,)),
        pltpu.SemaphoreType.DMA((3,)),
        pltpu.SemaphoreType.DMA((number,)),
        pltpu.SemaphoreType.DMA((number,)),
    ]
    anywhere = pl.BlockSpec(memory_space=pl.ANY)
    return pl.pallas_call(
        functools.partial(layer_kernel, tasks, shards),
        out_shape=out_shape,
        in_specs=[pl.BlockSpec(memory_space=pltpu.SMEM)] * 3 + [anywhere] * 14,
        out_specs=[anywhere] * 7 + [pl.BlockSpec(memory_space=pltpu.VMEM)],
        scratch_shapes=scratch,
        compiler_params=pltpu.CompilerParams(
            collective_id=1, has_side_effects=True, vmem_limit_bytes=63 * 2**20
        ),
        cost_estimate=pl.CostEstimate(flops=35_000_000_000, bytes_accessed=60_000_000, transcendentals=10_000_000),
        name="layer",
    )(*counts, *arrays, small, *mats)


def on_device(
    inputs, encoded, cotangent, tgt_len, src_len, task_counts,
    gain_self, query_self, key_self, value_self, out_self, bias_table,
    gain_cross, query_cross, key_cross, value_cross, out_cross, gain_ffn, ffn_in, ffn_out,
):
    tasks, rows = task_counts.shape[0], gain_self.shape[0]
    shards, buckets = D // rows, bias_table.shape[0]
    at = lax.axis_index("shard")
    small = jnp.zeros((SMALL, D), BF)
    gains = jnp.stack([gain_self, gain_cross, gain_ffn])
    small = lax.dynamic_update_slice(small, gains, (0, at * rows))
    small = lax.dynamic_update_slice(small, bias_table.T, (3, at * buckets))
    mats = (
        query_self, key_self, value_self, out_self, query_cross, key_cross, value_cross, out_cross, ffn_in, ffn_out,
    )
    arrays = (inputs.reshape(ROWS, D), encoded.reshape(ROWS, D), cotangent.reshape(ROWS, D))
    layer_out, grad_in, grad_enc, units, g_in, g_out, _, sums = run_layer(
        arrays, mats, small, (tgt_len, src_len, task_counts), tasks, shards
    )
    g_gain = lax.dynamic_slice(sums, (0, at * rows), (3, rows))
    g_table = lax.dynamic_slice(sums, (3, at * buckets), (H, buckets)).T
    return (
        layer_out.reshape(inputs.shape), grad_in.reshape(inputs.shape), grad_enc.reshape(inputs.shape),
        g_gain[0], units[0], units[1], units[2], units[3], g_table,
        g_gain[1], units[4], units[5], units[6], units[7],
        g_gain[2], g_in, g_out.reshape(4 * rows, D),
    )


def solution(mesh):
    placed = (
        P(("task", "shard"), None, None),
        P(("task", "shard"), None, None),
        P(("task", "shard"), None, None),
        P(("task", "shard")),
        P(("task", "shard")),
        P(),
        P("shard"),
        P("shard", None),
        P("shard", None),
        P("shard", None),
        P("shard", None),
        P("shard", None),
        P("shard"),
        P("shard", None),
        P("shard", None),
        P("shard", None),
        P("shard", None),
        P("shard"),
        P("shard", None),
        P("shard", None),
    )
    return jax.shard_map(
        on_device,
        mesh=mesh,
        in_specs=placed,
        out_specs=(
            P(("task", "shard"), None, None),
            P(("task", "shard"), None, None),
            P(("task", "shard"), None, None),
            P("shard"),
            P("shard", None),
            P("shard", None),
            P("shard", None),
            P("shard", None),
            P("shard", None),
            P("shard"),
            P("shard", None),
            P("shard", None),
            P("shard", None),
            P("shard", None),
            P("shard"),
            P("shard", None),
            P("shard", None),
        ),
        check_vma=False,
    )
```

```python
import functools
import math

import jax
import jax.numpy as jnp
import numpy as np
from jax import lax
from jax.experimental import pallas as pl
from jax.experimental.pallas import tpu as pltpu
from jax.sharding import PartitionSpec as P

H = 12
DH = 64
NB = 32
D = 768
EPSILON = 1e-06
MASKED = -1000000000.0
LIMITS = np.array(
    list(range(1, 16))
    + [math.ceil(16.0 * 8.0 ** ((bucket - 16) / 16.0)) for bucket in range(16, 32)],
    dtype=np.int32,
)
MESH = pl.DeviceIdType.MESH
BF = jnp.bfloat16
F32 = jnp.float32
COLS = 4
SMALL = 16


class Place:
    def __init__(self, tasks, shards):
        self.tasks, self.zs = tasks, shards // COLS
        self.t, self.s = lax.axis_index("task"), lax.axis_index("shard")
        self.half = lax.rem(self.t, 2)
        self.other = 1 - self.half
        self.z, self.q = lax.div(self.s, COLS), lax.rem(self.s, COLS)
        flip_x = self.q + 1 - 2 * lax.rem(self.q, 2)
        flip_y = lax.rem(self.q + 2, COLS)
        self.qx, self.qy = flip_x, flip_y
        self.q2 = flip_x + self.half * (flip_y - flip_x)
        self.q3 = flip_y + self.half * (flip_x - flip_y)
        self.q4 = COLS - 1 - self.q
        self.core = (self.t + 1 - 2 * self.half, self.s)
        self.second = (self.t, self.z * COLS + self.q2)
        self.third = (self.t, self.z * COLS + self.q3)

    def along_z(self, step):
        z = lax.rem(self.z + step, self.zs)
        return z, (self.t, z * COLS + self.q)

    def along_task(self, step):
        return (lax.rem(self.t + 2 * step, self.tasks), self.s)

    def greet(self, task_peers):
        peers = [self.core, self.second, self.third]
        peers += [self.along_z(k)[1] for k in range(1, self.zs)]
        if task_peers:
            peers += [self.along_task(k) for k in range(1, self.tasks // 2)]
        barrier = pltpu.get_barrier_semaphore()
        for peer in peers:
            pl.semaphore_signal(barrier, inc=1, device_id=peer, device_id_type=MESH)
        pl.semaphore_wait(barrier, len(peers))


class Sends:
    def __init__(self, send_sem, recv_sem):
        self.send_sem, self.recv_sem, self.made, self.done = send_sem, recv_sem, {}, set()

    def copy(self, key):
        number, describe = self.made[key]
        src, dst, device = describe()
        return pltpu.make_async_remote_copy(
            src_ref=src,
            dst_ref=dst,
            send_sem=self.send_sem.at[number],
            recv_sem=self.recv_sem.at[number],
            device_id=device,
            device_id_type=MESH,
        )

    def start(self, key, describe):
        self.made[key] = (len(self.made), describe)
        self.copy(key).start()

    def arrived(self, key):
        self.copy(key).wait_recv()

    def sent(self, key):
        self.copy(key).wait_send()
        self.done.add(key)

    def finish(self):
        for key in [key for key in self.made if key not in self.done]:
            self.sent(key)


NS, QS, KS, VS, MS, NC, QC, KC, VC, MC, NF, G3, DQ, DK, DV = range(15)
DM = NF
ROWS = 512
BLOCK = 128
BLOCKS = ROWS // BLOCK
TALL = 256


def halves(body):
    @pl.loop(0, 2)
    def _(i):
        body(pl.ds(pl.multiple_of(i * (ROWS // 2), ROWS // 2), ROWS // 2))


def dot(a, b):
    return jnp.dot(a, b, preferred_element_type=F32)


def dot_t(a, b):
    return lax.dot_general(a, b, (((1,), (1,)), ((), ())), preferred_element_type=F32)


def t_dot(a, b):
    return lax.dot_general(a, b, (((0,), (0,)), ((), ())), preferred_element_type=F32)


def normed(v):
    inverse = lax.rsqrt(jnp.mean(v * v, axis=-1, keepdims=True) + EPSILON)
    return v * inverse, inverse


def smooth_parts(v):
    c = math.sqrt(2.0 / math.pi)
    square = v * v
    tanh = jnp.tanh(v * (c + (c * 0.044715) * square))
    left = 0.5 * (1.0 + tanh)
    slope = left + 0.5 * v * (1.0 - tanh * tanh) * (c + (3.0 * c * 0.044715) * square)
    return v * left, slope


class Layer:
    def __init__(
        self, tgt_len, src_len, x, enc, w, wo, pi, po, act, after_self, after_cross, upstream, dn, small, dsmall, strip, line,
        key_mask, share, places,
    ):
        self.tgt_len = tgt_len
        self.src_len = src_len
        self.x = x
        self.enc = enc
        self.w = w
        self.wo = wo
        self.pi = pi
        self.po = po
        self.act = act
        self.after_self = after_self
        self.after_cross = after_cross
        self.upstream = upstream
        self.dn = dn
        self.small = small
        self.dsmall = dsmall
        self.strip = strip
        self.line = line
        self.key_mask = key_mask
        self.share = share
        self.places = places

    def unit(self, n):
        return self.w[n].reshape(D, D)

    def live(self, start, size):
        rows = start + lax.broadcasted_iota(jnp.int32, (size, 1), 0)
        return rows < self.tgt_len[0]

    def gain(self, row):
        return self.small[pl.ds(row, 1), :]


    def sum_small(self):
        @pl.loop(0, self.places)
        def _(n):
            more = self.act[DV, pl.ds(pl.multiple_of(n * SMALL, SMALL), SMALL), :].astype(F32)
            self.add_rows(self.small, slice(0, SMALL), more, True)

    def masks(self):
        cols = lax.broadcasted_iota(jnp.int32, (8, ROWS), 1)
        self.key_mask[0:8, :] = jnp.where(cols < self.tgt_len[0], 0.0, MASKED)
        self.key_mask[8:16, :] = jnp.where(cols < self.src_len[0], 0.0, MASKED)

    def bucket_of(self, distance):
        bucket = jnp.zeros(distance.shape, jnp.int32)
        for limit in LIMITS:
            bucket = bucket + (distance >= int(limit)).astype(jnp.int32)
        return bucket

    def bias_strip(self):
        wide = 768
        lane = lax.broadcasted_iota(jnp.int32, (NB, wide), 1)
        bucket = self.bucket_of(jnp.maximum(511 - lane, 0))
        onehot = (bucket == lax.broadcasted_iota(jnp.int32, (NB, wide), 0)).astype(F32)
        table = self.small[:, 0:NB]
        line = jnp.dot(table, onehot, precision=lax.Precision.HIGHEST, preferred_element_type=F32)
        line = jnp.where(lax.broadcasted_iota(jnp.int32, (SMALL, wide), 1) <= 511, line, MASKED)
        self.line[...] = line

        @pl.loop(0, H)
        def _(h):
            row = jnp.broadcast_to(self.line[pl.ds(h + 3, 1), :], (BLOCK, wide))
            rolled = pltpu.roll(row, wide - 127, 1, stride=1, stride_axis=0)
            self.strip[h] = rolled[:, 0:ROWS].astype(BF)

    def clear_strip(self):
        self.dstrip[...] = jnp.zeros_like(self.dstrip)

    def bias_grad(self):
        wide = ROWS + BLOCK

        @pl.loop(0, H)
        def _(h):
            total = None
            for r in range(BLOCK // 8):
                rows = jnp.concatenate(
                    [self.dstrip[h, 8 * r : 8 * r + 8, :], jnp.zeros((8, BLOCK), F32)], axis=1
                )
                if r:
                    rows = pltpu.roll(rows, wide - 8 * r, 1)
                total = rows if total is None else total + rows
            self.lines[h] = total

        grad = jnp.zeros((H, NB), F32)
        lane = lax.broadcasted_iota(jnp.int32, (NB, wide), 1)
        for s in range(8):
            distance = ROWS - BLOCK + s - lane + jnp.where(lane >= ROWS, wide, 0)
            bucket = self.bucket_of(jnp.maximum(distance, 0))
            fits = bucket == lax.broadcasted_iota(jnp.int32, (NB, wide), 0)
            grad = grad + lax.dot_general(
                self.lines[:, s, :], fits.astype(F32), (((1,), (1,)), ((), ())),
                precision=lax.Precision.HIGHEST, preferred_element_type=F32,
            )
        self.dsmall[3 : 3 + H, 0:NB] = grad


    def norm_self(self):
        @pl.loop(0, BLOCKS)
        def _(i):
            rows = pl.ds(pl.multiple_of(i * BLOCK, BLOCK), BLOCK)
            n, _ = normed(self.x[rows, :].astype(F32))
            self.act[NS, rows, :] = (n * self.gain(0)).astype(BF)

    def pair(self, value, h):
        lane = lax.broadcasted_iota(jnp.int32, value.shape, 1)
        return jnp.where((lane < 64) == (h == 0), value, jnp.zeros_like(value))

    def probs(self, q, k, head, first, keys, cross):
        s = dot_t(q, k)
        if cross:
            s = s + self.key_mask[8:9, 0:keys]
        else:
            parts = []
            for here in range(first, keys, BLOCK):
                strip = self.strip[head, :, ROWS - here - BLOCK :].astype(F32)
                if here + BLOCK < keys:
                    beyond = jnp.full((BLOCK, keys - here - BLOCK), MASKED, F32)
                    strip = jnp.concatenate([strip, beyond], axis=1)
                parts.append(strip)
            s = s + (jnp.concatenate(parts, axis=0) + self.key_mask[0:1, 0:keys])
        p = jnp.exp(s - jnp.max(s, axis=-1, keepdims=True))
        return p * (1.0 / jnp.sum(p, axis=-1, keepdims=True))

    def attend(self, hp, cross):
        base = NC if cross else NS
        cols = pl.ds(pl.multiple_of(hp * 128, 128), 128)
        k, v = self.act[base + 2, :, cols], self.act[base + 3, :, cols]
        for first in range(0, ROWS, TALL):
            rows = slice(first, first + TALL)
            keys = ROWS if cross else first + TALL
            q = self.act[base + 1, rows, cols]
            total = None
            for h in range(2):
                p = self.probs(self.pair(q, h), k[:keys], 2 * hp + h, first, keys, cross).astype(BF)
                term = dot(p, self.pair(v[:keys], h))
                total = term if total is None else total + term
            self.act[base + 4, rows, cols] = total.astype(BF)

    def close_self(self):
        self.dn[...] = dot(self.act[MS], self.unit(3))

        @pl.loop(0, BLOCKS)
        def _(i):
            rows = pl.ds(pl.multiple_of(i * BLOCK, BLOCK), BLOCK)
            after = self.x[rows, :].astype(F32) + self.dn[rows, :]
            self.after_self[rows, :] = after
            n, _ = normed(after)
            self.act[NC, rows, :] = (n * self.gain(1)).astype(BF)

    def project_query(self):
        self.act[QC] = dot(self.act[NC], self.unit(4)).astype(BF)

    def close_cross(self):
        self.dn[...] = dot(self.act[MC], self.unit(7))

        @pl.loop(0, BLOCKS)
        def _(i):
            rows = pl.ds(pl.multiple_of(i * BLOCK, BLOCK), BLOCK)
            after = self.after_self[rows, :] + self.dn[rows, :]
            self.after_cross[rows, :] = after
            n, _ = normed(after)
            self.act[NF, rows, :] = (n * self.gain(2)).astype(BF)

    def live_cot(self):
        @pl.loop(0, BLOCKS)
        def _(i):
            start = pl.multiple_of(i * BLOCK, BLOCK)
            rows = pl.ds(start, BLOCK)
            cot = self.act[G3, rows, :]
            self.act[G3, rows, :] = jnp.where(self.live(start, BLOCK), cot, jnp.zeros_like(cot))

    def ffn_hidden(self, j):
        self.dn[...] = dot(self.act[NF], self.unit(8 + j))

        @pl.loop(0, BLOCKS)
        def _(i):
            rows = pl.ds(pl.multiple_of(i * BLOCK, BLOCK), BLOCK)
            act, slope = smooth_parts(self.dn[rows, :])
            self.hidden[j, rows, :] = act.astype(BF)
            self.slope[j, rows, :] = slope.astype(BF)

    def outer(self, a, b, store):
        @pl.loop(0, 2)
        def _(m):
            cols = pl.ds(pl.multiple_of(m * 384, 128), 384)
            store(m, (t_dot(a[:, cols], b[...]) * self.share[0]).astype(BF))

    def grad_unit(self, n, a, b):
        half, rows = self.w.shape[1] // 2, self.w.shape[3]
        place = self.w if n < 8 else self.pi
        number = {0: n, 1: n + 4, 2: n - 8}[n // 4]

        def store(m, value):
            place[number, pl.ds(m * half, half)] = value.reshape(half, COLS, rows, D)

        self.outer(a, b, store)

    def grad_ffn_out(self, j):
        some, rows = self.wo.shape[0] // 4, self.wo.shape[3]

        def store(m, value):
            if some == 1:
                self.po[j, pl.ds(2 * m, 2)] = value.reshape(2, 4, rows, D)
            else:
                self.po[pl.ds(j * some + m * (some // 2), some // 2)] = value.reshape(some // 2, COLS, 4, rows, D)

        self.outer(self.hidden.at[j], self.act.at[G3], store)

    def ffn_out(self, j):
        @halves
        def _(rows):
            self.after_cross[rows, :] += dot(self.hidden[j, rows, :], self.wo_rows(j))

    def ffn_result(self):
        @pl.loop(0, BLOCKS)
        def _(i):
            start = pl.multiple_of(i * BLOCK, BLOCK)
            rows = pl.ds(start, BLOCK)
            self.act[DQ, rows, :] = jnp.where(self.live(start, BLOCK), self.after_cross[rows, :], 0.0).astype(BF)

    def wo_rows(self, j):
        eighth = self.wo.shape[0] // 4
        return self.wo[pl.ds(j * eighth, eighth)].reshape(D, D)


    def ffn_back(self, j):
        @halves
        def _(rows):
            grad = dot_t(self.act[G3, rows, :], self.wo_rows(j)) * self.slope[j, rows, :].astype(F32)
            self.slope[j, rows, :] = grad.astype(BF)
        @halves
        def _(rows):
            self.add_rows(self.dn, rows, dot_t(self.slope[j, rows, :], self.unit(8 + j)), j)

    def add_rows(self, ref, rows, value, more):
        if more:
            ref[rows, :] += value
        else:
            ref[rows, :] = value

    def norm_back(self, values, gain_row, upstream, dst, branch):
        self.dsmall[gain_row : gain_row + 1, :] = jnp.zeros((1, D), F32)

        @pl.loop(0, BLOCKS)
        def _(i):
            rows = pl.ds(pl.multiple_of(i * BLOCK, BLOCK), BLOCK)
            n, inverse = normed(values(rows))
            dn = self.dn[rows, :]
            self.dsmall[gain_row : gain_row + 1, :] += jnp.sum(dn * n, axis=0, keepdims=True)
            scaled = dn * self.gain(gain_row)
            back = inverse * (scaled - n * jnp.mean(scaled * n, axis=-1, keepdims=True))
            total = upstream(rows) + back
            if dst is not None:
                dst[rows, :] = total
            branch[rows, :] = total.astype(BF)

    def ffn_norm_back(self):
        self.norm_back(
            lambda rows: self.after_cross[rows, :], 2,
            lambda rows: self.act[G3, rows, :].astype(F32), self.upstream, self.act.at[G3],
        )

    def mix_back(self, unit):
        self.act[DM] = dot_t(self.act[G3], self.unit(unit)).astype(BF)

    def attend_back(self, hp, cross):
        base, to = (NC, DQ) if cross else (NS, QC)
        cols = pl.ds(pl.multiple_of(hp * 128, 128), 128)
        k, v = self.act[base + 2, :, cols], self.act[base + 3, :, cols]
        own = [self.pair(k, h) for h in range(2)]
        for first in reversed(range(0, ROWS, TALL)):
            rows = slice(first, first + TALL)
            keys = ROWS if cross else first + TALL
            q, dm = self.act[base + 1, rows, cols], self.act[DM, rows, cols]
            prod = dm.astype(F32) * self.act[base + 4, rows, cols].astype(F32)
            dq = dk = dv = None
            for h in range(2):
                qh, dmh = self.pair(q, h), self.pair(dm, h)
                p = self.probs(qh, k[:keys], 2 * hp + h, first, keys, cross)
                dp = dot_t(dmh, v[:keys])
                delta = jnp.sum(self.pair(prod, h), axis=-1, keepdims=True)
                ds = p * (dp - delta)
                if not cross:
                    for here in range(first, keys, BLOCK):
                        upto = here + BLOCK
                        self.dstrip[2 * hp + h, :, ROWS - upto :] += ds[here - first : upto - first, :upto]
                ds = ds.astype(BF)
                terms = (dot(ds, own[h][:keys]), t_dot(ds, qh), t_dot(p.astype(BF), dmh))
                dq, dk, dv = terms if dq is None else (dq + terms[0], dk + terms[1], dv + terms[2])
            self.act[to, rows, cols] = dq.astype(BF)
            self.add_rows(self.dn.at[:, 0:128], slice(0, keys), dk, first + TALL < ROWS)
            self.add_rows(self.dn.at[:, 128:256], slice(0, keys), dv, first + TALL < ROWS)
        self.act[to + 1, :, cols] = self.dn[:, 0:128].astype(BF)
        self.act[to + 2, :, cols] = self.dn[:, 128:256].astype(BF)

    def source_back(self, k):
        @halves
        def _(rows):
            back = dot_t(self.act[DK + k, rows, :], self.unit(5 + k))
            if k:
                self.act[MC, rows, :] = (self.after_self[rows, :] + back).astype(BF)
            else:
                self.after_self[rows, :] = back

    def query_back(self):
        self.dn[...] = dot_t(self.act[DQ], self.unit(4))

    def cross_norm_back(self):
        self.norm_back(
            lambda rows: self.after_self[rows, :], 1,
            lambda rows: self.upstream[rows, :], self.upstream, self.act.at[G3],
        )

    def self_back(self, k):
        @halves
        def _(rows):
            self.add_rows(self.dn, rows, dot_t(self.act[QC + k, rows, :], self.unit(k)), k)

    def self_norm_back(self):
        self.norm_back(
            lambda rows: self.x[rows, :].astype(F32), 0,
            lambda rows: self.upstream[rows, :], None, self.act.at[NC],
        )


UNITS = 8
WINDOW = 2


class Plan:
    def __init__(self):
        self.work, self.events, self.at, self.log = [], [], {}, []
        self.now = 0.0

    def piece(self, name, cost, needs, run):
        self.work.append((name, cost, needs, run))

    def event(self, name, cost, needs, run):
        self.events.append((name, cost, needs, run))

    def due(self, needs):
        if any(name not in self.at for name, _ in needs):
            return None
        return max([self.at[name] + wait for name, wait in needs], default=0.0)

    def take(self, where, item, start):
        name, cost, _, run = item
        where.remove(item)
        self.now = max(self.now, start) + cost
        run()
        self.at[name] = self.now
        self.log.append((round(self.now, 1), name))

    def run_until(self, name):
        while (self.work or self.events) if name is None else any(each not in self.at for each in name):
            dues = [(self.due(item[2]), number) for number, item in enumerate(self.events)]
            dues = [pair for pair in dues if pair[0] is not None]
            first = min(dues, default=None)
            if first is not None and first[0] <= self.now:
                self.take(self.events, self.events[first[1]], first[0])
                continue
            ready = [item for item in self.work if all(name in self.at for name in item[2])]
            if ready:
                self.take(self.work, ready[0], self.now)
            else:
                self.take(self.events, self.events[first[1]], first[0])


class Gather:
    def __init__(self, place, layer, mats, small_ref, local_sem, sends):
        self.place, self.layer, self.mats, self.small_ref = place, layer, mats, small_ref
        self.local_sem, self.sends = local_sem, sends

    def column(self, c, q):
        if c < 6:
            return self.layer.w.at[2 * c + self.place.half, :, q]
        return self.layer.wo.at[:, q, 2 * (c - 6) + self.place.half]

    def slab(self, c, z, q):
        if c < 6:
            return self.layer.w.at[2 * c + self.place.half, z, q]
        return self.layer.wo.at[z, q, 2 * (c - 6) + self.place.half]

    def both(self, key, here, device):
        self.sends.start(key, lambda: (here(), here(), device()))

    def local(self):
        place, w, wo = self.place, self.layer.w, self.layer.wo
        z, q = place.z, place.q
        rows = w.shape[3]
        self.copies = []
        for n in range(16):
            if n < 8:
                src, dst = self.mats[n], w.at[n, z, q]
            elif n < 12:
                src, dst = self.mats[8].at[:, pl.ds(D * (n - 8), D)], w.at[n, z, q]
            else:
                src, dst = self.mats[9].at[pl.ds(rows * (n - 12), rows)], wo.at[z, q, n - 12]
            self.copies.append(pltpu.make_async_copy(src, dst, self.local_sem.at[n // 2]))
        for n in range(16):
            @pl.when(place.half == n % 2)
            def _():
                self.copies[n].start()
        self.small_copy = pltpu.make_async_copy(self.small_ref, self.small_at(z, q), self.local_sem.at[8])
        self.small_copy.start()

    def small_at(self, z, q):
        row = (q * self.place.zs + z) * SMALL
        return self.layer.act.at[DV, pl.ds(pl.multiple_of(row, SMALL), SMALL)]

    def small_column(self, q):
        size = self.place.zs * SMALL
        return self.layer.act.at[DV, pl.ds(pl.multiple_of(q * size, SMALL), size)]

    def start_small(self):
        self.small_copy.wait()
        place = self.place
        for k in range(1, place.zs):
            self.both(("zs", k), lambda: self.small_at(place.z, place.q), lambda k=k: place.along_z(k)[1])

    def small_second(self):
        place = self.place
        for k in range(1, place.zs):
            self.sends.arrived(("zs", k))
        self.both("as", lambda: self.small_column(place.q), lambda: place.second)
        self.both("bs", lambda: self.small_column(place.q), lambda: place.third)

    def small_third(self):
        place = self.place
        self.sends.arrived("as")
        self.both("cs", lambda: self.small_column(place.q2), lambda: place.third)

    def small_ready(self):
        self.sends.arrived("bs")
        self.sends.arrived("cs")

    def start_z(self, c):
        place = self.place
        self.copies[2 * c].wait()
        for k in range(1, place.zs):
            self.both(("z", c, k), lambda: self.slab(c, place.z, place.q), lambda k=k: place.along_z(k)[1])

    def send_column(self, name, c, q, device):
        self.both((name, c), lambda: self.column(c, q), lambda: device)

    def from_z(self, c):
        place = self.place
        for k in range(1, place.zs):
            self.sends.arrived(("z", c, k))
        self.send_column("a", c, place.q, place.second)
        self.send_column("b", c, place.q, place.third)
        self.send_column("d1", c, place.q, place.core)

    def from_second(self, c):
        place = self.place
        self.sends.arrived(("a", c))
        self.send_column("c", c, place.q2, place.third)
        self.send_column("d2", c, place.q2, place.core)

    def from_third(self, c):
        place = self.place
        self.sends.arrived(("b", c))
        self.send_column("d3", c, place.q3, place.core)
        self.sends.arrived(("c", c))
        self.send_column("d4", c, place.q4, place.core)

    def sent(self, part):
        for c in range(2 * part, 2 * part + 2):
            for key in [("z", c, k) for k in range(1, self.place.zs)]:
                self.sends.sent(key)
            for name in ("a", "b", "c", "d1", "d2", "d3", "d4"):
                self.sends.sent((name, c))
        if part == 3:
            for key in [("zs", k) for k in range(1, self.place.zs)] + ["as", "bs", "cs"]:
                self.sends.sent(key)

    def ready(self, c):
        for name in ("d1", "d2", "d3", "d4"):
            self.sends.arrived((name, c))

    def plan(self, plan):
        hop = HOP
        plan.event("zs", 0.3, [], self.start_small)
        for c in range(UNITS):
            needs = [("zs", 0.0)] if c < AHEAD else [(f"a{c - AHEAD}", 0.0)]
            plan.event(f"z{c}", 0.2, needs, functools.partial(self.start_z, c))
            needs = [(f"z{c}", hop["z"])] + ([(f"a{c - 1}", hop["period"])] if c else [])
            plan.event(f"a{c}", 0.2, needs, functools.partial(self.from_z, c))
            plan.event(f"b{c}", 0.2, [(f"a{c}", hop["a"])], functools.partial(self.from_second, c))
            plan.event(f"c{c}", 0.2, [(f"b{c}", hop["c"])], functools.partial(self.from_third, c))
            plan.event(f"w{c}", 0.1, [(f"c{c}", hop["core"])], functools.partial(self.ready, c))
        plan.event("as", 0.2, [("zs", 2.5)], self.small_second)
        plan.event("cs", 0.1, [("as", 2.0)], self.small_third)
        plan.event("small", 0.1, [("cs", 2.0)], self.small_ready)


class Scatter:
    def __init__(self, place, layer, slots, outs, fin, from_task, tasks_here, credits, local_sem, task_sem, sends):
        self.place, self.layer, self.outs, self.fin, self.from_task = place, layer, outs, fin, from_task
        self.tasks_here, self.task_sem = tasks_here, task_sem
        self.from_core, self.from_third, self.from_second, self.from_z = slots
        self.core_credit, self.third_credit, self.second_credit, self.z_credit = credits
        self.local_sem, self.sends = local_sem, sends

    def part(self, c, part):
        layer = self.layer
        if c < 2:
            return layer.w.at[2 * c + part]
        if c < 4:
            return layer.w.at[2 * c + part + 4]
        if c < 6:
            return layer.pi.at[2 * c + part - 8]
        return layer.po.at[:, :, 2 * (c - 6) + part]

    def column(self, c, q):
        if c < 6:
            return self.part(c, self.place.half).at[:, q]
        return self.layer.po.at[:, q, 2 * (c - 6) + self.place.half]

    def slab(self, c, z, q):
        if c < 6:
            return self.part(c, self.place.half).at[z, q]
        return self.layer.po.at[z, q, 2 * (c - 6) + self.place.half]

    def add(self, c, q, arrived):
        @pl.loop(0, self.place.zs)
        def _(z):
            here = self.slab(c, z, q)
            here[...] = (here[...].astype(F32) + arrived(z)[...].astype(F32)).astype(BF)

    def credit(self, semaphore, device):
        pl.semaphore_signal(semaphore, inc=1, device_id=device, device_id_type=MESH)

    def to_core(self, r, c):
        place = self.place
        if r >= WINDOW:
            pl.semaphore_wait(self.core_credit, 1)
        self.sends.start(("D", c), lambda: (self.part(c, place.other), self.from_core.at[r % WINDOW], place.core))

    def to_third(self, r, c, last):
        place, slot = self.place, r % WINDOW
        self.sends.arrived(("D", c))
        for q in (place.q4, place.q3):
            self.add(c, q, lambda z, q=q: self.from_core.at[slot, z, q])
        if r >= WINDOW:
            pl.semaphore_wait(self.third_credit, 1)
        self.sends.start(("C", c), lambda: (self.column(c, place.q4), self.from_third.at[slot, 1], place.third))
        self.sends.start(("B", c), lambda: (self.column(c, place.q3), self.from_third.at[slot, 0], place.third))
        for q in (place.q2, place.q):
            self.add(c, q, lambda z, q=q: self.from_core.at[slot, z, q])
        if not last:
            self.credit(self.core_credit, place.core)

    def to_second(self, r, c):
        place, slot = self.place, r % WINDOW
        self.sends.arrived(("C", c))
        self.add(c, place.q2, lambda z: self.from_third.at[slot, 1, z])
        if r >= WINDOW:
            pl.semaphore_wait(self.second_credit, 1)
        self.sends.start(("A", c), lambda: (self.column(c, place.q2), self.from_second.at[slot], place.second))

    def to_z(self, r, c, last):
        place, slot = self.place, r % WINDOW
        self.sends.arrived(("B", c))
        self.sends.arrived(("A", c))

        @pl.loop(0, place.zs)
        def _(z):
            here = self.slab(c, z, place.q)
            total = here[...].astype(F32) + self.from_third[slot, 0, z].astype(F32)
            here[...] = (total + self.from_second[slot, z].astype(F32)).astype(BF)

        if not last:
            self.credit(self.third_credit, place.third)
            self.credit(self.second_credit, place.second)
        for k in range(1, place.zs):
            if r >= WINDOW:
                pl.semaphore_wait(self.z_credit.at[k - 1], 1)

            def describe(k=k):
                to, device = place.along_z(k)
                return self.slab(c, to, place.q), self.from_z.at[slot, k - 1], device

            self.sends.start(("Z", c, k), describe)

    def target(self, c):
        half = self.place.half
        if c < 4:
            return self.outs[0].at[2 * c + half]
        if c < 6:
            return self.outs[1].at[:, pl.ds(pl.multiple_of((2 * c - 8 + half) * D, D), D)]
        return self.outs[2].at[2 * (c - 6) + half]

    def last(self, r, c, last):
        place, slot = self.place, r % WINDOW
        for k in range(1, place.zs):
            self.sends.arrived(("Z", c, k))
        total = self.slab(c, place.z, place.q)[...].astype(F32)
        for k in range(1, place.zs):
            total = total + self.from_z[slot, k - 1].astype(F32)
        if not last:
            for k in range(1, place.zs):
                self.credit(self.z_credit.at[k - 1], place.along_z(place.zs - k)[1])
        if r >= WINDOW:
            before = self.order[r - WINDOW]
            self.store(before).wait()
            self.sends.sent(("F", before))
        self.fin[slot] = total
        if place.tasks > 2:
            self.over_tasks(r, c, slot)
        self.store(c).start()
        self.sends.start(("F", c), lambda: (self.fin.at[slot], self.target(c), place.core))

    def over_tasks(self, r, c, slot):
        place, pairs = self.place, self.place.tasks // 2
        group = lax.div(place.t, 2)

        def local(src, dst):
            copy = pltpu.make_async_copy(src, dst, self.task_sem)
            copy.start()
            copy.wait()

        for k in range(1, pairs):
            self.sends.start(("T", c, k), lambda k=k: (
                self.fin.at[slot], self.from_task.at[r, lax.div(place.t, 2)], place.along_task(k)))
        local(self.fin.at[slot], self.from_task.at[r, group])
        for k in range(1, pairs):
            self.sends.arrived(("T", c, k))
        for k in range(1, pairs):
            self.sends.sent(("T", c, k))
        local(self.from_task.at[r], self.tasks_here)
        total = self.tasks_here[0]
        for k in range(1, pairs):
            total = total + self.tasks_here[k]
        self.fin[slot] = total

    def store(self, c):
        slot = self.order.index(c) % WINDOW
        return pltpu.make_async_copy(self.fin.at[slot], self.target(c), self.local_sem.at[slot])

    def sent(self, c):
        for name in "DCBA":
            self.sends.sent((name, c))
        for k in range(1, self.place.zs):
            self.sends.sent(("Z", c, k))

    def finish(self):
        for c in self.order[-WINDOW:]:
            self.store(c).wait()
        for c in self.order:
            self.sends.arrived(("F", c))

    def plan(self, plan, order, needs):
        self.order, hop = order, HOP
        for r, c in enumerate(order):
            last = r >= len(order) - WINDOW
            first = [(name, 0.0) for name in needs[c]]
            if r >= WINDOW:
                first.append((f"t{order[r - WINDOW]}", 1.0))
            plan.event(f"d{c}", 0.2, first, functools.partial(self.to_core, r, c))
            first = [(f"d{c}", hop["D"])]
            if r:
                first.append((f"t{order[r - 1]}", hop["turn"]))
            if r >= WINDOW:
                first.append((f"y{order[r - WINDOW]}", 1.0))
            plan.event(f"t{c}", 1.4, first, functools.partial(self.to_third, r, c, last))
            first = [(f"t{c}", hop["C"])]
            if r >= WINDOW:
                first.append((f"y{order[r - WINDOW]}", 1.0))
            plan.event(f"s{c}", 0.5, first, functools.partial(self.to_second, r, c))
            first = [(f"s{c}", hop["A"])]
            if r >= WINDOW:
                first.append((f"l{order[r - WINDOW]}", 1.0))
            plan.event(f"y{c}", 0.7, first, functools.partial(self.to_z, r, c, last))
            plan.event(f"l{c}", 0.4, [(f"y{c}", hop["Z"])], functools.partial(self.last, r, c, last))


class SmallSums:
    def __init__(self, place, layer, slots, sends):
        self.place, self.layer, self.slots, self.sends = place, layer, slots, sends

    def device(self, number):
        place = self.place
        return [place.core, (place.t, place.z * COLS + place.qx), (place.t, place.z * COLS + place.qy)][number]

    def hop(self, number):
        place, slots = self.place, self.slots
        if number == 0:
            slots[0] = self.layer.dsmall[...] * self.layer.share[0]
        else:
            self.sends.arrived(("s", number - 1))
            slots[2 * number] = slots[2 * number - 2] + slots[2 * number - 1]
        if number < 3:
            self.sends.start(("s", number), lambda: (slots.at[2 * number], slots.at[2 * number + 1], self.device(number)))

    def along_z(self):
        place, slots = self.place, self.slots
        self.sends.arrived(("s", 2))
        mine = slots.at[6 + place.z]
        mine[...] = slots[4] + slots[5]
        for k in range(1, place.zs):
            self.sends.start(("sz", k), lambda k=k: (slots.at[6 + place.z], slots.at[6 + place.z], place.along_z(k)[1]))

    def end(self, out):
        place, slots = self.place, self.slots
        for k in range(1, place.zs):
            self.sends.arrived(("sz", k))
        total = slots[6]
        for k in range(1, place.zs):
            total = total + slots[6 + k]
        if place.tasks > 2:
            base, group = 6 + place.zs, lax.div(place.t, 2)
            mine = slots.at[base + group]
            mine[...] = total
            for k in range(1, place.tasks // 2):
                self.sends.start(("st", k), lambda k=k: (
                    slots.at[base + lax.div(place.t, 2)], slots.at[base + lax.div(place.t, 2)], place.along_task(k)))
            for k in range(1, place.tasks // 2):
                self.sends.arrived(("st", k))
            total = slots[base]
            for k in range(1, place.tasks // 2):
                total = total + slots[base + k]
        out[...] = total

    def plan(self, plan, needs, out):
        plan.event("m0", 0.1, [(name, 0.0) for name in needs], functools.partial(self.hop, 0))
        plan.event("m1", 0.1, [("m0", 2.0)], functools.partial(self.hop, 1))
        plan.event("m2", 0.1, [("m1", 3.0)], functools.partial(self.hop, 2))
        plan.event("m3", 0.1, [("m2", 3.0)], self.along_z)
        plan.event("m4", 0.1, [("m3", 4.0)], functools.partial(self.end, out))


HOP = {"z": 8.0, "period": 9.5, "a": 11.0, "c": 13.0, "core": 4.0, "turn": 6.0, "D": 4.0, "C": 8.0, "A": 8.0, "Z": 12.0}
AHEAD = 2


def layer_kernel(tasks, shards, *refs):
    tgt_len, src_len, counts, x_hbm, enc_hbm, cot_hbm, small_ref = refs[:7]
    mats = refs[7:17]
    layer_out, grad_in, grad_enc, *outs, from_task, small_out = refs[17:25]
    (w, wo, pi, po, act, hidden, after_self, after_cross, upstream, dn, x, enc, small, dsmall, strip, line, key_mask,
     share, *slots_refs) = refs[25:]
    from_core, from_third, from_second, from_z, fin, tasks_here, small_slots = slots_refs[:7]
    credits, local_sem, in_sem, out_sem, send_sem, recv_sem = slots_refs[7:11], *slots_refs[11:]
    place = Place(tasks, shards)
    layer = Layer(
        tgt_len=tgt_len, src_len=src_len, x=x, enc=enc, w=w, wo=wo, pi=pi, po=po, act=act,
        after_self=after_self, after_cross=after_cross, upstream=upstream, dn=dn, small=small, dsmall=dsmall, strip=strip, line=line,
        key_mask=key_mask, share=share, places=shards,
    )
    sends = Sends(send_sem, recv_sem)
    gather = Gather(place, layer, mats, small_ref, local_sem, sends)
    gather.local()
    loads = []
    for number, (src, dst) in enumerate([(x_hbm, x), (cot_hbm, act.at[G3]), (enc_hbm, enc)]):
        loads.append(pltpu.make_async_copy(src, dst, in_sem.at[number]))
        loads[-1].start()
    total = counts[0]
    for task in range(1, tasks):
        total = total + counts[task]
    share[0] = counts[place.t].astype(F32) / total.astype(F32)
    place.greet(True)
    scatter = Scatter(
        place, layer, (from_core, from_third, from_second, from_z), outs, fin, from_task, tasks_here, credits,
        local_sem.at[pl.ds(9, WINDOW)], local_sem.at[9 + WINDOW], sends,
    )
    tail = SmallSums(place, layer, small_slots, sends)
    plan = Plan()
    gather.plan(plan)
    stores = {}

    def store(number, slot, out):
        stores[number] = lambda: pltpu.make_async_copy(act.at[slot], out, out_sem.at[number])
        stores[number]().start()

    part = functools.partial

    def attend(cross, third):
        @pl.loop(0, H // 6)
        def _(hp):
            layer.attend(hp + third * (H // 6), cross)

    none = lax.div(place.t, tasks)

    def attend_back(cross, hp):
        @pl.loop(hp + none, hp + 1)
        def _(here):
            layer.attend_back(here, cross)

    def project_self(first, last):
        @pl.loop(first, last)
        def _(u):
            act[QS + u] = dot(act[NS], layer.unit(u)).astype(BF)

    def source(u):
        act[KC + u] = dot(enc[...], layer.unit(5 + u)).astype(BF)

    piece = plan.piece

    def begin():
        loads[1].wait()
        layer.masks()
        small[...] = jnp.zeros_like(small)
        layer.live_cot()
        loads[0].wait()
        loads[2].wait()

    piece("begin", 0.8, ["zs"], begin)
    piece("strip", 1.5, ["small", "begin"], lambda: [layer.sum_small(), layer.bias_strip(), layer.norm_self()])
    piece("qk", 1.6, ["strip", "w0"], part(project_self, 0, 2))
    piece("v", 0.8, ["strip", "w1"], part(project_self, 2, 3))
    for k in range(3):
        piece(f"self{k}", 2.6, [f"self{k - 1}"] if k else ["qk", "v"], part(attend, False, k))
    piece("close_self", 1.5, ["self2"], layer.close_self)
    piece("kc", 0.8, ["w2", "begin"], part(source, 0))
    piece("qc", 0.8, ["close_self", "w2"], layer.project_query)
    piece("vc", 0.8, ["w3", "begin"], part(source, 1))
    for k in range(3):
        piece(f"cross{k}", 3.0, [f"cross{k - 1}"] if k else ["qc", "kc", "vc"], part(attend, True, k))
    piece("close_cross", 0.7, ["cross2", "w3"], layer.close_cross)

    for c in range(4):
        piece(f"sent{c}", 0.1, [f"w{UNITS - 1}", "close_cross"] if c == 0 else [f"sent{c - 1}"], part(gather.sent, c))

    layer.hidden = hidden

    def ffn(slope):
        layer.slope = slope
        for j in range(4):
            piece(f"h{j}", 1.4, ["close_cross", f"w{4 + j // 2}"], part(layer.ffn_hidden, j))
        for j in range(4):
            piece(f"go{j}", 0.8, [f"h{j}"], part(layer.grad_ffn_out, j))
        for j in range(4):
            piece(f"fb{j}", 1.6, [f"h{k}" for k in range(4)] + ["w6", "w7"], part(layer.ffn_back, j))
        for j in range(4):
            piece(f"gi{j}", 0.9, [f"fb{j}"], part(layer.grad_unit, 8 + j, act.at[NF], slope.at[j]))
        plan.run_until([f"gi{j}" for j in range(4)] + [f"fb{j}" for j in range(4)])

    def back(dstrip, lines):
        layer.dstrip, layer.lines = dstrip, lines
        piece("fnb", 2.0, [], layer.ffn_norm_back)
        piece("dmc", 0.8, ["fnb", "sent3"], part(layer.mix_back, 7))
        piece("g7", 0.8, ["fnb", "sent3"], part(layer.grad_unit, 7, act.at[MC], act.at[G3]))
        for k in range(H // 2):
            piece(f"bc{k}", 2.3, [f"bc{k - 1}"] if k else ["dmc"], part(attend_back, True, k))
        for n, src, grad in ((6, enc, DV), (5, enc, DK), (4, act.at[NC], DQ)):
            piece(f"g{n}", 0.8, ["bc5", "sent3"], part(layer.grad_unit, n, src, act.at[grad]))
        piece("qb", 0.8, ["bc5"], layer.query_back)
        piece("cnb", 2.0, ["qb"], layer.cross_norm_back)
        piece("dms", 1.2, ["cnb", "g7"], lambda: [layer.mix_back(3), layer.clear_strip()])
        piece("g3", 0.8, ["dms"], part(layer.grad_unit, 3, act.at[MS], act.at[G3]))
        for k in range(H // 2):
            needs = [f"bs{k - 1}"] if k else ["dms", "g4", "g5", "g6"]
            piece(f"bs{k}", 1.9, needs, part(attend_back, False, k))
        for k in range(3):
            piece(f"sb{k}", 0.9, [f"sb{k - 1}"] if k else ["bs5"], part(layer.self_back, k))
        for k in (2, 1, 0):
            piece(f"g{k}", 0.8, ["sb2"], part(layer.grad_unit, k, act.at[NS], act.at[QC + k]))
        piece("bias", 2.4, ["bs5"], layer.bias_grad)
        piece("snb", 2.0, ["sb2"], lambda: [layer.self_norm_back(), store(1, NC, grad_in)])
        piece("eb0", 0.8, ["bs5"], part(layer.source_back, 0))
        piece("eb1", 0.8, ["eb0"], lambda: [layer.source_back(1), store(2, MC, grad_enc)])
        for j in range(4):
            piece(f"out{j}", 0.9, ["bs5"], part(layer.ffn_out, j))
        piece("out", 0.6, [f"out{j}" for j in range(4)], lambda: [layer.ffn_result(), store(0, DQ, layer_out)])
        plan.run_until(None)

    order = (6, 7, 4, 5, 3, 2, 1, 0)
    needs = {c: [f"g{2 * c}", f"g{2 * c + 1}"] for c in range(4)}
    needs.update({4: ["gi0", "gi1"], 5: ["gi2", "gi3"]})
    needs.update({c: [f"go{j}" for j in range(4)] + [f"w{UNITS - 1}"] for c in (6, 7)})
    scatter.plan(plan, order, needs)
    tail.plan(plan, ["snb", "bias", "cnb", "fnb"], small_out)
    pl.run_scoped(ffn, pltpu.VMEM((4, ROWS, D), BF))
    pl.run_scoped(
        back, pltpu.VMEM((H, BLOCK, ROWS), F32), pltpu.VMEM((H, 8, ROWS + BLOCK), F32)
    )
    scatter.finish()
    for number in range(3):
        stores[number]().wait()
    sends.finish()


def run_layer(arrays, mats, small, counts, tasks, shards):
    zs, pairs, rows = shards // COLS, tasks // 2, mats[0].shape[0]
    shape = jax.ShapeDtypeStruct
    vmem = pltpu.VMEM
    unit = (zs, COLS, rows, D)
    full = shape((ROWS, D), BF)
    out_shape = (
        full, full, full,
        shape((8, rows, D), F32), shape((rows, 4 * D), F32), shape((4, rows, D), F32),
        shape((UNITS, pairs, rows, D) if tasks > 2 else (8, 128), F32), shape((SMALL, D), F32),
    )
    scratch = [
        vmem((12,) + unit, BF),
        vmem((zs, COLS, 4, rows, D), BF),
        vmem((4,) + unit, BF),
        vmem((zs, COLS, 4, rows, D), BF),
        vmem((15, ROWS, D), BF),
        vmem((4, ROWS, D), BF),
        vmem((ROWS, D), F32),
        vmem((ROWS, D), F32),
        vmem((ROWS, D), F32),
        vmem((ROWS, D), F32),
        vmem((ROWS, D), BF),
        vmem((ROWS, D), BF),
        vmem((SMALL, D), F32),
        vmem((SMALL, D), F32),
        vmem((H, BLOCK, ROWS), BF),
        vmem((SMALL, D), F32),
        vmem((SMALL, ROWS), F32),
        pltpu.SMEM((1,), F32),
        vmem((WINDOW,) + unit, BF),
        vmem((WINDOW, 2, zs, rows, D), BF),
        vmem((WINDOW, zs, rows, D), BF),
        vmem((WINDOW, zs - 1, rows, D), BF),
        vmem((WINDOW, rows, D), F32),
        vmem((pairs, rows, D) if tasks > 2 else (8, 128), F32),
        vmem((6 + zs + pairs, SMALL, D), F32),
        pltpu.SemaphoreType.REGULAR,
        pltpu.SemaphoreType.REGULAR,
        pltpu.SemaphoreType.REGULAR,
        pltpu.SemaphoreType.REGULAR((zs - 1,)),
    ]
    number = UNITS * (zs - 1 + 7) + (zs - 1) + 3 + UNITS * (5 + zs - 1 + pairs - 1) + 3 + zs - 1 + pairs - 1
    scratch += [
        pltpu.SemaphoreType.DMA((10 + WINDOW,)),
        pltpu.SemaphoreType.DMA((3,)),
        pltpu.SemaphoreType.DMA((3,)),
        pltpu.SemaphoreType.DMA((number,)),
        pltpu.SemaphoreType.DMA((number,)),
    ]
    anywhere = pl.BlockSpec(memory_space=pl.ANY)
    return pl.pallas_call(
        functools.partial(layer_kernel, tasks, shards),
        out_shape=out_shape,
        in_specs=[pl.BlockSpec(memory_space=pltpu.SMEM)] * 3 + [anywhere] * 14,
        out_specs=[anywhere] * 7 + [pl.BlockSpec(memory_space=pltpu.VMEM)],
        scratch_shapes=scratch,
        compiler_params=pltpu.CompilerParams(
            collective_id=1, has_side_effects=True, vmem_limit_bytes=63 * 2**20
        ),
        cost_estimate=pl.CostEstimate(flops=35_000_000_000, bytes_accessed=60_000_000, transcendentals=10_000_000),
        name="layer",
    )(*counts, *arrays, small, *mats)


def on_device(
    inputs, encoded, cotangent, tgt_len, src_len, task_counts,
    gain_self, query_self, key_self, value_self, out_self, bias_table,
    gain_cross, query_cross, key_cross, value_cross, out_cross, gain_ffn, ffn_in, ffn_out,
):
    tasks, rows = task_counts.shape[0], gain_self.shape[0]
    shards, buckets = D // rows, bias_table.shape[0]
    at = lax.axis_index("shard")
    small = jnp.zeros((SMALL, D), BF)
    gains = jnp.stack([gain_self, gain_cross, gain_ffn])
    small = lax.dynamic_update_slice(small, gains, (0, at * rows))
    small = lax.dynamic_update_slice(small, bias_table.T, (3, at * buckets))
    mats = (
        query_self, key_self, value_self, out_self, query_cross, key_cross, value_cross, out_cross, ffn_in, ffn_out,
    )
    arrays = (inputs.reshape(ROWS, D), encoded.reshape(ROWS, D), cotangent.reshape(ROWS, D))
    layer_out, grad_in, grad_enc, units, g_in, g_out, _, sums = run_layer(
        arrays, mats, small, (tgt_len, src_len, task_counts), tasks, shards
    )
    g_gain = lax.dynamic_slice(sums, (0, at * rows), (3, rows))
    g_table = lax.dynamic_slice(sums, (3, at * buckets), (H, buckets)).T
    return (
        layer_out.reshape(inputs.shape), grad_in.reshape(inputs.shape), grad_enc.reshape(inputs.shape),
        g_gain[0], units[0], units[1], units[2], units[3], g_table,
        g_gain[1], units[4], units[5], units[6], units[7],
        g_gain[2], g_in, g_out.reshape(4 * rows, D),
    )


def solution(mesh):
    placed = (
        P(("task", "shard"), None, None),
        P(("task", "shard"), None, None),
        P(("task", "shard"), None, None),
        P(("task", "shard")),
        P(("task", "shard")),
        P(),
        P("shard"),
        P("shard", None),
        P("shard", None),
        P("shard", None),
        P("shard", None),
        P("shard", None),
        P("shard"),
        P("shard", None),
        P("shard", None),
        P("shard", None),
        P("shard", None),
        P("shard"),
        P("shard", None),
        P("shard", None),
    )
    return jax.shard_map(
        on_device,
        mesh=mesh,
        in_specs=placed,
        out_specs=(
            P(("task", "shard"), None, None),
            P(("task", "shard"), None, None),
            P(("task", "shard"), None, None),
            P("shard"),
            P("shard", None),
            P("shard", None),
            P("shard", None),
            P("shard", None),
            P("shard", None),
            P("shard"),
            P("shard", None),
            P("shard", None),
            P("shard", None),
            P("shard", None),
            P("shard"),
            P("shard", None),
            P("shard", None),
        ),
        check_vma=False,
    )
```

```python
import functools
import math

import jax
import jax.numpy as jnp
import numpy as np
from jax import lax
from jax.experimental import pallas as pl
from jax.experimental.pallas import tpu as pltpu
from jax.sharding import PartitionSpec as P

H = 12
DH = 64
NB = 32
D = 768
EPSILON = 1e-06
MASKED = -1000000000.0
LIMITS = np.array(
    list(range(1, 16))
    + [math.ceil(16.0 * 8.0 ** ((bucket - 16) / 16.0)) for bucket in range(16, 32)],
    dtype=np.int32,
)
MESH = pl.DeviceIdType.MESH
BF = jnp.bfloat16
F32 = jnp.float32
COLS = 4
SMALL = 16


class Place:
    def __init__(self, tasks, shards):
        self.tasks, self.zs = tasks, shards // COLS
        self.t, self.s = lax.axis_index("task"), lax.axis_index("shard")
        self.half = lax.rem(self.t, 2)
        self.other = 1 - self.half
        self.z, self.q = lax.div(self.s, COLS), lax.rem(self.s, COLS)
        flip_x = self.q + 1 - 2 * lax.rem(self.q, 2)
        flip_y = lax.rem(self.q + 2, COLS)
        self.qx, self.qy = flip_x, flip_y
        self.q2 = flip_x + self.half * (flip_y - flip_x)
        self.q3 = flip_y + self.half * (flip_x - flip_y)
        self.q4 = COLS - 1 - self.q
        self.core = (self.t + 1 - 2 * self.half, self.s)
        self.second = (self.t, self.z * COLS + self.q2)
        self.third = (self.t, self.z * COLS + self.q3)

    def along_z(self, step):
        z = lax.rem(self.z + step, self.zs)
        return z, (self.t, z * COLS + self.q)

    def along_task(self, step):
        return (lax.rem(self.t + 2 * step, self.tasks), self.s)

    def greet(self, task_peers):
        peers = [self.core, self.second, self.third]
        peers += [self.along_z(k)[1] for k in range(1, self.zs)]
        if task_peers:
            peers += [self.along_task(k) for k in range(1, self.tasks // 2)]
        barrier = pltpu.get_barrier_semaphore()
        for peer in peers:
            pl.semaphore_signal(barrier, inc=1, device_id=peer, device_id_type=MESH)
        pl.semaphore_wait(barrier, len(peers))


class Sends:
    def __init__(self, send_sem, recv_sem):
        self.send_sem, self.recv_sem, self.made, self.done = send_sem, recv_sem, {}, set()

    def copy(self, key):
        number, describe = self.made[key]
        src, dst, device = describe()
        return pltpu.make_async_remote_copy(
            src_ref=src,
            dst_ref=dst,
            send_sem=self.send_sem.at[number],
            recv_sem=self.recv_sem.at[number],
            device_id=device,
            device_id_type=MESH,
        )

    def start(self, key, describe):
        self.made[key] = (len(self.made), describe)
        self.copy(key).start()

    def arrived(self, key):
        self.copy(key).wait_recv()

    def sent(self, key):
        self.copy(key).wait_send()
        self.done.add(key)

    def finish(self):
        for key in [key for key in self.made if key not in self.done]:
            self.sent(key)


NS, QS, KS, VS, MS, NC, QC, KC, VC, MC, NF, G3, DQ, DK, DV = range(15)
DM = NF
ROWS = 512
BLOCK = 128
BLOCKS = ROWS // BLOCK
TALL = 256


def halves(body):
    @pl.loop(0, 2)
    def _(i):
        body(pl.ds(pl.multiple_of(i * (ROWS // 2), ROWS // 2), ROWS // 2))


def dot(a, b):
    return jnp.dot(a, b, preferred_element_type=F32)


def dot_t(a, b):
    return lax.dot_general(a, b, (((1,), (1,)), ((), ())), preferred_element_type=F32)


def t_dot(a, b):
    return lax.dot_general(a, b, (((0,), (0,)), ((), ())), preferred_element_type=F32)


def normed(v):
    inverse = lax.rsqrt(jnp.mean(v * v, axis=-1, keepdims=True) + EPSILON)
    return v * inverse, inverse


def smooth_parts(v):
    c = math.sqrt(2.0 / math.pi)
    square = v * v
    tanh = jnp.tanh(v * (c + (c * 0.044715) * square))
    left = 0.5 * (1.0 + tanh)
    slope = left + 0.5 * v * (1.0 - tanh * tanh) * (c + (3.0 * c * 0.044715) * square)
    return v * left, slope


class Layer:
    def __init__(
        self, tgt_len, src_len, x, enc, w, wo, pi, po, act, after_self, after_cross, upstream, dn, small, dsmall, strip, line,
        key_mask, share, places,
    ):
        self.tgt_len = tgt_len
        self.src_len = src_len
        self.x = x
        self.enc = enc
        self.w = w
        self.wo = wo
        self.pi = pi
        self.po = po
        self.act = act
        self.after_self = after_self
        self.after_cross = after_cross
        self.upstream = upstream
        self.dn = dn
        self.small = small
        self.dsmall = dsmall
        self.strip = strip
        self.line = line
        self.key_mask = key_mask
        self.share = share
        self.places = places

    def unit(self, n):
        return self.w[n].reshape(D, D)

    def live(self, start, size):
        rows = start + lax.broadcasted_iota(jnp.int32, (size, 1), 0)
        return rows < self.tgt_len[0]

    def gain(self, row):
        return self.small[pl.ds(row, 1), :]


    def sum_small(self):
        @pl.loop(0, self.places)
        def _(n):
            more = self.act[DV, pl.ds(pl.multiple_of(n * SMALL, SMALL), SMALL), :].astype(F32)
            self.add_rows(self.small, slice(0, SMALL), more, True)

    def masks(self):
        cols = lax.broadcasted_iota(jnp.int32, (8, ROWS), 1)
        self.key_mask[0:8, :] = jnp.where(cols < self.tgt_len[0], 0.0, MASKED)
        self.key_mask[8:16, :] = jnp.where(cols < self.src_len[0], 0.0, MASKED)

    def bucket_of(self, distance):
        bucket = jnp.zeros(distance.shape, jnp.int32)
        for limit in LIMITS:
            bucket = bucket + (distance >= int(limit)).astype(jnp.int32)
        return bucket

    def bias_strip(self):
        wide = 768
        lane = lax.broadcasted_iota(jnp.int32, (NB, wide), 1)
        bucket = self.bucket_of(jnp.maximum(511 - lane, 0))
        onehot = (bucket == lax.broadcasted_iota(jnp.int32, (NB, wide), 0)).astype(F32)
        table = self.small[:, 0:NB]
        line = jnp.dot(table, onehot, precision=lax.Precision.HIGHEST, preferred_element_type=F32)
        line = jnp.where(lax.broadcasted_iota(jnp.int32, (SMALL, wide), 1) <= 511, line, MASKED)
        self.line[...] = line

        @pl.loop(0, H)
        def _(h):
            row = jnp.broadcast_to(self.line[pl.ds(h + 3, 1), :], (BLOCK, wide))
            rolled = pltpu.roll(row, wide - 127, 1, stride=1, stride_axis=0)
            self.strip[h] = rolled[:, 0:ROWS].astype(BF)

    def clear_strip(self):
        self.dstrip[...] = jnp.zeros_like(self.dstrip)

    def bias_grad(self):
        wide = ROWS + BLOCK

        @pl.loop(0, H)
        def _(h):
            total = None
            for r in range(BLOCK // 8):
                rows = jnp.concatenate(
                    [self.dstrip[h, 8 * r : 8 * r + 8, :], jnp.zeros((8, BLOCK), F32)], axis=1
                )
                if r:
                    rows = pltpu.roll(rows, wide - 8 * r, 1)
                total = rows if total is None else total + rows
            self.lines[h] = total

        grad = jnp.zeros((H, NB), F32)
        lane = lax.broadcasted_iota(jnp.int32, (NB, wide), 1)
        for s in range(8):
            distance = ROWS - BLOCK + s - lane + jnp.where(lane >= ROWS, wide, 0)
            bucket = self.bucket_of(jnp.maximum(distance, 0))
            fits = bucket == lax.broadcasted_iota(jnp.int32, (NB, wide), 0)
            grad = grad + lax.dot_general(
                self.lines[:, s, :], fits.astype(F32), (((1,), (1,)), ((), ())),
                precision=lax.Precision.HIGHEST, preferred_element_type=F32,
            )
        self.dsmall[3 : 3 + H, 0:NB] = grad


    def norm_self(self):
        @pl.loop(0, BLOCKS)
        def _(i):
            rows = pl.ds(pl.multiple_of(i * BLOCK, BLOCK), BLOCK)
            n, _ = normed(self.x[rows, :].astype(F32))
            self.act[NS, rows, :] = (n * self.gain(0)).astype(BF)

    def pair(self, value, h):
        lane = lax.broadcasted_iota(jnp.int32, value.shape, 1)
        return jnp.where((lane < 64) == (h == 0), value, jnp.zeros_like(value))

    def probs(self, q, k, head, first, keys, cross):
        s = dot_t(q, k)
        if cross:
            s = s + self.key_mask[8:9, 0:keys]
        else:
            parts = []
            for here in range(first, keys, BLOCK):
                strip = self.strip[head, :, ROWS - here - BLOCK :].astype(F32)
                if here + BLOCK < keys:
                    beyond = jnp.full((BLOCK, keys - here - BLOCK), MASKED, F32)
                    strip = jnp.concatenate([strip, beyond], axis=1)
                parts.append(strip)
            s = s + (jnp.concatenate(parts, axis=0) + self.key_mask[0:1, 0:keys])
        p = jnp.exp(s - jnp.max(s, axis=-1, keepdims=True))
        return p * (1.0 / jnp.sum(p, axis=-1, keepdims=True))

    def attend(self, hp, cross):
        base = NC if cross else NS
        cols = pl.ds(pl.multiple_of(hp * 128, 128), 128)
        k, v = self.act[base + 2, :, cols], self.act[base + 3, :, cols]
        for first in range(0, ROWS, TALL):
            rows = slice(first, first + TALL)
            keys = ROWS if cross else first + TALL
            q = self.act[base + 1, rows, cols]
            total = None
            for h in range(2):
                p = self.probs(self.pair(q, h), k[:keys], 2 * hp + h, first, keys, cross).astype(BF)
                term = dot(p, self.pair(v[:keys], h))
                total = term if total is None else total + term
            self.act[base + 4, rows, cols] = total.astype(BF)

    def close_self(self):
        self.dn[...] = dot(self.act[MS], self.unit(3))

        @pl.loop(0, BLOCKS)
        def _(i):
            rows = pl.ds(pl.multiple_of(i * BLOCK, BLOCK), BLOCK)
            after = self.x[rows, :].astype(F32) + self.dn[rows, :]
            self.after_self[rows, :] = after
            n, _ = normed(after)
            self.act[NC, rows, :] = (n * self.gain(1)).astype(BF)

    def project_query(self):
        self.act[QC] = dot(self.act[NC], self.unit(4)).astype(BF)

    def close_cross(self):
        self.dn[...] = dot(self.act[MC], self.unit(7))

        @pl.loop(0, BLOCKS)
        def _(i):
            rows = pl.ds(pl.multiple_of(i * BLOCK, BLOCK), BLOCK)
            after = self.after_self[rows, :] + self.dn[rows, :]
            self.after_cross[rows, :] = after
            n, _ = normed(after)
            self.act[NF, rows, :] = (n * self.gain(2)).astype(BF)

    def live_cot(self):
        @pl.loop(0, BLOCKS)
        def _(i):
            start = pl.multiple_of(i * BLOCK, BLOCK)
            rows = pl.ds(start, BLOCK)
            cot = self.act[G3, rows, :]
            self.act[G3, rows, :] = jnp.where(self.live(start, BLOCK), cot, jnp.zeros_like(cot))

    def ffn_hidden(self, j):
        self.dn[...] = dot(self.act[NF], self.unit(8 + j))

        @pl.loop(0, BLOCKS)
        def _(i):
            rows = pl.ds(pl.multiple_of(i * BLOCK, BLOCK), BLOCK)
            act, slope = smooth_parts(self.dn[rows, :])
            self.hidden[j, rows, :] = act.astype(BF)
            self.slope[j, rows, :] = slope.astype(BF)

    def outer(self, a, b, store):
        @pl.loop(0, 2)
        def _(m):
            cols = pl.ds(pl.multiple_of(m * 384, 128), 384)
            store(m, (t_dot(a[:, cols], b[...]) * self.share[0]).astype(BF))

    def grad_unit(self, n, a, b):
        half, rows = self.w.shape[1] // 2, self.w.shape[3]
        place = self.w if n < 8 else self.pi
        number = {0: n, 1: n + 4, 2: n - 8}[n // 4]

        def store(m, value):
            place[number, pl.ds(m * half, half)] = value.reshape(half, COLS, rows, D)

        self.outer(a, b, store)

    def grad_ffn_out(self, j):
        some, rows = self.wo.shape[0] // 4, self.wo.shape[3]

        def store(m, value):
            if some == 1:
                self.po[j, pl.ds(2 * m, 2)] = value.reshape(2, 4, rows, D)
            else:
                self.po[pl.ds(j * some + m * (some // 2), some // 2)] = value.reshape(some // 2, COLS, 4, rows, D)

        self.outer(self.hidden.at[j], self.act.at[G3], store)

    def ffn_out(self, j):
        @halves
        def _(rows):
            self.after_cross[rows, :] += dot(self.hidden[j, rows, :], self.wo_rows(j))

    def ffn_result(self):
        @pl.loop(0, BLOCKS)
        def _(i):
            start = pl.multiple_of(i * BLOCK, BLOCK)
            rows = pl.ds(start, BLOCK)
            self.act[DQ, rows, :] = jnp.where(self.live(start, BLOCK), self.after_cross[rows, :], 0.0).astype(BF)

    def wo_rows(self, j):
        eighth = self.wo.shape[0] // 4
        return self.wo[pl.ds(j * eighth, eighth)].reshape(D, D)


    def ffn_back(self, j):
        @halves
        def _(rows):
            grad = dot_t(self.act[G3, rows, :], self.wo_rows(j)) * self.slope[j, rows, :].astype(F32)
            self.slope[j, rows, :] = grad.astype(BF)
        @halves
        def _(rows):
            self.add_rows(self.dn, rows, dot_t(self.slope[j, rows, :], self.unit(8 + j)), j)

    def add_rows(self, ref, rows, value, more):
        if more:
            ref[rows, :] += value
        else:
            ref[rows, :] = value

    def norm_back(self, values, gain_row, upstream, dst, branch):
        self.dsmall[gain_row : gain_row + 1, :] = jnp.zeros((1, D), F32)

        @pl.loop(0, BLOCKS)
        def _(i):
            rows = pl.ds(pl.multiple_of(i * BLOCK, BLOCK), BLOCK)
            n, inverse = normed(values(rows))
            dn = self.dn[rows, :]
            self.dsmall[gain_row : gain_row + 1, :] += jnp.sum(dn * n, axis=0, keepdims=True)
            scaled = dn * self.gain(gain_row)
            back = inverse * (scaled - n * jnp.mean(scaled * n, axis=-1, keepdims=True))
            total = upstream(rows) + back
            if dst is not None:
                dst[rows, :] = total
            branch[rows, :] = total.astype(BF)

    def ffn_norm_back(self):
        self.norm_back(
            lambda rows: self.after_cross[rows, :], 2,
            lambda rows: self.act[G3, rows, :].astype(F32), self.upstream, self.act.at[G3],
        )

    def mix_back(self, unit):
        self.act[DM] = dot_t(self.act[G3], self.unit(unit)).astype(BF)

    def attend_back(self, hp, cross):
        base, to = (NC, DQ) if cross else (NS, QC)
        cols = pl.ds(pl.multiple_of(hp * 128, 128), 128)
        k, v = self.act[base + 2, :, cols], self.act[base + 3, :, cols]
        own = [self.pair(k, h) for h in range(2)]
        for first in reversed(range(0, ROWS, TALL)):
            rows = slice(first, first + TALL)
            keys = ROWS if cross else first + TALL
            q, dm = self.act[base + 1, rows, cols], self.act[DM, rows, cols]
            prod = dm.astype(F32) * self.act[base + 4, rows, cols].astype(F32)
            dq = dk = dv = None
            for h in range(2):
                qh, dmh = self.pair(q, h), self.pair(dm, h)
                p = self.probs(qh, k[:keys], 2 * hp + h, first, keys, cross)
                dp = dot_t(dmh, v[:keys])
                delta = jnp.sum(self.pair(prod, h), axis=-1, keepdims=True)
                ds = p * (dp - delta)
                if not cross:
                    for here in range(first, keys, BLOCK):
                        upto = here + BLOCK
                        self.dstrip[2 * hp + h, :, ROWS - upto :] += ds[here - first : upto - first, :upto]
                ds = ds.astype(BF)
                terms = (dot(ds, own[h][:keys]), t_dot(ds, qh), t_dot(p.astype(BF), dmh))
                dq, dk, dv = terms if dq is None else (dq + terms[0], dk + terms[1], dv + terms[2])
            self.act[to, rows, cols] = dq.astype(BF)
            self.add_rows(self.dn.at[:, 0:128], slice(0, keys), dk, first + TALL < ROWS)
            self.add_rows(self.dn.at[:, 128:256], slice(0, keys), dv, first + TALL < ROWS)
        self.act[to + 1, :, cols] = self.dn[:, 0:128].astype(BF)
        self.act[to + 2, :, cols] = self.dn[:, 128:256].astype(BF)

    def source_back(self, k):
        @halves
        def _(rows):
            back = dot_t(self.act[DK + k, rows, :], self.unit(5 + k))
            if k:
                self.act[MC, rows, :] = (self.after_self[rows, :] + back).astype(BF)
            else:
                self.after_self[rows, :] = back

    def query_back(self):
        self.dn[...] = dot_t(self.act[DQ], self.unit(4))

    def cross_norm_back(self):
        self.norm_back(
            lambda rows: self.after_self[rows, :], 1,
            lambda rows: self.upstream[rows, :], self.upstream, self.act.at[G3],
        )

    def self_back(self, k):
        @halves
        def _(rows):
            self.add_rows(self.dn, rows, dot_t(self.act[QC + k, rows, :], self.unit(k)), k)

    def self_norm_back(self):
        self.norm_back(
            lambda rows: self.x[rows, :].astype(F32), 0,
            lambda rows: self.upstream[rows, :], None, self.act.at[NC],
        )


UNITS = 8
WINDOW = 2


class Plan:
    def __init__(self):
        self.work, self.events, self.at, self.log = [], [], {}, []
        self.now = 0.0

    def piece(self, name, cost, needs, run):
        self.work.append((name, cost, needs, run))

    def event(self, name, cost, needs, run):
        self.events.append((name, cost, needs, run))

    def due(self, needs):
        if any(name not in self.at for name, _ in needs):
            return None
        return max([self.at[name] + wait for name, wait in needs], default=0.0)

    def take(self, where, item, start):
        name, cost, _, run = item
        where.remove(item)
        self.now = max(self.now, start) + cost
        run()
        self.at[name] = self.now
        self.log.append((round(self.now, 1), name))

    def run_until(self, name):
        while (self.work or self.events) if name is None else any(each not in self.at for each in name):
            dues = [(self.due(item[2]), number) for number, item in enumerate(self.events)]
            dues = [pair for pair in dues if pair[0] is not None]
            first = min(dues, default=None)
            if first is not None and first[0] <= self.now:
                self.take(self.events, self.events[first[1]], first[0])
                continue
            ready = [item for item in self.work if all(name in self.at for name in item[2])]
            if ready:
                self.take(self.work, ready[0], self.now)
            else:
                self.take(self.events, self.events[first[1]], first[0])


class Gather:
    def __init__(self, place, layer, mats, small_ref, local_sem, sends):
        self.place, self.layer, self.mats, self.small_ref = place, layer, mats, small_ref
        self.local_sem, self.sends = local_sem, sends

    def column(self, c, q):
        if c < 6:
            return self.layer.w.at[2 * c + self.place.half, :, q]
        return self.layer.wo.at[:, q, 2 * (c - 6) + self.place.half]

    def slab(self, c, z, q):
        if c < 6:
            return self.layer.w.at[2 * c + self.place.half, z, q]
        return self.layer.wo.at[z, q, 2 * (c - 6) + self.place.half]

    def both(self, key, here, device):
        self.sends.start(key, lambda: (here(), here(), device()))

    def local(self):
        place, w, wo = self.place, self.layer.w, self.layer.wo
        z, q = place.z, place.q
        rows = w.shape[3]
        self.copies = []
        for n in range(16):
            if n < 8:
                src, dst = self.mats[n], w.at[n, z, q]
            elif n < 12:
                src, dst = self.mats[8].at[:, pl.ds(D * (n - 8), D)], w.at[n, z, q]
            else:
                src, dst = self.mats[9].at[pl.ds(rows * (n - 12), rows)], wo.at[z, q, n - 12]
            self.copies.append(pltpu.make_async_copy(src, dst, self.local_sem.at[n // 2]))
        for n in range(16):
            @pl.when(place.half == n % 2)
            def _():
                self.copies[n].start()
        self.small_copy = pltpu.make_async_copy(self.small_ref, self.small_at(z, q), self.local_sem.at[8])
        self.small_copy.start()

    def small_at(self, z, q):
        row = (q * self.place.zs + z) * SMALL
        return self.layer.act.at[DV, pl.ds(pl.multiple_of(row, SMALL), SMALL)]

    def small_column(self, q):
        size = self.place.zs * SMALL
        return self.layer.act.at[DV, pl.ds(pl.multiple_of(q * size, SMALL), size)]

    def start_small(self):
        self.small_copy.wait()
        place = self.place
        for k in range(1, place.zs):
            self.both(("zs", k), lambda: self.small_at(place.z, place.q), lambda k=k: place.along_z(k)[1])

    def small_second(self):
        place = self.place
        for k in range(1, place.zs):
            self.sends.arrived(("zs", k))
        self.both("as", lambda: self.small_column(place.q), lambda: place.second)
        self.both("bs", lambda: self.small_column(place.q), lambda: place.third)

    def small_third(self):
        place = self.place
        self.sends.arrived("as")
        self.both("cs", lambda: self.small_column(place.q2), lambda: place.third)

    def small_ready(self):
        self.sends.arrived("bs")
        self.sends.arrived("cs")

    def start_z(self, c):
        place = self.place
        self.copies[2 * c].wait()
        for k in range(1, place.zs):
            self.both(("z", c, k), lambda: self.slab(c, place.z, place.q), lambda k=k: place.along_z(k)[1])

    def send_column(self, name, c, q, device):
        self.both((name, c), lambda: self.column(c, q), lambda: device)

    def from_z(self, c):
        place = self.place
        for k in range(1, place.zs):
            self.sends.arrived(("z", c, k))
        self.send_column("a", c, place.q, place.second)
        self.send_column("b", c, place.q, place.third)
        self.send_column("d1", c, place.q, place.core)

    def from_second(self, c):
        place = self.place
        self.sends.arrived(("a", c))
        self.send_column("c", c, place.q2, place.third)
        self.send_column("d2", c, place.q2, place.core)

    def from_third(self, c):
        place = self.place
        self.sends.arrived(("b", c))
        self.send_column("d3", c, place.q3, place.core)
        self.sends.arrived(("c", c))
        self.send_column("d4", c, place.q4, place.core)

    def sent(self, part):
        for c in range(2 * part, 2 * part + 2):
            for key in [("z", c, k) for k in range(1, self.place.zs)]:
                self.sends.sent(key)
            for name in ("a", "b", "c", "d1", "d2", "d3", "d4"):
                self.sends.sent((name, c))
        if part == 3:
            for key in [("zs", k) for k in range(1, self.place.zs)] + ["as", "bs", "cs"]:
                self.sends.sent(key)

    def ready(self, c):
        for name in ("d1", "d2", "d3", "d4"):
            self.sends.arrived((name, c))

    def plan(self, plan):
        hop = HOP
        plan.event("zs", 0.3, [("z0", 0.0)], self.start_small)
        for c in range(UNITS):
            needs = [] if c == 0 else [("zs", 0.0)] if c < AHEAD else [(f"a{c - AHEAD}", 0.0)]
            plan.event(f"z{c}", 0.2, needs, functools.partial(self.start_z, c))
            needs = [(f"z{c}", hop["z"])] + ([(f"a{c - 1}", hop["period"])] if c else [])
            plan.event(f"a{c}", 0.2, needs, functools.partial(self.from_z, c))
            plan.event(f"b{c}", 0.2, [(f"a{c}", hop["a"])], functools.partial(self.from_second, c))
            plan.event(f"c{c}", 0.2, [(f"b{c}", hop["c"])], functools.partial(self.from_third, c))
            plan.event(f"w{c}", 0.1, [(f"c{c}", hop["core"])], functools.partial(self.ready, c))
        plan.event("as", 0.2, [("zs", 2.5)], self.small_second)
        plan.event("cs", 0.1, [("as", 2.0)], self.small_third)
        plan.event("small", 0.1, [("cs", 2.0)], self.small_ready)


class Scatter:
    def __init__(self, place, layer, slots, outs, fin, from_task, tasks_here, credits, local_sem, task_sem, sends):
        self.place, self.layer, self.outs, self.fin, self.from_task = place, layer, outs, fin, from_task
        self.tasks_here, self.task_sem = tasks_here, task_sem
        self.from_core, self.from_third, self.from_second, self.from_z = slots
        self.core_credit, self.third_credit, self.second_credit, self.z_credit = credits
        self.local_sem, self.sends = local_sem, sends

    def part(self, c, part):
        layer = self.layer
        if c < 2:
            return layer.w.at[2 * c + part]
        if c < 4:
            return layer.w.at[2 * c + part + 4]
        if c < 6:
            return layer.pi.at[2 * c + part - 8]
        return layer.po.at[:, :, 2 * (c - 6) + part]

    def column(self, c, q):
        if c < 6:
            return self.part(c, self.place.half).at[:, q]
        return self.layer.po.at[:, q, 2 * (c - 6) + self.place.half]

    def slab(self, c, z, q):
        if c < 6:
            return self.part(c, self.place.half).at[z, q]
        return self.layer.po.at[z, q, 2 * (c - 6) + self.place.half]

    def add(self, c, q, arrived):
        @pl.loop(0, self.place.zs)
        def _(z):
            here = self.slab(c, z, q)
            here[...] = (here[...].astype(F32) + arrived(z)[...].astype(F32)).astype(BF)

    def credit(self, semaphore, device):
        pl.semaphore_signal(semaphore, inc=1, device_id=device, device_id_type=MESH)

    def to_core(self, r, c):
        place = self.place
        if r >= WINDOW:
            pl.semaphore_wait(self.core_credit, 1)
        self.sends.start(("D", c), lambda: (self.part(c, place.other), self.from_core.at[r % WINDOW], place.core))

    def to_third(self, r, c, last):
        place, slot = self.place, r % WINDOW
        self.sends.arrived(("D", c))
        for q in (place.q4, place.q3):
            self.add(c, q, lambda z, q=q: self.from_core.at[slot, z, q])
        if r >= WINDOW:
            pl.semaphore_wait(self.third_credit, 1)
        self.sends.start(("C", c), lambda: (self.column(c, place.q4), self.from_third.at[slot, 1], place.third))
        self.sends.start(("B", c), lambda: (self.column(c, place.q3), self.from_third.at[slot, 0], place.third))
        for q in (place.q2, place.q):
            self.add(c, q, lambda z, q=q: self.from_core.at[slot, z, q])
        if not last:
            self.credit(self.core_credit, place.core)

    def to_second(self, r, c):
        place, slot = self.place, r % WINDOW
        self.sends.arrived(("C", c))
        self.add(c, place.q2, lambda z: self.from_third.at[slot, 1, z])
        if r >= WINDOW:
            pl.semaphore_wait(self.second_credit, 1)
        self.sends.start(("A", c), lambda: (self.column(c, place.q2), self.from_second.at[slot], place.second))

    def to_z(self, r, c, last):
        place, slot = self.place, r % WINDOW
        self.sends.arrived(("B", c))
        self.sends.arrived(("A", c))

        @pl.loop(0, place.zs)
        def _(z):
            here = self.slab(c, z, place.q)
            total = here[...].astype(F32) + self.from_third[slot, 0, z].astype(F32)
            here[...] = (total + self.from_second[slot, z].astype(F32)).astype(BF)

        if not last:
            self.credit(self.third_credit, place.third)
            self.credit(self.second_credit, place.second)
        for k in range(1, place.zs):
            if r >= WINDOW:
                pl.semaphore_wait(self.z_credit.at[k - 1], 1)

            def describe(k=k):
                to, device = place.along_z(k)
                return self.slab(c, to, place.q), self.from_z.at[slot, k - 1], device

            self.sends.start(("Z", c, k), describe)

    def target(self, c):
        half = self.place.half
        if c < 4:
            return self.outs[0].at[2 * c + half]
        if c < 6:
            return self.outs[1].at[:, pl.ds(pl.multiple_of((2 * c - 8 + half) * D, D), D)]
        return self.outs[2].at[2 * (c - 6) + half]

    def last(self, r, c, last):
        place, slot = self.place, r % WINDOW
        for k in range(1, place.zs):
            self.sends.arrived(("Z", c, k))
        total = self.slab(c, place.z, place.q)[...].astype(F32)
        for k in range(1, place.zs):
            total = total + self.from_z[slot, k - 1].astype(F32)
        if not last:
            for k in range(1, place.zs):
                self.credit(self.z_credit.at[k - 1], place.along_z(place.zs - k)[1])
        if r >= WINDOW:
            before = self.order[r - WINDOW]
            self.store(before).wait()
            self.sends.sent(("F", before))
        self.fin[slot] = total
        if place.tasks > 2:
            self.over_tasks(r, c, slot)
        self.store(c).start()
        self.sends.start(("F", c), lambda: (self.fin.at[slot], self.target(c), place.core))

    def over_tasks(self, r, c, slot):
        place, pairs = self.place, self.place.tasks // 2
        group = lax.div(place.t, 2)

        def local(src, dst):
            copy = pltpu.make_async_copy(src, dst, self.task_sem)
            copy.start()
            copy.wait()

        for k in range(1, pairs):
            self.sends.start(("T", c, k), lambda k=k: (
                self.fin.at[slot], self.from_task.at[r, lax.div(place.t, 2)], place.along_task(k)))
        local(self.fin.at[slot], self.from_task.at[r, group])
        for k in range(1, pairs):
            self.sends.arrived(("T", c, k))
        for k in range(1, pairs):
            self.sends.sent(("T", c, k))
        local(self.from_task.at[r], self.tasks_here)
        total = self.tasks_here[0]
        for k in range(1, pairs):
            total = total + self.tasks_here[k]
        self.fin[slot] = total

    def store(self, c):
        slot = self.order.index(c) % WINDOW
        return pltpu.make_async_copy(self.fin.at[slot], self.target(c), self.local_sem.at[slot])

    def sent(self, c):
        for name in "DCBA":
            self.sends.sent((name, c))
        for k in range(1, self.place.zs):
            self.sends.sent(("Z", c, k))

    def finish(self):
        for c in self.order[-WINDOW:]:
            self.store(c).wait()
        for c in self.order:
            self.sends.arrived(("F", c))

    def plan(self, plan, order, needs):
        self.order, hop = order, HOP
        for r, c in enumerate(order):
            last = r >= len(order) - WINDOW
            first = [(name, 0.0) for name in needs[c]]
            if r >= WINDOW:
                first.append((f"t{order[r - WINDOW]}", 1.0))
            plan.event(f"d{c}", 0.2, first, functools.partial(self.to_core, r, c))
            first = [(f"d{c}", hop["D"])]
            if r:
                first.append((f"t{order[r - 1]}", hop["turn"]))
            if r >= WINDOW:
                first.append((f"y{order[r - WINDOW]}", 1.0))
            plan.event(f"t{c}", 1.4, first, functools.partial(self.to_third, r, c, last))
            first = [(f"t{c}", hop["C"])]
            if r >= WINDOW:
                first.append((f"y{order[r - WINDOW]}", 1.0))
            plan.event(f"s{c}", 0.5, first, functools.partial(self.to_second, r, c))
            first = [(f"s{c}", hop["A"])]
            if r >= WINDOW:
                first.append((f"l{order[r - WINDOW]}", 1.0))
            plan.event(f"y{c}", 0.7, first, functools.partial(self.to_z, r, c, last))
            plan.event(f"l{c}", 0.4, [(f"y{c}", hop["Z"])], functools.partial(self.last, r, c, last))


class SmallSums:
    def __init__(self, place, layer, slots, sends):
        self.place, self.layer, self.slots, self.sends = place, layer, slots, sends

    def device(self, number):
        place = self.place
        return [place.core, (place.t, place.z * COLS + place.qx), (place.t, place.z * COLS + place.qy)][number]

    def hop(self, number):
        place, slots = self.place, self.slots
        if number == 0:
            slots[0] = self.layer.dsmall[...] * self.layer.share[0]
        else:
            self.sends.arrived(("s", number - 1))
            slots[2 * number] = slots[2 * number - 2] + slots[2 * number - 1]
        if number < 3:
            self.sends.start(("s", number), lambda: (slots.at[2 * number], slots.at[2 * number + 1], self.device(number)))

    def along_z(self):
        place, slots = self.place, self.slots
        self.sends.arrived(("s", 2))
        mine = slots.at[6 + place.z]
        mine[...] = slots[4] + slots[5]
        for k in range(1, place.zs):
            self.sends.start(("sz", k), lambda k=k: (slots.at[6 + place.z], slots.at[6 + place.z], place.along_z(k)[1]))

    def end(self, out):
        place, slots = self.place, self.slots
        for k in range(1, place.zs):
            self.sends.arrived(("sz", k))
        total = slots[6]
        for k in range(1, place.zs):
            total = total + slots[6 + k]
        if place.tasks > 2:
            base, group = 6 + place.zs, lax.div(place.t, 2)
            mine = slots.at[base + group]
            mine[...] = total
            for k in range(1, place.tasks // 2):
                self.sends.start(("st", k), lambda k=k: (
                    slots.at[base + lax.div(place.t, 2)], slots.at[base + lax.div(place.t, 2)], place.along_task(k)))
            for k in range(1, place.tasks // 2):
                self.sends.arrived(("st", k))
            total = slots[base]
            for k in range(1, place.tasks // 2):
                total = total + slots[base + k]
        out[...] = total

    def plan(self, plan, needs, out):
        plan.event("m0", 0.1, [(name, 0.0) for name in needs], functools.partial(self.hop, 0))
        plan.event("m1", 0.1, [("m0", 2.0)], functools.partial(self.hop, 1))
        plan.event("m2", 0.1, [("m1", 3.0)], functools.partial(self.hop, 2))
        plan.event("m3", 0.1, [("m2", 3.0)], self.along_z)
        plan.event("m4", 0.1, [("m3", 4.0)], functools.partial(self.end, out))


HOP = {"z": 8.0, "period": 9.5, "a": 11.0, "c": 13.0, "core": 4.0, "turn": 6.0, "D": 4.0, "C": 8.0, "A": 8.0, "Z": 12.0}
AHEAD = 2


def layer_kernel(tasks, shards, *refs):
    tgt_len, src_len, counts, x_hbm, enc_hbm, cot_hbm, small_ref = refs[:7]
    mats = refs[7:17]
    layer_out, grad_in, grad_enc, *outs, from_task, small_out = refs[17:25]
    (w, wo, pi, po, act, hidden, after_self, after_cross, upstream, dn, x, enc, small, dsmall, strip, line, key_mask,
     share, *slots_refs) = refs[25:]
    from_core, from_third, from_second, from_z, fin, tasks_here, small_slots = slots_refs[:7]
    credits, local_sem, in_sem, out_sem, send_sem, recv_sem = slots_refs[7:11], *slots_refs[11:]
    place = Place(tasks, shards)
    layer = Layer(
        tgt_len=tgt_len, src_len=src_len, x=x, enc=enc, w=w, wo=wo, pi=pi, po=po, act=act,
        after_self=after_self, after_cross=after_cross, upstream=upstream, dn=dn, small=small, dsmall=dsmall, strip=strip, line=line,
        key_mask=key_mask, share=share, places=shards,
    )
    sends = Sends(send_sem, recv_sem)
    gather = Gather(place, layer, mats, small_ref, local_sem, sends)
    gather.local()
    loads = []
    for number, (src, dst) in enumerate([(x_hbm, x), (cot_hbm, act.at[G3]), (enc_hbm, enc)]):
        loads.append(pltpu.make_async_copy(src, dst, in_sem.at[number]))
        loads[-1].start()
    total = counts[0]
    for task in range(1, tasks):
        total = total + counts[task]
    share[0] = counts[place.t].astype(F32) / total.astype(F32)
    place.greet(True)
    scatter = Scatter(
        place, layer, (from_core, from_third, from_second, from_z), outs, fin, from_task, tasks_here, credits,
        local_sem.at[pl.ds(9, WINDOW)], local_sem.at[9 + WINDOW], sends,
    )
    tail = SmallSums(place, layer, small_slots, sends)
    plan = Plan()
    gather.plan(plan)
    stores = {}

    def store(number, slot, out):
        stores[number] = lambda: pltpu.make_async_copy(act.at[slot], out, out_sem.at[number])
        stores[number]().start()

    part = functools.partial

    def attend(cross, third):
        @pl.loop(0, H // 6)
        def _(hp):
            layer.attend(hp + third * (H // 6), cross)

    none = lax.div(place.t, tasks)

    def attend_back(cross, hp):
        @pl.loop(hp + none, hp + 1)
        def _(here):
            layer.attend_back(here, cross)

    def project_self(first, last):
        @pl.loop(first, last)
        def _(u):
            act[QS + u] = dot(act[NS], layer.unit(u)).astype(BF)

    def source(u):
        act[KC + u] = dot(enc[...], layer.unit(5 + u)).astype(BF)

    piece = plan.piece

    def begin():
        loads[1].wait()
        layer.masks()
        small[...] = jnp.zeros_like(small)
        layer.live_cot()
        loads[0].wait()
        loads[2].wait()

    piece("begin", 0.8, ["zs"], begin)
    piece("strip", 1.5, ["small", "begin"], lambda: [layer.sum_small(), layer.bias_strip(), layer.norm_self()])
    piece("qk", 1.6, ["strip", "w0"], part(project_self, 0, 2))
    piece("v", 0.8, ["strip", "w1"], part(project_self, 2, 3))
    for k in range(3):
        piece(f"self{k}", 2.6, [f"self{k - 1}"] if k else ["qk", "v"], part(attend, False, k))
    piece("close_self", 1.5, ["self2"], layer.close_self)
    piece("kc", 0.8, ["w2", "begin"], part(source, 0))
    piece("qc", 0.8, ["close_self", "w2"], layer.project_query)
    piece("vc", 0.8, ["w3", "begin"], part(source, 1))
    for k in range(3):
        piece(f"cross{k}", 3.0, [f"cross{k - 1}"] if k else ["qc", "kc", "vc"], part(attend, True, k))
    piece("close_cross", 0.7, ["cross2", "w3"], layer.close_cross)

    for c in range(4):
        piece(f"sent{c}", 0.1, [f"w{UNITS - 1}", "close_cross"] if c == 0 else [f"sent{c - 1}"], part(gather.sent, c))

    layer.hidden = hidden

    def ffn(slope):
        layer.slope = slope
        for j in range(4):
            piece(f"h{j}", 1.4, ["close_cross", f"w{4 + j // 2}"], part(layer.ffn_hidden, j))
        for j in range(4):
            piece(f"go{j}", 0.8, [f"h{j}"], part(layer.grad_ffn_out, j))
        for j in range(4):
            piece(f"fb{j}", 1.6, [f"h{k}" for k in range(4)] + ["w6", "w7"], part(layer.ffn_back, j))
        for j in range(4):
            piece(f"gi{j}", 0.9, [f"fb{j}"], part(layer.grad_unit, 8 + j, act.at[NF], slope.at[j]))
        plan.run_until([f"gi{j}" for j in range(4)] + [f"fb{j}" for j in range(4)])

    def back(dstrip, lines):
        layer.dstrip, layer.lines = dstrip, lines
        piece("fnb", 2.0, [], layer.ffn_norm_back)
        piece("dmc", 0.8, ["fnb", "sent3"], part(layer.mix_back, 7))
        piece("g7", 0.8, ["fnb", "sent3"], part(layer.grad_unit, 7, act.at[MC], act.at[G3]))
        for k in range(H // 2):
            piece(f"bc{k}", 2.3, [f"bc{k - 1}"] if k else ["dmc"], part(attend_back, True, k))
        for n, src, grad in ((6, enc, DV), (5, enc, DK), (4, act.at[NC], DQ)):
            piece(f"g{n}", 0.8, ["bc5", "sent3"], part(layer.grad_unit, n, src, act.at[grad]))
        piece("qb", 0.8, ["bc5"], layer.query_back)
        piece("cnb", 2.0, ["qb"], layer.cross_norm_back)
        piece("dms", 1.2, ["cnb", "g7"], lambda: [layer.mix_back(3), layer.clear_strip()])
        piece("g3", 0.8, ["dms"], part(layer.grad_unit, 3, act.at[MS], act.at[G3]))
        for k in range(H // 2):
            needs = [f"bs{k - 1}"] if k else ["dms", "g4", "g5", "g6"]
            piece(f"bs{k}", 1.9, needs, part(attend_back, False, k))
        for k in range(3):
            piece(f"sb{k}", 0.9, [f"sb{k - 1}"] if k else ["bs5"], part(layer.self_back, k))
        for k in (2, 1, 0):
            piece(f"g{k}", 0.8, ["sb2"], part(layer.grad_unit, k, act.at[NS], act.at[QC + k]))
        piece("bias", 2.4, ["bs5"], layer.bias_grad)
        piece("snb", 2.0, ["sb2"], lambda: [layer.self_norm_back(), store(1, NC, grad_in)])
        piece("eb0", 0.8, ["bs5"], part(layer.source_back, 0))
        piece("eb1", 0.8, ["eb0"], lambda: [layer.source_back(1), store(2, MC, grad_enc)])
        for j in range(4):
            piece(f"out{j}", 0.9, ["bs5"], part(layer.ffn_out, j))
        piece("out", 0.6, [f"out{j}" for j in range(4)], lambda: [layer.ffn_result(), store(0, DQ, layer_out)])
        plan.run_until(None)

    order = (6, 7, 4, 5, 3, 2, 1, 0)
    needs = {c: [f"g{2 * c}", f"g{2 * c + 1}"] for c in range(4)}
    needs.update({4: ["gi0", "gi1"], 5: ["gi2", "gi3"]})
    needs.update({c: [f"go{j}" for j in range(4)] + [f"w{UNITS - 1}"] for c in (6, 7)})
    scatter.plan(plan, order, needs)
    tail.plan(plan, ["snb", "bias", "cnb", "fnb"], small_out)
    pl.run_scoped(ffn, pltpu.VMEM((4, ROWS, D), BF))
    pl.run_scoped(
        back, pltpu.VMEM((H, BLOCK, ROWS), F32), pltpu.VMEM((H, 8, ROWS + BLOCK), F32)
    )
    scatter.finish()
    for number in range(3):
        stores[number]().wait()
    sends.finish()


def run_layer(arrays, mats, small, counts, tasks, shards):
    zs, pairs, rows = shards // COLS, tasks // 2, mats[0].shape[0]
    shape = jax.ShapeDtypeStruct
    vmem = pltpu.VMEM
    unit = (zs, COLS, rows, D)
    full = shape((ROWS, D), BF)
    out_shape = (
        full, full, full,
        shape((8, rows, D), F32), shape((rows, 4 * D), F32), shape((4, rows, D), F32),
        shape((UNITS, pairs, rows, D) if tasks > 2 else (8, 128), F32), shape((SMALL, D), F32),
    )
    scratch = [
        vmem((12,) + unit, BF),
        vmem((zs, COLS, 4, rows, D), BF),
        vmem((4,) + unit, BF),
        vmem((zs, COLS, 4, rows, D), BF),
        vmem((15, ROWS, D), BF),
        vmem((4, ROWS, D), BF),
        vmem((ROWS, D), F32),
        vmem((ROWS, D), F32),
        vmem((ROWS, D), F32),
        vmem((ROWS, D), F32),
        vmem((ROWS, D), BF),
        vmem((ROWS, D), BF),
        vmem((SMALL, D), F32),
        vmem((SMALL, D), F32),
        vmem((H, BLOCK, ROWS), BF),
        vmem((SMALL, D), F32),
        vmem((SMALL, ROWS), F32),
        pltpu.SMEM((1,), F32),
        vmem((WINDOW,) + unit, BF),
        vmem((WINDOW, 2, zs, rows, D), BF),
        vmem((WINDOW, zs, rows, D), BF),
        vmem((WINDOW, zs - 1, rows, D), BF),
        vmem((WINDOW, rows, D), F32),
        vmem((pairs, rows, D) if tasks > 2 else (8, 128), F32),
        vmem((6 + zs + pairs, SMALL, D), F32),
        pltpu.SemaphoreType.REGULAR,
        pltpu.SemaphoreType.REGULAR,
        pltpu.SemaphoreType.REGULAR,
        pltpu.SemaphoreType.REGULAR((zs - 1,)),
    ]
    number = UNITS * (zs - 1 + 7) + (zs - 1) + 3 + UNITS * (5 + zs - 1 + pairs - 1) + 3 + zs - 1 + pairs - 1
    scratch += [
        pltpu.SemaphoreType.DMA((10 + WINDOW,)),
        pltpu.SemaphoreType.DMA((3,)),
        pltpu.SemaphoreType.DMA((3,)),
        pltpu.SemaphoreType.DMA((number,)),
        pltpu.SemaphoreType.DMA((number,)),
    ]
    anywhere = pl.BlockSpec(memory_space=pl.ANY)
    return pl.pallas_call(
        functools.partial(layer_kernel, tasks, shards),
        out_shape=out_shape,
        in_specs=[pl.BlockSpec(memory_space=pltpu.SMEM)] * 3 + [anywhere] * 14,
        out_specs=[anywhere] * 7 + [pl.BlockSpec(memory_space=pltpu.VMEM)],
        scratch_shapes=scratch,
        compiler_params=pltpu.CompilerParams(
            collective_id=1, has_side_effects=True, vmem_limit_bytes=63 * 2**20
        ),
        cost_estimate=pl.CostEstimate(flops=35_000_000_000, bytes_accessed=60_000_000, transcendentals=10_000_000),
        name="layer",
    )(*counts, *arrays, small, *mats)


def on_device(
    inputs, encoded, cotangent, tgt_len, src_len, task_counts,
    gain_self, query_self, key_self, value_self, out_self, bias_table,
    gain_cross, query_cross, key_cross, value_cross, out_cross, gain_ffn, ffn_in, ffn_out,
):
    tasks, rows = task_counts.shape[0], gain_self.shape[0]
    shards, buckets = D // rows, bias_table.shape[0]
    at = lax.axis_index("shard")
    small = jnp.zeros((SMALL, D), BF)
    gains = jnp.stack([gain_self, gain_cross, gain_ffn])
    small = lax.dynamic_update_slice(small, gains, (0, at * rows))
    small = lax.dynamic_update_slice(small, bias_table.T, (3, at * buckets))
    mats = (
        query_self, key_self, value_self, out_self, query_cross, key_cross, value_cross, out_cross, ffn_in, ffn_out,
    )
    arrays = (inputs.reshape(ROWS, D), encoded.reshape(ROWS, D), cotangent.reshape(ROWS, D))
    layer_out, grad_in, grad_enc, units, g_in, g_out, _, sums = run_layer(
        arrays, mats, small, (tgt_len, src_len, task_counts), tasks, shards
    )
    g_gain = lax.dynamic_slice(sums, (0, at * rows), (3, rows))
    g_table = lax.dynamic_slice(sums, (3, at * buckets), (H, buckets)).T
    return (
        layer_out.reshape(inputs.shape), grad_in.reshape(inputs.shape), grad_enc.reshape(inputs.shape),
        g_gain[0], units[0], units[1], units[2], units[3], g_table,
        g_gain[1], units[4], units[5], units[6], units[7],
        g_gain[2], g_in, g_out.reshape(4 * rows, D),
    )


def solution(mesh):
    placed = (
        P(("task", "shard"), None, None),
        P(("task", "shard"), None, None),
        P(("task", "shard"), None, None),
        P(("task", "shard")),
        P(("task", "shard")),
        P(),
        P("shard"),
        P("shard", None),
        P("shard", None),
        P("shard", None),
        P("shard", None),
        P("shard", None),
        P("shard"),
        P("shard", None),
        P("shard", None),
        P("shard", None),
        P("shard", None),
        P("shard"),
        P("shard", None),
        P("shard", None),
    )
    return jax.shard_map(
        on_device,
        mesh=mesh,
        in_specs=placed,
        out_specs=(
            P(("task", "shard"), None, None),
            P(("task", "shard"), None, None),
            P(("task", "shard"), None, None),
            P("shard"),
            P("shard", None),
            P("shard", None),
            P("shard", None),
            P("shard", None),
            P("shard", None),
            P("shard"),
            P("shard", None),
            P("shard", None),
            P("shard", None),
            P("shard", None),
            P("shard"),
            P("shard", None),
            P("shard", None),
        ),
        check_vma=False,
    )
```
